32 devices in a mesh: row: 8 (over y, x, core), col: 4 (over z).
Axes of the slice: x: 2, y: 2, z: 4, core: 2. Of those that a mesh axis runs over, the one named last changes fastest.
Arguments:
- image: float32 [1024, 512], P('row', 'col'), may hold values from -10.1 to 10.1
Outputs:
- features: bfloat16 [12, 1024, 512], P(None, 'row', 'col')
The draws below stay inside these ranges and needn't reach their ends.
All inputs are finite; a program needn't handle non-finite values.
Results may differ from the reference program's by a relative error of at most 0.0014.
Values sent between devices are 32-bit elements; how exact they have to be, the bound alone decides.
No kernel may reach another device: no remote copies, remote signals or barrier semaphores. Data moves between devices by JAX's collectives and lax.ppermute only.
A program may use at most 64 MiB of HBM per device.

```python
import math
import jax
import jax.numpy as jnp
from jax import lax

SIG_A = 128
SIG_B = 256
HEIGHT = 1024
WIDTH = 512


def draw_image(key, part):
    first_key, second_key = jax.random.split(key)
    rough = jnp.clip(jax.random.normal(first_key, (HEIGHT, WIDTH), jnp.float32), -5.0, 5.0)
    factor = jnp.exp(jax.random.uniform(second_key, (HEIGHT, WIDTH), jnp.float32, math.log(0.5), math.log(2.0)))
    result = rough * factor
    return result


def setup_inputs(seed: int = 0) -> dict:
    key_list = jax.random.split(jax.random.key(seed), 2)
    return {
        "image": draw_image(jax.random.fold_in(key_list[1], 71), 0),
    }


DER_FIRST = (1.0 / 280, -4.0 / 105, 1.0 / 5, -4.0 / 5, 0.0, 4.0 / 5, -1.0 / 5, 4.0 / 105, -1.0 / 280)
DER_SECOND = (-1.0 / 560, 8.0 / 315, -1.0 / 5, 8.0 / 5, -205.0 / 72, 8.0 / 5, -1.0 / 5, 8.0 / 315, -1.0 / 560)
DERICHE_POLES = ((1.68, 3.735, 1.783, 0.6318), (-0.6803, -0.2598, 1.723, 1.997))

def pole_values(deviation):
    normal_sum = 0.0
    for cos_weight, sin_weight, decay, freq in DERICHE_POLES:
        magnitude = math.exp(-decay / deviation)
        real_z = magnitude * math.cos(freq / deviation)
        imag_z = magnitude * math.sin(freq / deviation)
        denom = (1.0 - real_z) ** 2 + imag_z ** 2
        real_q = (real_z - magnitude * magnitude) / denom
        imag_q = imag_z / denom
        normal_sum += cos_weight + 2.0 * (cos_weight * real_q + sin_weight * imag_q)
    pole_list = []
    center = 0.0
    for cos_weight, sin_weight, decay, freq in DERICHE_POLES:
        pole_list.append((cos_weight / normal_sum, -sin_weight / normal_sum, decay / deviation, freq / deviation))
        center += cos_weight / normal_sum
    return (center, pole_list)

def smooth_first(field, deviation):
    center, pole_list = pole_values(deviation)
    shape_tail = (1,) * (field.ndim - 1)
    real_z = []
    imag_z = []
    real_b = []
    imag_b = []
    for real_a, imag_a, rate, freq in pole_list:
        zr = math.exp(-rate) * math.cos(freq)
        zi = math.exp(-rate) * math.sin(freq)
        real_z.append(zr)
        imag_z.append(zi)
        real_b.append(real_a * zr - imag_a * zi)
        imag_b.append(real_a * zi + imag_a * zr)
    real_z = jnp.array(real_z, field.dtype).reshape((2,) + shape_tail)
    imag_z = jnp.array(imag_z, field.dtype).reshape((2,) + shape_tail)
    real_b = jnp.array(real_b, field.dtype).reshape((2,) + shape_tail)
    imag_b = jnp.array(imag_b, field.dtype).reshape((2,) + shape_tail)

    def advance(carry, line):
        state_re, state_im = carry
        emitted = lax.optimization_barrier(jnp.sum(real_b * state_re - imag_b * state_im, axis=0))
        next_re = real_z * state_re - imag_z * state_im + line[None]
        next_im = real_z * state_im + imag_z * state_re
        return ((next_re, next_im), emitted)
    start = jnp.zeros((2,) + field.shape[1:], field.dtype)
    _, causal = lax.scan(advance, (start, start), field)
    _, anticausal = lax.scan(advance, (start, start), field, reverse=True)
    return center * field + causal + anticausal

def tap_sum(source, coeffs, axis, length):
    accum = coeffs[0] * lax.slice_in_dim(source, 0, length, axis=axis)
    for offset in range(1, 9):
        accum = accum + coeffs[offset] * lax.slice_in_dim(source, offset, offset + length, axis=axis)
    return accum

def derivative_fields(padded, rows, cols):
    along_cols = tap_sum(padded, DER_FIRST, 1, cols)
    center = padded[4:4 + rows, 4:4 + cols]
    grad_x = along_cols[4:4 + rows]
    grad_y = tap_sum(padded[:, 4:4 + cols], DER_FIRST, 0, rows)
    curve_xx = tap_sum(padded[4:4 + rows], DER_SECOND, 1, cols)
    curve_xy = tap_sum(along_cols, DER_FIRST, 0, rows)
    curve_yy = tap_sum(padded[:, 4:4 + cols], DER_SECOND, 0, rows)
    return jnp.stack([center, grad_x, grad_y, curve_xx, curve_xy, curve_yy])

def reference(image):
    rows, cols = image.shape
    padded = jnp.pad(image, 4)
    fields = derivative_fields(padded, rows, cols)
    results = []
    for deviation in (SIG_A, SIG_B):
        across = jnp.transpose(smooth_first(jnp.transpose(fields, (2, 0, 1)), deviation), (1, 2, 0))
        downward = jnp.transpose(smooth_first(jnp.transpose(across, (1, 0, 2)), deviation), (1, 0, 2))
        base = 2.0 * math.sqrt(math.pi) * deviation
        factors = jnp.array([base, base * deviation, base * deviation, base * deviation ** 2, base * deviation ** 2, base * deviation ** 2], jnp.float32)
        results.append(downward * factors[:, None, None])
    return jnp.concatenate(results, axis=0).astype(jnp.bfloat16)
```

```python
import math

import jax
import jax.numpy as jnp
import ml_dtypes
import numpy as np
from jax import lax
from jax.experimental import pallas as pl
from jax.experimental.pallas import tpu as pltpu
from jax.sharding import PartitionSpec as P

SIG_A = 128
SIG_B = 256
DEVIATIONS = (SIG_A, SIG_B)

DER_FIRST = (
    1.0 / 280,
    -4.0 / 105,
    1.0 / 5,
    -4.0 / 5,
    0.0,
    4.0 / 5,
    -1.0 / 5,
    4.0 / 105,
    -1.0 / 280,
)
DER_SECOND = (
    -1.0 / 560,
    8.0 / 315,
    -1.0 / 5,
    8.0 / 5,
    -205.0 / 72,
    8.0 / 5,
    -1.0 / 5,
    8.0 / 315,
    -1.0 / 560,
)
IDENTITY = (0.0, 0.0, 0.0, 0.0, 1.0, 0.0, 0.0, 0.0, 0.0)
STENCILS = (IDENTITY, DER_FIRST, DER_SECOND)
DERICHE_POLES = ((1.68, 3.735, 1.783, 0.6318), (-0.6803, -0.2598, 1.723, 1.997))
FEATURES = ((0, 0), (0, 1), (1, 0), (0, 2), (1, 1), (2, 0))

HALO = 4
CAUSAL, FIRST, LAST, ANTICAUSAL = 0, 8, 12, 16
BASIS = 24
SENT = 16
LANES = 128


def pole_values(deviation):
    normal_sum = 0.0
    for cos_weight, sin_weight, decay, freq in DERICHE_POLES:
        z = np.exp(complex(-decay, freq) / deviation)
        q = z / (1.0 - z)
        normal_sum += cos_weight + 2.0 * (cos_weight * q.real + sin_weight * q.imag)
    weights = [complex(cw, -sw) / normal_sum for cw, sw, _, _ in DERICHE_POLES]
    exponents = [complex(decay, -freq) / deviation for _, _, decay, freq in DERICHE_POLES]
    return np.array(weights), np.array(exponents)


def all_poles():
    return [pole_values(deviation) for deviation in DEVIATIONS]


def smooth_kernel(poles, distance):
    weights, exponents = poles
    return sum(
        (w * np.exp(-e * np.abs(distance))).real for w, e in zip(weights, exponents)
    )


def summary_table(length):
    cells = np.arange(length)
    table = np.zeros((BASIS, length))
    row = 0
    for _, exponents in all_poles():
        for e in exponents:
            causal = np.exp(-e * (length - 1 - cells))
            anticausal = np.exp(-e * cells)
            table[CAUSAL + row], table[CAUSAL + row + 1] = causal.real, causal.imag
            table[ANTICAUSAL + row], table[ANTICAUSAL + row + 1] = (
                anticausal.real,
                anticausal.imag,
            )
            row += 2
    for i in range(HALO):
        table[FIRST + i, i] = 1.0
        table[LAST + i, length - HALO + i] = 1.0
    return table


def cell_weight(poles, stencil, out_cells, in_cells, total):
    result = np.zeros((len(out_cells), len(in_cells)))
    for t in range(-HALO, HALO + 1):
        field_cells = in_cells - t
        inside = (field_cells >= 0) & (field_cells < total)
        distance = out_cells[:, None] - field_cells[None, :]
        result += stencil[t + HALO] * smooth_kernel(poles, distance) * inside[None, :]
    return result


def summary_weight(level, stencil, block, source, length, blocks):
    poles = all_poles()[level]
    weights, exponents = poles
    total = length * blocks
    out_cells = block * length + np.arange(length)
    after = block > source
    base = CAUSAL if after else FIRST
    offset = (CAUSAL if after else ANTICAUSAL) + 4 * level
    sign = 1.0 if after else -1.0
    anchor = source * length + (length - 1 if after else 0)
    table = np.zeros((length, BASIS))
    for p, (w, e) in enumerate(zip(weights, exponents)):
        eigen = sum(stencil[t + HALO] * np.exp(-sign * e * t) for t in range(-HALO, HALO + 1))
        gain = w * eigen * np.exp(-e * np.abs(out_cells - anchor))
        table[:, offset + 2 * p] = gain.real
        table[:, offset + 2 * p + 1] = -gain.imag

    def far_form(cells):
        result = np.zeros((length, len(cells)))
        for t in range(-HALO, HALO + 1):
            distance = sign * (out_cells[:, None] - (cells - t)[None, :])
            result += stencil[t + HALO] * sum(
                (w * np.exp(-e * distance)).real for w, e in zip(weights, exponents)
            )
        return result

    for position, start in ((FIRST, 0), (LAST, length - HALO)):
        cells = source * length + start + np.arange(HALO)
        at_end = (cells[0] == 0) or (cells[-1] == total - 1)
        adjacent = (cells[-1] + 1 == out_cells[0]) or (out_cells[-1] + 1 == cells[0])
        if at_end or adjacent:
            table[:, position : position + HALO] = cell_weight(
                poles, stencil, out_cells, cells, total
            ) - far_form(cells)
    return table[:, base : base + SENT]


def operator_tables(length, blocks, gains):
    remote = -(-SENT * blocks // LANES) * LANES
    tables = np.zeros((blocks, 2, 3, length, length + remote))
    for block in range(blocks):
        cells = block * length + np.arange(length)
        for level, poles in enumerate(all_poles()):
            for s, stencil in enumerate(STENCILS):
                view = tables[block, level, s]
                view[:, :length] = cell_weight(poles, stencil, cells, cells, length * blocks)
                for source in range(blocks):
                    if source != block:
                        start = length + SENT * source
                        view[:, start : start + SENT] = summary_weight(
                            level, stencil, block, source, length, blocks
                        )
                view *= gains[level][s]
    return tables


def window_tables(tables, length, blocks):
    middle = blocks // 2
    own = np.stack([tables[b, ..., :length] for b in (0, middle, blocks - 1)])
    inner = np.zeros((2 * blocks - 1,) + tables.shape[1:-1] + (SENT,))
    for block in range(blocks):
        for source in range(1, blocks - 1):
            start = length + SENT * source
            inner[source - block + blocks - 1] = tables[block, ..., start : start + SENT]
    ends = np.stack(
        [
            tables[..., length + SENT * end : length + SENT * (end + 1)]
            for end in (0, blocks - 1)
        ],
        axis=1,
    )

    def cells_first(table, lead):
        moved = np.moveaxis(table, -1, lead)
        return moved.reshape(moved.shape[: lead + 1] + (-1,))

    inner = cells_first(inner, 1)
    return (
        np.moveaxis(split_table(cells_first(own, 1)), 0, 1),
        split_table(inner.reshape(-1, inner.shape[-1])),
        np.moveaxis(split_table(cells_first(ends, 2)), 0, 2),
    )


def split_table(values):
    high = values.astype(ml_dtypes.bfloat16)
    low = (values - high.astype(np.float64)).astype(ml_dtypes.bfloat16)
    return np.stack([high, low])


def split(values):
    high = values.astype(jnp.bfloat16)
    low = (values - high.astype(jnp.float32)).astype(jnp.bfloat16)
    return high, low


def dot3(left, right, dims=((1,), (0,))):
    def dot(a, b):
        return lax.dot_general(a, b, (dims, ((), ())), preferred_element_type=jnp.float32)

    return dot(left[0], right[0]) + (dot(left[0], right[1]) + dot(left[1], right[0]))


NT = ((1,), (1,))


def summarize(
    rows, cols, image, sums, row_op, own_op, inner_op, ends_op, sent, block, row_own, col_own, tables, sems
):
    row, col = lax.axis_index("row"), lax.axis_index("col")
    width = image.shape[1]
    variant = jnp.where(col == 0, 0, jnp.where(col == cols - 1, 2, 1))
    window = pl.multiple_of(SENT * (cols - col), SENT)
    last = width + SENT * (cols - 1)

    def col_rows(start, count):
        return col_own.at[:, pl.ds(start, count)]

    pairs = [
        (image, block),
        (sums, tables),
        (row_op.at[row], row_own),
        (own_op.at[variant], col_rows(0, width)),
        (ends_op.at[col, 0], col_rows(width, SENT)),
        (
            inner_op.at[:, pl.ds(window, SENT * (cols - 2))],
            col_rows(width + SENT, SENT * (cols - 2)),
        ),
        (ends_op.at[col, 1], col_rows(last, SENT)),
    ]
    copies = [pltpu.make_async_copy(*pair, sems.at[i]) for i, pair in enumerate(pairs)]
    for copy in copies:
        copy.start()
    copies[0].wait()
    copies[1].wait()
    cells = split(block[...])
    row_sums = dot3((tables[0, 0], tables[0, 1]), cells)
    col_table = (tables[1, 0], tables[1, 1])
    col_sums = dot3(col_table, cells, NT)
    both = dot3(split(row_sums), col_table, NT)
    lane = lax.broadcasted_iota(jnp.int32, both.shape, 1)
    shift = SENT * lax.rem(col, LANES // SENT)
    ahead = pltpu.roll(jnp.where(lane < SENT, both, 0.0), shift, 1)
    back = pltpu.roll(both, LANES - FIRST, 1)
    back = pltpu.roll(jnp.where(lane < SENT, back, 0.0), shift, 1)

    def after(values):
        return values[CAUSAL : CAUSAL + SENT]

    def before(values):
        return values[FIRST : FIRST + SENT]

    for to_row in range(rows):
        row_after = to_row > row
        straight = jnp.where(row_after, after(row_sums), before(row_sums))
        right = jnp.where(row_after, after(ahead), before(ahead))
        left = jnp.where(row_after, after(back), before(back))
        for to_col in range(cols):
            across = jnp.where(to_col > col, after(col_sums), before(col_sums))
            corner = jnp.where(to_col > col, right, left)
            piece = jnp.where(to_col == col, straight, corner)
            sent[to_row * cols + to_col] = jnp.where(to_row == row, across, piece)
    rest = col_own.shape[1] - last - SENT
    if rest:
        col_own[:, last + SENT :] = jnp.zeros((2, rest, col_own.shape[2]), jnp.bfloat16)
    for copy in copies[2:]:
        copy.wait()


def combine(rows, cols, block, got, row_own, col_own, out, staged, sems):
    row, col = lax.axis_index("row"), lax.axis_index("col")
    length = block.shape[0]
    groups = -(-SENT * cols // LANES)
    fill = groups * LANES - SENT * cols
    across = got[pl.ds(row * cols, cols)].reshape(SENT * cols, length)
    if fill:
        across = jnp.concatenate([across, jnp.zeros((fill, length), jnp.float32)])
    upper = jnp.concatenate([block[...], across.T], axis=1)
    lower = []
    for from_row in range(rows):
        parts = [got[from_row * cols + col]]
        for group in range(groups):
            total = jnp.zeros((SENT, LANES), jnp.float32)
            for from_col in range(group * (LANES // SENT), min(cols, (group + 1) * (LANES // SENT))):
                total += jnp.where(from_col == col, 0.0, got[from_row * cols + from_col])
            parts.append(total)
        lower.append(jnp.concatenate(parts, axis=1))
    fill = -(-SENT * rows // LANES) * LANES - SENT * rows
    if fill:
        lower.append(jnp.zeros((fill, upper.shape[1]), jnp.float32))
    known = split(jnp.concatenate([upper] + lower))
    width = out.shape[2]
    copies = []
    for level in range(2):
        span = 3 * width
        smoothed = split(
            dot3(known, [col_own[i, :, span * level : span * (level + 1)] for i in range(2)])
        )
        for f, (row_stencil, col_stencil) in enumerate(FEATURES):
            columns = slice(width * col_stencil, width * (col_stencil + 1))
            feature = dot3(
                [row_own[i, level, row_stencil] for i in range(2)],
                [part[:, columns] for part in smoothed],
            )
            channel = len(FEATURES) * level + f
            staged[channel] = feature.astype(jnp.bfloat16)
            copies.append(
                pltpu.make_async_copy(staged.at[channel], out.at[channel], sems.at[channel])
            )
            copies[-1].start()
    for copy in copies:
        copy.wait()


def on_device(rows, cols, image):
    height, width = image.shape
    base = [2.0 * math.sqrt(math.pi) * s for s in DEVIATIONS]
    row_tables = operator_tables(
        height, rows, [[b * s**k for k in range(3)] for b, s in zip(base, DEVIATIONS)]
    )
    col_tables = operator_tables(width, cols, [[s**k for k in range(3)] for s in DEVIATIONS])
    row_op = np.moveaxis(split_table(row_tables), 0, 1)
    own_op, inner_op, ends_op = window_tables(col_tables, width, cols)
    col_own_shape = (2, col_tables.shape[-1], own_op.shape[-1])
    sums = np.zeros((2, 2, LANES, max(height, width)))
    sums[0, :, :BASIS, :height] = split_table(summary_table(height))
    sums[1, :, :BASIS, :width] = split_table(summary_table(width))
    sums = sums.astype(ml_dtypes.bfloat16)

    def in_vmem(count):
        return [pl.BlockSpec(memory_space=pltpu.VMEM)] * count

    params = pltpu.CompilerParams(vmem_limit_bytes=16 * 1024 * 1024)
    operands = [image] + [jnp.asarray(x) for x in (sums, row_op, own_op, inner_op, ends_op)]
    operands = [pltpu.with_memory_space_constraint(x, pltpu.HBM) for x in operands]
    sent, block, row_own, col_own = pl.pallas_call(
        lambda *refs: summarize(rows, cols, *refs),
        out_shape=[
            pltpu.VMEM((rows * cols, SENT, LANES), jnp.float32),
            pltpu.VMEM((height, width), jnp.float32),
            pltpu.VMEM(row_op.shape[1:], jnp.bfloat16),
            pltpu.VMEM(col_own_shape, jnp.bfloat16),
        ],
        in_specs=[pl.BlockSpec(memory_space=pltpu.HBM)] * len(operands),
        out_specs=in_vmem(4),
        scratch_shapes=[
            pltpu.VMEM(sums.shape, jnp.bfloat16),
            pltpu.SemaphoreType.DMA((7,)),
        ],
        compiler_params=params,
        name="summaries",
    )(*operands)
    got = lax.all_to_all(sent, ("row", "col"), 0, 0)
    features = 2 * len(FEATURES)
    return pl.pallas_call(
        lambda *refs: combine(rows, cols, *refs),
        out_shape=jax.ShapeDtypeStruct((features, height, width), jnp.bfloat16),
        in_specs=in_vmem(4),
        out_specs=pl.BlockSpec(memory_space=pl.ANY),
        scratch_shapes=[
            pltpu.VMEM((features, height, width), jnp.bfloat16),
            pltpu.SemaphoreType.DMA((features,)),
        ],
        compiler_params=params,
        name="combine",
    )(block, got, row_own, col_own)


def solution(mesh):
    rows, cols = mesh.shape["row"], mesh.shape["col"]
    return jax.shard_map(
        lambda image: on_device(rows, cols, image),
        mesh=mesh,
        in_specs=(P("row", "col"),),
        out_specs=P(None, "row", "col"),
        check_vma=False,
    )
```

```python
import math

import jax
import jax.numpy as jnp
import ml_dtypes
import numpy as np
from jax import lax
from jax.experimental import pallas as pl
from jax.experimental.pallas import tpu as pltpu
from jax.sharding import PartitionSpec as P

SIG_A = 128
SIG_B = 256
DEVIATIONS = (SIG_A, SIG_B)

DER_FIRST = (
    1.0 / 280,
    -4.0 / 105,
    1.0 / 5,
    -4.0 / 5,
    0.0,
    4.0 / 5,
    -1.0 / 5,
    4.0 / 105,
    -1.0 / 280,
)
DER_SECOND = (
    -1.0 / 560,
    8.0 / 315,
    -1.0 / 5,
    8.0 / 5,
    -205.0 / 72,
    8.0 / 5,
    -1.0 / 5,
    8.0 / 315,
    -1.0 / 560,
)
IDENTITY = (0.0, 0.0, 0.0, 0.0, 1.0, 0.0, 0.0, 0.0, 0.0)
STENCILS = (IDENTITY, DER_FIRST, DER_SECOND)
DERICHE_POLES = ((1.68, 3.735, 1.783, 0.6318), (-0.6803, -0.2598, 1.723, 1.997))
FEATURES = ((0, 0), (0, 1), (1, 0), (0, 2), (1, 1), (2, 0))

HALO = 4
CAUSAL, FIRST, LAST, ANTICAUSAL = 0, 8, 12, 16
BASIS = 24
SENT = 16
LANES = 128


def pole_values(deviation):
    normal_sum = 0.0
    for cos_weight, sin_weight, decay, freq in DERICHE_POLES:
        z = np.exp(complex(-decay, freq) / deviation)
        q = z / (1.0 - z)
        normal_sum += cos_weight + 2.0 * (cos_weight * q.real + sin_weight * q.imag)
    weights = [complex(cw, -sw) / normal_sum for cw, sw, _, _ in DERICHE_POLES]
    exponents = [complex(decay, -freq) / deviation for _, _, decay, freq in DERICHE_POLES]
    return np.array(weights), np.array(exponents)


def all_poles():
    return [pole_values(deviation) for deviation in DEVIATIONS]


def smooth_kernel(poles, distance):
    weights, exponents = poles
    return sum(
        (w * np.exp(-e * np.abs(distance))).real for w, e in zip(weights, exponents)
    )


def summary_table(length):
    cells = np.arange(length)
    table = np.zeros((BASIS, length))
    row = 0
    for _, exponents in all_poles():
        for e in exponents:
            causal = np.exp(-e * (length - 1 - cells))
            anticausal = np.exp(-e * cells)
            table[CAUSAL + row], table[CAUSAL + row + 1] = causal.real, causal.imag
            table[ANTICAUSAL + row], table[ANTICAUSAL + row + 1] = (
                anticausal.real,
                anticausal.imag,
            )
            row += 2
    for i in range(HALO):
        table[FIRST + i, i] = 1.0
        table[LAST + i, length - HALO + i] = 1.0
    return table


def cell_weight(poles, stencil, out_cells, in_cells, total):
    result = np.zeros((len(out_cells), len(in_cells)))
    for t in range(-HALO, HALO + 1):
        field_cells = in_cells - t
        inside = (field_cells >= 0) & (field_cells < total)
        distance = out_cells[:, None] - field_cells[None, :]
        result += stencil[t + HALO] * smooth_kernel(poles, distance) * inside[None, :]
    return result


def summary_weight(level, stencil, block, source, length, blocks):
    poles = all_poles()[level]
    weights, exponents = poles
    total = length * blocks
    out_cells = block * length + np.arange(length)
    after = block > source
    base = CAUSAL if after else FIRST
    offset = (CAUSAL if after else ANTICAUSAL) + 4 * level
    sign = 1.0 if after else -1.0
    anchor = source * length + (length - 1 if after else 0)
    table = np.zeros((length, BASIS))
    for p, (w, e) in enumerate(zip(weights, exponents)):
        eigen = sum(stencil[t + HALO] * np.exp(-sign * e * t) for t in range(-HALO, HALO + 1))
        gain = w * eigen * np.exp(-e * np.abs(out_cells - anchor))
        table[:, offset + 2 * p] = gain.real
        table[:, offset + 2 * p + 1] = -gain.imag

    def far_form(cells):
        result = np.zeros((length, len(cells)))
        for t in range(-HALO, HALO + 1):
            distance = sign * (out_cells[:, None] - (cells - t)[None, :])
            result += stencil[t + HALO] * sum(
                (w * np.exp(-e * distance)).real for w, e in zip(weights, exponents)
            )
        return result

    for position, start in ((FIRST, 0), (LAST, length - HALO)):
        cells = source * length + start + np.arange(HALO)
        at_end = (cells[0] == 0) or (cells[-1] == total - 1)
        adjacent = (cells[-1] + 1 == out_cells[0]) or (out_cells[-1] + 1 == cells[0])
        if at_end or adjacent:
            table[:, position : position + HALO] = cell_weight(
                poles, stencil, out_cells, cells, total
            ) - far_form(cells)
    return table[:, base : base + SENT]


def operator_tables(length, blocks, gains):
    remote = -(-SENT * blocks // LANES) * LANES
    tables = np.zeros((blocks, 2, 3, length, length + remote))
    for block in range(blocks):
        cells = block * length + np.arange(length)
        for level, poles in enumerate(all_poles()):
            for s, stencil in enumerate(STENCILS):
                view = tables[block, level, s]
                view[:, :length] = cell_weight(poles, stencil, cells, cells, length * blocks)
                for source in range(blocks):
                    if source != block:
                        start = length + SENT * source
                        view[:, start : start + SENT] = summary_weight(
                            level, stencil, block, source, length, blocks
                        )
                view *= gains[level][s]
    return tables


def window_tables(tables, length, blocks):
    middle = blocks // 2
    own = np.stack([tables[b, ..., :length] for b in (0, middle, blocks - 1)])
    inner = np.zeros((2 * blocks - 1,) + tables.shape[1:-1] + (SENT,))
    for block in range(blocks):
        for source in range(1, blocks - 1):
            start = length + SENT * source
            inner[source - block + blocks - 1] = tables[block, ..., start : start + SENT]
    ends = np.stack(
        [
            tables[..., length + SENT * end : length + SENT * (end + 1)]
            for end in (0, blocks - 1)
        ],
        axis=1,
    )

    def cells_first(table, lead):
        moved = np.moveaxis(table, -1, lead)
        return moved.reshape(moved.shape[: lead + 1] + (-1,))

    inner = cells_first(inner, 1)
    return (
        np.moveaxis(split_table(cells_first(own, 1)), 0, 1),
        split_table(inner.reshape(-1, inner.shape[-1])),
        np.moveaxis(split_table(cells_first(ends, 2)), 0, 2),
    )


def split_table(values):
    high = values.astype(ml_dtypes.bfloat16)
    low = (values - high.astype(np.float64)).astype(ml_dtypes.bfloat16)
    return np.stack([high, low])


def split(values):
    high = values.astype(jnp.bfloat16)
    low = (values - high.astype(jnp.float32)).astype(jnp.bfloat16)
    return high, low


def dot3(left, right, dims=((1,), (0,))):
    left = jnp.concatenate([left[0], left[0], left[1]], axis=dims[0][0])
    right = jnp.concatenate([right[0], right[1], right[0]], axis=dims[1][0])
    return lax.dot_general(left, right, (dims, ((), ())), preferred_element_type=jnp.float32)


NT = ((1,), (1,))


def summarize(
    rows, cols, image, sums, row_op, own_op, inner_op, ends_op, sent, block, row_own, col_own, tables, sems
):
    row, col = lax.axis_index("row"), lax.axis_index("col")
    width = image.shape[1]
    variant = jnp.where(col == 0, 0, jnp.where(col == cols - 1, 2, 1))
    window = pl.multiple_of(SENT * (cols - col), SENT)
    last = width + SENT * (cols - 1)

    def col_rows(start, count):
        return col_own.at[:, pl.ds(start, count)]

    pairs = [
        (image, block),
        (sums, tables),
        (row_op.at[row], row_own),
        (own_op.at[variant], col_rows(0, width)),
        (ends_op.at[col, 0], col_rows(width, SENT)),
        (
            inner_op.at[:, pl.ds(window, SENT * (cols - 2))],
            col_rows(width + SENT, SENT * (cols - 2)),
        ),
        (ends_op.at[col, 1], col_rows(last, SENT)),
    ]
    copies = [pltpu.make_async_copy(*pair, sems.at[i]) for i, pair in enumerate(pairs)]
    for copy in copies:
        copy.start()
    copies[0].wait()
    copies[1].wait()
    cells = split(block[...])
    row_sums = dot3((tables[0, 0], tables[0, 1]), cells)
    col_table = (tables[1, 0], tables[1, 1])
    col_sums = dot3(col_table, cells, NT)
    both = dot3(split(row_sums), col_table, NT)
    fill = jnp.zeros((both.shape[0], LANES - both.shape[1]), jnp.float32)
    both = jnp.concatenate([both, fill], axis=1)
    lane = lax.broadcasted_iota(jnp.int32, both.shape, 1)
    shift = SENT * lax.rem(col, LANES // SENT)
    ahead = pltpu.roll(jnp.where(lane < SENT, both, 0.0), shift, 1)
    back = pltpu.roll(both, LANES - FIRST, 1)
    back = pltpu.roll(jnp.where(lane < SENT, back, 0.0), shift, 1)

    def after(values):
        return values[CAUSAL : CAUSAL + SENT]

    def before(values):
        return values[FIRST : FIRST + SENT]

    for to_row in range(rows):
        row_after = to_row > row
        straight = jnp.where(row_after, after(row_sums), before(row_sums))
        right = jnp.where(row_after, after(ahead), before(ahead))
        left = jnp.where(row_after, after(back), before(back))
        for to_col in range(cols):
            across = jnp.where(to_col > col, after(col_sums), before(col_sums))
            corner = jnp.where(to_col > col, right, left)
            piece = jnp.where(to_col == col, straight, corner)
            sent[to_row * cols + to_col] = jnp.where(to_row == row, across, piece)
    rest = col_own.shape[1] - last - SENT
    if rest:
        col_own[:, last + SENT :] = jnp.zeros((2, rest, col_own.shape[2]), jnp.bfloat16)
    for copy in copies[2:]:
        copy.wait()


def combine(rows, cols, block, got, row_own, col_own, out, staged, sems):
    row, col = lax.axis_index("row"), lax.axis_index("col")
    length = block.shape[0]
    groups = -(-SENT * cols // LANES)
    fill = groups * LANES - SENT * cols
    across = got[pl.ds(row * cols, cols)].reshape(SENT * cols, length)
    if fill:
        across = jnp.concatenate([across, jnp.zeros((fill, length), jnp.float32)])
    upper = jnp.concatenate([block[...], across.T], axis=1)
    lower = []
    for from_row in range(rows):
        parts = [got[from_row * cols + col]]
        for group in range(groups):
            total = jnp.zeros((SENT, LANES), jnp.float32)
            for from_col in range(group * (LANES // SENT), min(cols, (group + 1) * (LANES // SENT))):
                total += jnp.where(from_col == col, 0.0, got[from_row * cols + from_col])
            parts.append(total)
        lower.append(jnp.concatenate(parts, axis=1))
    fill = -(-SENT * rows // LANES) * LANES - SENT * rows
    if fill:
        lower.append(jnp.zeros((fill, upper.shape[1]), jnp.float32))
    known = split(jnp.concatenate([upper] + lower))
    width = out.shape[2]
    copies = []
    along_cols = dot3(known, [col_own[i] for i in range(2)])
    for level in range(2):
        span = 3 * width
        smoothed = split(along_cols[:, span * level : span * (level + 1)])
        products = [
            dot3(
                [row_own[i, level, k] for i in range(2)],
                [part[:, : (3 - k) * width] for part in smoothed],
            )
            for k in range(3)
        ]
        for f, (row_stencil, col_stencil) in enumerate(FEATURES):
            feature = products[row_stencil][:, width * col_stencil : width * (col_stencil + 1)]
            channel = len(FEATURES) * level + f
            staged[channel] = feature.astype(jnp.bfloat16)
            copies.append(
                pltpu.make_async_copy(staged.at[channel], out.at[channel], sems.at[channel])
            )
            copies[-1].start()
    for copy in copies:
        copy.wait()


def on_device(rows, cols, image):
    height, width = image.shape
    base = [2.0 * math.sqrt(math.pi) * s for s in DEVIATIONS]
    row_tables = operator_tables(
        height, rows, [[b * s**k for k in range(3)] for b, s in zip(base, DEVIATIONS)]
    )
    col_tables = operator_tables(width, cols, [[s**k for k in range(3)] for s in DEVIATIONS])
    row_op = np.moveaxis(split_table(row_tables), 0, 1)
    own_op, inner_op, ends_op = window_tables(col_tables, width, cols)
    col_own_shape = (2, col_tables.shape[-1], own_op.shape[-1])
    sums = np.zeros((2, 2, 32, max(height, width)))
    sums[0, :, :BASIS, :height] = split_table(summary_table(height))
    sums[1, :, :BASIS, :width] = split_table(summary_table(width))
    sums = sums.astype(ml_dtypes.bfloat16)

    def in_vmem(count):
        return [pl.BlockSpec(memory_space=pltpu.VMEM)] * count

    params = pltpu.CompilerParams(vmem_limit_bytes=16 * 1024 * 1024)
    operands = [image] + [jnp.asarray(x) for x in (sums, row_op, own_op, inner_op, ends_op)]
    operands = [pltpu.with_memory_space_constraint(x, pltpu.HBM) for x in operands]
    sent, block, row_own, col_own = pl.pallas_call(
        lambda *refs: summarize(rows, cols, *refs),
        out_shape=[
            pltpu.VMEM((rows * cols, SENT, LANES), jnp.float32),
            pltpu.VMEM((height, width), jnp.float32),
            pltpu.VMEM(row_op.shape[1:], jnp.bfloat16),
            pltpu.VMEM(col_own_shape, jnp.bfloat16),
        ],
        in_specs=[pl.BlockSpec(memory_space=pltpu.HBM)] * len(operands),
        out_specs=in_vmem(4),
        scratch_shapes=[
            pltpu.VMEM(sums.shape, jnp.bfloat16),
            pltpu.SemaphoreType.DMA((7,)),
        ],
        compiler_params=params,
        name="summaries",
    )(*operands)
    got = lax.all_to_all(sent, ("row", "col"), 0, 0)
    features = 2 * len(FEATURES)
    return pl.pallas_call(
        lambda *refs: combine(rows, cols, *refs),
        out_shape=jax.ShapeDtypeStruct((features, height, width), jnp.bfloat16),
        in_specs=in_vmem(4),
        out_specs=pl.BlockSpec(memory_space=pl.ANY),
        scratch_shapes=[
            pltpu.VMEM((features, height, width), jnp.bfloat16),
            pltpu.SemaphoreType.DMA((features,)),
        ],
        compiler_params=params,
        name="combine",
    )(block, got, row_own, col_own)


def solution(mesh):
    rows, cols = mesh.shape["row"], mesh.shape["col"]
    return jax.shard_map(
        lambda image: on_device(rows, cols, image),
        mesh=mesh,
        in_specs=(P("row", "col"),),
        out_specs=P(None, "row", "col"),
        check_vma=False,
    )
```

```python
import math

import jax
import jax.numpy as jnp
import ml_dtypes
import numpy as np
from jax import lax
from jax.experimental import pallas as pl
from jax.experimental.pallas import tpu as pltpu
from jax.sharding import PartitionSpec as P

SIG_A = 128
SIG_B = 256
DEVIATIONS = (SIG_A, SIG_B)

DER_FIRST = (
    1.0 / 280,
    -4.0 / 105,
    1.0 / 5,
    -4.0 / 5,
    0.0,
    4.0 / 5,
    -1.0 / 5,
    4.0 / 105,
    -1.0 / 280,
)
DER_SECOND = (
    -1.0 / 560,
    8.0 / 315,
    -1.0 / 5,
    8.0 / 5,
    -205.0 / 72,
    8.0 / 5,
    -1.0 / 5,
    8.0 / 315,
    -1.0 / 560,
)
IDENTITY = (0.0, 0.0, 0.0, 0.0, 1.0, 0.0, 0.0, 0.0, 0.0)
STENCILS = (IDENTITY, DER_FIRST, DER_SECOND)
DERICHE_POLES = ((1.68, 3.735, 1.783, 0.6318), (-0.6803, -0.2598, 1.723, 1.997))
FEATURES = ((0, 0), (0, 1), (1, 0), (0, 2), (1, 1), (2, 0))

HALO = 4
CAUSAL, FIRST, LAST, ANTICAUSAL = 0, 8, 12, 16
BASIS = 24
SENT = 16
LANES = 128
ROW_ROWS = 48
COL_ROWS = 32
PIECE = SENT // 2 + 1


def pole_values(deviation):
    normal_sum = 0.0
    for cos_weight, sin_weight, decay, freq in DERICHE_POLES:
        z = np.exp(complex(-decay, freq) / deviation)
        q = z / (1.0 - z)
        normal_sum += cos_weight + 2.0 * (cos_weight * q.real + sin_weight * q.imag)
    weights = [complex(cw, -sw) / normal_sum for cw, sw, _, _ in DERICHE_POLES]
    exponents = [complex(decay, -freq) / deviation for _, _, decay, freq in DERICHE_POLES]
    return np.array(weights), np.array(exponents)


def all_poles():
    return [pole_values(deviation) for deviation in DEVIATIONS]


def smooth_kernel(poles, distance):
    weights, exponents = poles
    return sum(
        (w * np.exp(-e * np.abs(distance))).real for w, e in zip(weights, exponents)
    )


def summary_table(length):
    cells = np.arange(length)
    table = np.zeros((BASIS, length))
    row = 0
    for _, exponents in all_poles():
        for e in exponents:
            causal = np.exp(-e * (length - 1 - cells))
            anticausal = np.exp(-e * cells)
            table[CAUSAL + row], table[CAUSAL + row + 1] = causal.real, causal.imag
            table[ANTICAUSAL + row], table[ANTICAUSAL + row + 1] = (
                anticausal.real,
                anticausal.imag,
            )
            row += 2
    for i in range(HALO):
        table[FIRST + i, i] = 1.0
        table[LAST + i, length - HALO + i] = 1.0
    return table


def cell_weight(poles, stencil, out_cells, in_cells, total):
    result = np.zeros((len(out_cells), len(in_cells)))
    for t in range(-HALO, HALO + 1):
        field_cells = in_cells - t
        inside = (field_cells >= 0) & (field_cells < total)
        distance = out_cells[:, None] - field_cells[None, :]
        result += stencil[t + HALO] * smooth_kernel(poles, distance) * inside[None, :]
    return result


def summary_weight(level, stencil, out_start, length, start, extent, total):
    poles = all_poles()[level]
    weights, exponents = poles
    out_cells = out_start + np.arange(length)
    after = out_start > start
    base = CAUSAL if after else FIRST
    offset = (CAUSAL if after else ANTICAUSAL) + 4 * level
    sign = 1.0 if after else -1.0
    anchor = start + (extent - 1 if after else 0)
    table = np.zeros((length, BASIS))
    for p, (w, e) in enumerate(zip(weights, exponents)):
        eigen = sum(stencil[t + HALO] * np.exp(-sign * e * t) for t in range(-HALO, HALO + 1))
        gain = w * eigen * np.exp(-e * np.abs(out_cells - anchor))
        table[:, offset + 2 * p] = gain.real
        table[:, offset + 2 * p + 1] = -gain.imag

    def far_form(cells):
        result = np.zeros((length, len(cells)))
        for t in range(-HALO, HALO + 1):
            distance = sign * (out_cells[:, None] - (cells - t)[None, :])
            result += stencil[t + HALO] * sum(
                (w * np.exp(-e * distance)).real for w, e in zip(weights, exponents)
            )
        return result

    for position, first in ((FIRST, start), (LAST, start + extent - HALO)):
        cells = first + np.arange(HALO)
        at_end = (cells[0] == 0) or (cells[-1] == total - 1)
        adjacent = (cells[-1] + 1 == out_cells[0]) or (out_cells[-1] + 1 == cells[0])
        if at_end or adjacent:
            table[:, position : position + HALO] = cell_weight(
                poles, stencil, out_cells, cells, total
            ) - far_form(cells)
    return table[:, base : base + SENT]


def operator_tables(length, blocks, sources, gains):
    remote = -(-SENT * len(sources(0)) // LANES) * LANES
    tables = np.zeros((blocks, 2, 3, length, length + remote))
    total = length * blocks
    for block in range(blocks):
        cells = block * length + np.arange(length)
        for level, poles in enumerate(all_poles()):
            for k, stencil in enumerate(STENCILS):
                view = tables[block, level, k]
                view[:, :length] = cell_weight(poles, stencil, cells, cells, total)
                for place, source in enumerate(sources(block)):
                    if source is not None:
                        at = length + SENT * place
                        view[:, at : at + SENT] = summary_weight(
                            level, stencil, cells[0], length, *source, total
                        )
                view *= gains[level][k]
    return tables


def window_tables(tables, length, blocks):
    middle = blocks // 2
    own = np.stack([tables[b, ..., :length] for b in (0, middle, blocks - 1)])
    inner = np.zeros((2 * blocks - 1,) + tables.shape[1:-1] + (SENT,))
    for block in range(blocks):
        for source in range(1, blocks - 1):
            start = length + SENT * source
            inner[source - block + blocks - 1] = tables[block, ..., start : start + SENT]
    ends = np.stack(
        [
            tables[..., length + SENT * end : length + SENT * (end + 1)]
            for end in (0, blocks - 1)
        ],
        axis=1,
    )

    def cells_first(table, lead):
        moved = np.moveaxis(table, -1, lead)
        return moved.reshape(moved.shape[: lead + 1] + (-1,))

    inner = cells_first(inner, 1)
    return (
        np.moveaxis(split_table(cells_first(own, 1)), 0, 1),
        split_table(inner.reshape(-1, inner.shape[-1])),
        np.moveaxis(split_table(cells_first(ends, 2)), 0, 2),
    )


def split_table(values):
    high = values.astype(ml_dtypes.bfloat16)
    low = (values - high.astype(np.float64)).astype(ml_dtypes.bfloat16)
    return np.stack([high, low])


def split(values):
    high = values.astype(jnp.bfloat16)
    low = (values - high.astype(jnp.float32)).astype(jnp.bfloat16)
    return high, low


def dot3(left, right, dims=((1,), (0,))):
    left = jnp.concatenate([left[0], left[0], left[1]], axis=dims[0][0])
    right = jnp.concatenate([right[0], right[1], right[0]], axis=dims[1][0])
    return lax.dot_general(left, right, (dims, ((), ())), preferred_element_type=jnp.float32)


NT = ((1,), (1,))


def prepare(
    cols,
    image,
    row_sums,
    col_sums,
    row_op,
    own_op,
    inner_op,
    ends_op,
    block,
    row_own,
    col_own,
    other_table,
    col_table,
    by_rows,
    by_cols,
    own_table,
    sems,
):
    row, col = lax.axis_index("row"), lax.axis_index("col")
    half = lax.rem(row, 2)
    width = image.shape[1]
    variant = jnp.where(col == 0, 0, jnp.where(col == cols - 1, 2, 1))
    window = pl.multiple_of(SENT * (cols - col), SENT)
    last = width + SENT * (cols - 1)

    def col_rows(start, count):
        return col_own.at[:, pl.ds(start, count)]

    pairs = [
        (image, block),
        (row_sums.at[half], own_table),
        (col_sums, col_table),
        (row_sums.at[1 - half], other_table),
        (row_op.at[row], row_own),
        (own_op.at[variant], col_rows(0, width)),
        (ends_op.at[col, 0], col_rows(width, SENT)),
        (
            inner_op.at[:, pl.ds(window, SENT * (cols - 2))],
            col_rows(width + SENT, SENT * (cols - 2)),
        ),
        (ends_op.at[col, 1], col_rows(last, SENT)),
    ]
    copies = [pltpu.make_async_copy(*pair, sems.at[i]) for i, pair in enumerate(pairs)]
    for copy in copies:
        copy.start()
    for copy in copies[:3]:
        copy.wait()
    cells = split(block[...])
    by_rows[...] = dot3([own_table[i] for i in range(2)], cells)
    by_cols[...] = dot3([col_table[i, :COL_ROWS] for i in range(2)], cells, NT)
    rest = col_own.shape[1] - last - SENT
    if rest:
        col_own[:, last + SENT :] = jnp.zeros((2, rest, col_own.shape[2]), jnp.bfloat16)
    for copy in copies[3:]:
        copy.wait()


def after(values):
    return values[CAUSAL : CAUSAL + SENT]


def before(values):
    return values[FIRST : FIRST + SENT]


def lane_place(shape):
    return lax.broadcasted_iota(jnp.int32, shape, 1) // SENT


def pack(rows, cols, other, other_table, col_table, by_rows, by_cols, sent, near):
    row, col = lax.axis_index("row"), lax.axis_index("col")
    chip, half = row // 2, lax.rem(row, 2)
    cells = split(other[...])
    own_rows = by_rows[...]
    other_rows = dot3([other_table[i] for i in range(2)], cells)
    other_cols = dot3([col_table[i, :COL_ROWS] for i in range(2)], cells, NT)
    near[...] = other_rows[BASIS : BASIS + SENT]
    over_rows = own_rows[:BASIS] + other_rows[:BASIS]
    own_near, other_near = own_rows[BASIS : BASIS + SENT], near[...]
    own_cols = by_cols[...]
    is_first = half == 0
    nears = [
        jnp.where(is_first, own_near, other_near),
        jnp.where(is_first, other_near, own_near),
    ]
    over_cols = [
        jnp.where(is_first, own_cols, other_cols),
        jnp.where(is_first, other_cols, own_cols),
    ]
    corners = dot3(
        split(jnp.concatenate([over_rows] + nears)),
        [col_table[i, COL_ROWS:] for i in range(2)],
        NT,
    )

    def share(values):
        return jnp.where(is_first, values[: SENT // 2], values[SENT // 2 :])

    straight = [share(after(over_rows)), share(before(over_rows))]
    across, flat, placed = [], [], []
    for to_half in range(2):
        across.append([share(after(over_cols[to_half])), share(before(over_cols[to_half]))])
    for side in range(2):
        tiled = corners[:, LANES * side : LANES * (side + 1)]
        mine = lane_place(tiled.shape) == lax.rem(col, LANES // SENT)
        masked = jnp.where(mine, tiled, 0.0)
        placed.append([share(after(masked)), share(before(masked))])
        lines = []
        for to_half in range(2):
            start = BASIS + SENT * (1 - to_half)
            part = share(tiled[start : start + SENT])
            diagonal = lane_place(part.shape) == lax.broadcasted_iota(jnp.int32, part.shape, 0)
            lines.append(jnp.sum(jnp.where(diagonal, part, 0.0), axis=0, keepdims=True))
        flat.append(lines)
    none = jnp.zeros((1, LANES), jnp.float32)
    for to_chip in range(rows // 2):
        is_after = to_chip > chip
        is_here = to_chip == chip
        line = jnp.where(is_after, straight[0], straight[1])
        sides = [jnp.where(is_after, *placed[side]) for side in range(2)]
        for to_half in range(2):
            for to_col in range(cols):
                is_right = to_col > col
                body = jnp.where(to_col == col, line, jnp.where(is_right, *sides))
                body = jnp.where(is_here, jnp.where(is_right, *across[to_half]), body)
                tail = jnp.where(is_right, flat[0][to_half], flat[1][to_half])
                at = PIECE * ((2 * to_chip + to_half) * cols + to_col)
                sent[at : at + PIECE - 1] = body
                sent[at + PIECE - 1 : at + PIECE] = jnp.where(is_here, tail, none)


def combine(rows, cols, block, got, near, row_own, col_own, out, staged, sems):
    row, col = lax.axis_index("row"), lax.axis_index("col")
    chip = row // 2
    length, width = block.shape
    groups = -(-SENT * cols // LANES)
    per_group = LANES // SENT
    nothing = jnp.zeros((SENT, LANES), jnp.float32)
    half_shape = (SENT // 2, LANES)
    diagonal = lane_place(half_shape) == lax.broadcasted_iota(jnp.int32, half_shape, 0)

    def piece(from_chip, from_col):
        ats = [PIECE * ((2 * from_chip + half) * cols + from_col) for half in range(2)]
        return jnp.concatenate([got[at : at + PIECE - 1] for at in ats])

    def corner(from_chip, from_col):
        ats = [PIECE * ((2 * from_chip + half) * cols + from_col) for half in range(2)]
        tails = [got[at + PIECE - 1 : at + PIECE] for at in ats]
        return jnp.concatenate([jnp.where(diagonal, tail, 0.0) for tail in tails])

    across, lower = [], []
    corners = [nothing] * groups
    pieces = [[piece(i, j) for j in range(cols)] for i in range(rows // 2)]
    for from_col in range(cols):
        here = nothing
        tail = nothing
        for from_chip in range(rows // 2):
            here = jnp.where(from_chip == chip, pieces[from_chip][from_col], here)
            tail = jnp.where(from_chip == chip, corner(from_chip, from_col), tail)
        across.append(here)
        shift = LANES // 2
        while shift >= SENT:
            tail = tail + pltpu.roll(tail, shift, 1)
            shift //= 2
        wanted = (lane_place(tail.shape) == from_col % per_group) & (from_col != col)
        corners[from_col // per_group] += jnp.where(wanted, tail, 0.0)
    if groups * per_group > cols:
        across.append(jnp.zeros((groups * LANES - SENT * cols, length), jnp.float32))
    upper = jnp.concatenate([block[...], jnp.concatenate(across).T], axis=1)
    for from_chip in range(rows // 2):
        is_here = from_chip == chip
        line = near[...]
        parts = [jnp.where(is_here, corner_sum, 0.0) for corner_sum in corners]
        for from_col in range(cols):
            found = pieces[from_chip][from_col]
            is_col = from_col == col
            line = jnp.where(jnp.logical_not(is_here) & is_col, found, line)
            group = from_col // per_group
            parts[group] += jnp.where(is_here | is_col, 0.0, found)
        lower.append(jnp.concatenate([line] + parts, axis=1))
    known = split(jnp.concatenate([upper] + lower))
    along_cols = dot3(known, [col_own[i] for i in range(2)])
    fill = row_own.shape[-1] - along_cols.shape[0]
    copies = []
    for level in range(2):
        span = 3 * width
        smoothed = split(along_cols[:, span * level : span * (level + 1)])
        if fill:
            rest = jnp.zeros((fill, span), jnp.bfloat16)
            smoothed = [jnp.concatenate([part, rest]) for part in smoothed]
        products = [
            dot3(
                [row_own[i, level, k] for i in range(2)],
                [part[:, : (3 - k) * width] for part in smoothed],
            )
            for k in range(3)
        ]
        for f, (row_stencil, col_stencil) in enumerate(FEATURES):
            feature = products[row_stencil][:, width * col_stencil : width * (col_stencil + 1)]
            channel = len(FEATURES) * level + f
            staged[channel] = feature.astype(jnp.bfloat16)
            copies.append(
                pltpu.make_async_copy(staged.at[channel], out.at[channel], sems.at[channel])
            )
            copies[-1].start()
    for copy in copies:
        copy.wait()


def row_tables(height, rows):
    def sources(block):
        chips = [(2 * height * chip, 2 * height) for chip in range(rows // 2)]
        chips[block // 2] = ((block ^ 1) * height, height)
        return chips

    base = [2.0 * math.sqrt(math.pi) * s for s in DEVIATIONS]
    gains = [[b * s**k for k in range(3)] for b, s in zip(base, DEVIATIONS)]
    whole, single = summary_table(2 * height), summary_table(height)
    sums = np.zeros((2, ROW_ROWS, height))
    for half, own in enumerate((after(single), before(single))):
        sums[half, :BASIS] = whole[:, half * height : (half + 1) * height]
        sums[half, BASIS : BASIS + SENT] = own
    return operator_tables(height, rows, sources, gains), sums


def col_tables(width, cols):
    def sources(block):
        return [None if b == block else (b * width, width) for b in range(cols)]

    gains = [[s**k for k in range(3)] for s in DEVIATIONS]
    single = summary_table(width)
    sums = np.zeros((COL_ROWS + 2 * LANES, width))
    sums[:BASIS] = single
    sums[COL_ROWS:] = np.concatenate(
        [np.tile(part, (LANES // SENT, 1)) for part in (after(single), before(single))]
    )
    return operator_tables(width, cols, sources, gains), sums


def on_device(rows, cols, image):
    height, width = image.shape
    row_weights, row_sums = row_tables(height, rows)
    col_weights, col_sums = col_tables(width, cols)
    row_op = np.moveaxis(split_table(row_weights), 0, 1)
    col_ops = window_tables(col_weights, width, cols)
    row_sums = np.moveaxis(split_table(row_sums), 0, 1)
    col_sums = split_table(col_sums)

    def in_vmem(count):
        return [pl.BlockSpec(memory_space=pltpu.VMEM)] * count

    params = pltpu.CompilerParams(vmem_limit_bytes=16 * 1024 * 1024)
    operands = [jnp.asarray(x) for x in (row_sums, col_sums, row_op, *col_ops)]
    operands = [pltpu.with_memory_space_constraint(x, pltpu.HBM) for x in [image] + operands]
    other = lax.ppermute(image, "row", [(i, i ^ 1) for i in range(rows)])
    block, row_own, col_own, other_table, col_table, by_rows, by_cols = pl.pallas_call(
        lambda *refs: prepare(cols, *refs),
        out_shape=[
            pltpu.VMEM((height, width), jnp.float32),
            pltpu.VMEM(row_op.shape[1:], jnp.bfloat16),
            pltpu.VMEM((2, col_weights.shape[-1], 6 * width), jnp.bfloat16),
            pltpu.VMEM(row_sums.shape[1:], jnp.bfloat16),
            pltpu.VMEM(col_sums.shape, jnp.bfloat16),
            pltpu.VMEM((ROW_ROWS, width), jnp.float32),
            pltpu.VMEM((COL_ROWS, height), jnp.float32),
        ],
        in_specs=[pl.BlockSpec(memory_space=pltpu.HBM)] * len(operands),
        out_specs=in_vmem(7),
        scratch_shapes=[
            pltpu.VMEM(row_sums.shape[1:], jnp.bfloat16),
            pltpu.SemaphoreType.DMA((9,)),
        ],
        compiler_params=params,
        cost_estimate=pl.CostEstimate(
            flops=6 * (ROW_ROWS + COL_ROWS) * height * width,
            bytes_accessed=4 * 1024 * 1024,
            transcendentals=0,
        ),
        name="prepare",
    )(*operands)
    sent, near = pl.pallas_call(
        lambda *refs: pack(rows, cols, *refs),
        out_shape=[
            pltpu.VMEM((PIECE * rows * cols, LANES), jnp.float32),
            pltpu.VMEM((SENT, width), jnp.float32),
        ],
        in_specs=in_vmem(5),
        out_specs=in_vmem(2),
        compiler_params=params,
        name="pack",
    )(other, other_table, col_table, by_rows, by_cols)
    got = lax.all_to_all(sent.reshape(rows * cols, PIECE, 1, LANES), ("row", "col"), 0, 0)
    features = 2 * len(FEATURES)
    return pl.pallas_call(
        lambda *refs: combine(rows, cols, *refs),
        out_shape=jax.ShapeDtypeStruct((features, height, width), jnp.bfloat16),
        in_specs=in_vmem(5),
        out_specs=pl.BlockSpec(memory_space=pl.ANY),
        scratch_shapes=[
            pltpu.VMEM((features, height, width), jnp.bfloat16),
            pltpu.SemaphoreType.DMA((features,)),
        ],
        compiler_params=params,
        name="combine",
    )(block, got.reshape(sent.shape), near, row_own, col_own)


def solution(mesh):
    rows, cols = mesh.shape["row"], mesh.shape["col"]
    return jax.shard_map(
        lambda image: on_device(rows, cols, image),
        mesh=mesh,
        in_specs=(P("row", "col"),),
        out_specs=P(None, "row", "col"),
        check_vma=False,
    )
```

```python
import math

import jax
import jax.numpy as jnp
import ml_dtypes
import numpy as np
from jax import lax
from jax.experimental import pallas as pl
from jax.experimental.pallas import tpu as pltpu
from jax.sharding import PartitionSpec as P

SIG_A = 128
SIG_B = 256
DEVIATIONS = (SIG_A, SIG_B)

DER_FIRST = (
    1.0 / 280,
    -4.0 / 105,
    1.0 / 5,
    -4.0 / 5,
    0.0,
    4.0 / 5,
    -1.0 / 5,
    4.0 / 105,
    -1.0 / 280,
)
DER_SECOND = (
    -1.0 / 560,
    8.0 / 315,
    -1.0 / 5,
    8.0 / 5,
    -205.0 / 72,
    8.0 / 5,
    -1.0 / 5,
    8.0 / 315,
    -1.0 / 560,
)
IDENTITY = (0.0, 0.0, 0.0, 0.0, 1.0, 0.0, 0.0, 0.0, 0.0)
STENCILS = (IDENTITY, DER_FIRST, DER_SECOND)
DERICHE_POLES = ((1.68, 3.735, 1.783, 0.6318), (-0.6803, -0.2598, 1.723, 1.997))
FEATURES = ((0, 0), (0, 1), (1, 0), (0, 2), (1, 1), (2, 0))

HALO = 4
CAUSAL, FIRST, LAST, ANTICAUSAL = 0, 8, 12, 16
BASIS = 24
SENT = 16
LANES = 128
ROW_ROWS = 48
COL_ROWS = 32
PIECE = SENT // 2 + 1


def pole_values(deviation):
    normal_sum = 0.0
    for cos_weight, sin_weight, decay, freq in DERICHE_POLES:
        z = np.exp(complex(-decay, freq) / deviation)
        q = z / (1.0 - z)
        normal_sum += cos_weight + 2.0 * (cos_weight * q.real + sin_weight * q.imag)
    weights = [complex(cw, -sw) / normal_sum for cw, sw, _, _ in DERICHE_POLES]
    exponents = [complex(decay, -freq) / deviation for _, _, decay, freq in DERICHE_POLES]
    return np.array(weights), np.array(exponents)


def all_poles():
    return [pole_values(deviation) for deviation in DEVIATIONS]


def smooth_kernel(poles, distance):
    weights, exponents = poles
    return sum(
        (w * np.exp(-e * np.abs(distance))).real for w, e in zip(weights, exponents)
    )


def summary_table(length):
    cells = np.arange(length)
    table = np.zeros((BASIS, length))
    row = 0
    for _, exponents in all_poles():
        for e in exponents:
            causal = np.exp(-e * (length - 1 - cells))
            anticausal = np.exp(-e * cells)
            table[CAUSAL + row], table[CAUSAL + row + 1] = causal.real, causal.imag
            table[ANTICAUSAL + row], table[ANTICAUSAL + row + 1] = (
                anticausal.real,
                anticausal.imag,
            )
            row += 2
    for i in range(HALO):
        table[FIRST + i, i] = 1.0
        table[LAST + i, length - HALO + i] = 1.0
    return table


def cell_weight(poles, stencil, out_cells, in_cells, total):
    result = np.zeros((len(out_cells), len(in_cells)))
    for t in range(-HALO, HALO + 1):
        field_cells = in_cells - t
        inside = (field_cells >= 0) & (field_cells < total)
        distance = out_cells[:, None] - field_cells[None, :]
        result += stencil[t + HALO] * smooth_kernel(poles, distance) * inside[None, :]
    return result


def summary_weight(level, stencil, out_start, length, start, extent, total):
    poles = all_poles()[level]
    weights, exponents = poles
    out_cells = out_start + np.arange(length)
    after = out_start > start
    base = CAUSAL if after else FIRST
    offset = (CAUSAL if after else ANTICAUSAL) + 4 * level
    sign = 1.0 if after else -1.0
    anchor = start + (extent - 1 if after else 0)
    table = np.zeros((length, BASIS))
    for p, (w, e) in enumerate(zip(weights, exponents)):
        eigen = sum(stencil[t + HALO] * np.exp(-sign * e * t) for t in range(-HALO, HALO + 1))
        gain = w * eigen * np.exp(-e * np.abs(out_cells - anchor))
        table[:, offset + 2 * p] = gain.real
        table[:, offset + 2 * p + 1] = -gain.imag

    def far_form(cells):
        result = np.zeros((length, len(cells)))
        for t in range(-HALO, HALO + 1):
            distance = sign * (out_cells[:, None] - (cells - t)[None, :])
            result += stencil[t + HALO] * sum(
                (w * np.exp(-e * distance)).real for w, e in zip(weights, exponents)
            )
        return result

    for position, first in ((FIRST, start), (LAST, start + extent - HALO)):
        cells = first + np.arange(HALO)
        at_end = (cells[0] == 0) or (cells[-1] == total - 1)
        adjacent = (cells[-1] + 1 == out_cells[0]) or (out_cells[-1] + 1 == cells[0])
        if at_end or adjacent:
            table[:, position : position + HALO] = cell_weight(
                poles, stencil, out_cells, cells, total
            ) - far_form(cells)
    return table[:, base : base + SENT]


def operator_tables(length, blocks, sources, gains):
    remote = -(-SENT * len(sources(0)) // LANES) * LANES
    tables = np.zeros((blocks, 2, 3, length, length + remote))
    total = length * blocks
    for block in range(blocks):
        cells = block * length + np.arange(length)
        for level, poles in enumerate(all_poles()):
            for k, stencil in enumerate(STENCILS):
                view = tables[block, level, k]
                view[:, :length] = cell_weight(poles, stencil, cells, cells, total)
                for place, source in enumerate(sources(block)):
                    if source is not None:
                        at = length + SENT * place
                        view[:, at : at + SENT] = summary_weight(
                            level, stencil, cells[0], length, *source, total
                        )
                view *= gains[level][k]
    return tables


def window_tables(tables, length, blocks):
    middle = blocks // 2
    own = np.stack([tables[b, ..., :length] for b in (0, middle, blocks - 1)])
    inner = np.zeros((2 * blocks - 1,) + tables.shape[1:-1] + (SENT,))
    for block in range(blocks):
        for source in range(1, blocks - 1):
            start = length + SENT * source
            inner[source - block + blocks - 1] = tables[block, ..., start : start + SENT]
    ends = np.stack(
        [
            tables[..., length + SENT * end : length + SENT * (end + 1)]
            for end in (0, blocks - 1)
        ],
        axis=1,
    )

    def cells_first(table, lead):
        moved = np.moveaxis(table, -1, lead)
        return moved.reshape(moved.shape[: lead + 1] + (-1,))

    inner = cells_first(inner, 1)
    return (
        np.moveaxis(split_table(cells_first(own, 1)), 0, 1),
        split_table(inner.reshape(-1, inner.shape[-1])),
        np.moveaxis(split_table(cells_first(ends, 2)), 0, 2),
    )


def split_table(values):
    high = values.astype(ml_dtypes.bfloat16)
    low = (values - high.astype(np.float64)).astype(ml_dtypes.bfloat16)
    return np.stack([high, low])


def split(values):
    high = values.astype(jnp.bfloat16)
    low = (values - high.astype(jnp.float32)).astype(jnp.bfloat16)
    return high, low


def dot3(left, right, dims=((1,), (0,))):
    left = jnp.concatenate([left[0], left[0], left[1]], axis=dims[0][0])
    right = jnp.concatenate([right[0], right[1], right[0]], axis=dims[1][0])
    return lax.dot_general(left, right, (dims, ((), ())), preferred_element_type=jnp.float32)


NT = ((1,), (1,))


def prepare(
    cols,
    image,
    row_sums,
    col_sums,
    row_op,
    own_op,
    inner_op,
    ends_op,
    block,
    row_own,
    col_own,
    other_table,
    col_table,
    by_rows,
    by_cols,
    own_table,
    sems,
):
    row, col = lax.axis_index("row"), lax.axis_index("col")
    half = lax.rem(row, 2)
    width = image.shape[1]
    variant = jnp.where(col == 0, 0, jnp.where(col == cols - 1, 2, 1))
    window = pl.multiple_of(SENT * (cols - col), SENT)
    last = width + SENT * (cols - 1)

    def col_rows(start, count):
        return col_own.at[:, pl.ds(start, count)]

    pairs = [
        (image, block),
        (row_sums.at[half], own_table),
        (col_sums, col_table),
        (row_sums.at[1 - half], other_table),
        (row_op.at[row], row_own),
        (own_op.at[variant], col_rows(0, width)),
        (ends_op.at[col, 0], col_rows(width, SENT)),
        (
            inner_op.at[:, pl.ds(window, SENT * (cols - 2))],
            col_rows(width + SENT, SENT * (cols - 2)),
        ),
        (ends_op.at[col, 1], col_rows(last, SENT)),
    ]
    copies = [pltpu.make_async_copy(*pair, sems.at[i]) for i, pair in enumerate(pairs)]
    for copy in copies:
        copy.start()
    for copy in copies[:3]:
        copy.wait()
    cells = split(block[...])
    by_rows[...] = dot3([own_table[i] for i in range(2)], cells)
    by_cols[...] = dot3([col_table[i, :COL_ROWS] for i in range(2)], cells, NT)
    rest = col_own.shape[1] - last - SENT
    if rest:
        col_own[:, last + SENT :] = jnp.zeros((2, rest, col_own.shape[2]), jnp.bfloat16)
    for copy in copies[3:]:
        copy.wait()


def exchange_order(rows, cols):
    def place(device):
        row, col = divmod(device, cols)
        return col % 2, row % 2, col // 2, row // 2

    return sorted(range(rows * cols), key=place)


def after(values):
    return values[CAUSAL : CAUSAL + SENT]


def before(values):
    return values[FIRST : FIRST + SENT]


def lane_place(shape):
    return lax.broadcasted_iota(jnp.int32, shape, 1) // SENT


def pack(rows, cols, other, other_table, col_table, by_rows, by_cols, sent, near):
    row, col = lax.axis_index("row"), lax.axis_index("col")
    chip, half = row // 2, lax.rem(row, 2)
    cells = split(other[...])
    own_rows = by_rows[...]
    other_rows = dot3([other_table[i] for i in range(2)], cells)
    other_cols = dot3([col_table[i, :COL_ROWS] for i in range(2)], cells, NT)
    near[...] = other_rows[BASIS : BASIS + SENT]
    over_rows = own_rows[:BASIS] + other_rows[:BASIS]
    own_near, other_near = own_rows[BASIS : BASIS + SENT], near[...]
    own_cols = by_cols[...]
    is_first = half == 0
    nears = [
        jnp.where(is_first, own_near, other_near),
        jnp.where(is_first, other_near, own_near),
    ]
    over_cols = [
        jnp.where(is_first, own_cols, other_cols),
        jnp.where(is_first, other_cols, own_cols),
    ]
    corners = dot3(
        split(jnp.concatenate([over_rows] + nears)),
        [col_table[i, COL_ROWS:] for i in range(2)],
        NT,
    )

    def share(values):
        return jnp.where(is_first, values[: SENT // 2], values[SENT // 2 :])

    straight = [share(after(over_rows)), share(before(over_rows))]
    across, flat, placed = [], [], []
    for to_half in range(2):
        across.append([share(after(over_cols[to_half])), share(before(over_cols[to_half]))])
    for side in range(2):
        tiled = corners[:, LANES * side : LANES * (side + 1)]
        mine = lane_place(tiled.shape) == lax.rem(col, LANES // SENT)
        masked = jnp.where(mine, tiled, 0.0)
        placed.append([share(after(masked)), share(before(masked))])
        lines = []
        for to_half in range(2):
            start = BASIS + SENT * (1 - to_half)
            part = share(tiled[start : start + SENT])
            diagonal = lane_place(part.shape) == lax.broadcasted_iota(jnp.int32, part.shape, 0)
            lines.append(jnp.sum(jnp.where(diagonal, part, 0.0), axis=0, keepdims=True))
        flat.append(lines)
    none = jnp.zeros((1, LANES), jnp.float32)
    order = exchange_order(rows, cols)
    for to_chip in range(rows // 2):
        is_after = to_chip > chip
        is_here = to_chip == chip
        line = jnp.where(is_after, straight[0], straight[1])
        sides = [jnp.where(is_after, *placed[side]) for side in range(2)]
        for to_half in range(2):
            for to_col in range(cols):
                is_right = to_col > col
                body = jnp.where(to_col == col, line, jnp.where(is_right, *sides))
                body = jnp.where(is_here, jnp.where(is_right, *across[to_half]), body)
                tail = jnp.where(is_right, flat[0][to_half], flat[1][to_half])
                at = PIECE * order.index((2 * to_chip + to_half) * cols + to_col)
                sent[at : at + PIECE - 1] = body
                sent[at + PIECE - 1 : at + PIECE] = jnp.where(is_here, tail, none)


def combine(rows, cols, block, got, near, row_own, col_own, out, staged, sems):
    row, col = lax.axis_index("row"), lax.axis_index("col")
    chip = row // 2
    length, width = block.shape
    groups = -(-SENT * cols // LANES)
    per_group = LANES // SENT
    order = exchange_order(rows, cols)
    nothing = jnp.zeros((SENT, LANES), jnp.float32)
    half_shape = (SENT // 2, LANES)
    diagonal = lane_place(half_shape) == lax.broadcasted_iota(jnp.int32, half_shape, 0)

    def places(from_chip, from_col):
        devices = [(2 * from_chip + half) * cols + from_col for half in range(2)]
        return [PIECE * order.index(device) for device in devices]

    def piece(from_chip, from_col):
        ats = places(from_chip, from_col)
        return jnp.concatenate([got[at : at + PIECE - 1] for at in ats])

    def corner(from_chip, from_col):
        ats = places(from_chip, from_col)
        tails = [got[at + PIECE - 1 : at + PIECE] for at in ats]
        return jnp.concatenate([jnp.where(diagonal, tail, 0.0) for tail in tails])

    across, lower = [], []
    corners = [nothing] * groups
    pieces = [[piece(i, j) for j in range(cols)] for i in range(rows // 2)]
    for from_col in range(cols):
        here = nothing
        tail = nothing
        for from_chip in range(rows // 2):
            here = jnp.where(from_chip == chip, pieces[from_chip][from_col], here)
            tail = jnp.where(from_chip == chip, corner(from_chip, from_col), tail)
        across.append(here)
        shift = LANES // 2
        while shift >= SENT:
            tail = tail + pltpu.roll(tail, shift, 1)
            shift //= 2
        wanted = (lane_place(tail.shape) == from_col % per_group) & (from_col != col)
        corners[from_col // per_group] += jnp.where(wanted, tail, 0.0)
    if groups * per_group > cols:
        across.append(jnp.zeros((groups * LANES - SENT * cols, length), jnp.float32))
    upper = jnp.concatenate([block[...], jnp.concatenate(across).T], axis=1)
    for from_chip in range(rows // 2):
        is_here = from_chip == chip
        line = near[...]
        parts = [jnp.where(is_here, corner_sum, 0.0) for corner_sum in corners]
        for from_col in range(cols):
            found = pieces[from_chip][from_col]
            is_col = from_col == col
            line = jnp.where(jnp.logical_not(is_here) & is_col, found, line)
            group = from_col // per_group
            parts[group] += jnp.where(is_here | is_col, 0.0, found)
        lower.append(jnp.concatenate([line] + parts, axis=1))
    known = split(jnp.concatenate([upper] + lower))
    along_cols = dot3(known, [col_own[i] for i in range(2)])
    fill = row_own.shape[-1] - along_cols.shape[0]
    copies = []
    for level in range(2):
        span = 3 * width
        smoothed = split(along_cols[:, span * level : span * (level + 1)])
        if fill:
            rest = jnp.zeros((fill, span), jnp.bfloat16)
            smoothed = [jnp.concatenate([part, rest]) for part in smoothed]
        products = [
            dot3(
                [row_own[i, level, k] for i in range(2)],
                [part[:, : (3 - k) * width] for part in smoothed],
            )
            for k in range(3)
        ]
        for f, (row_stencil, col_stencil) in enumerate(FEATURES):
            feature = products[row_stencil][:, width * col_stencil : width * (col_stencil + 1)]
            channel = len(FEATURES) * level + f
            staged[channel] = feature.astype(jnp.bfloat16)
            copies.append(
                pltpu.make_async_copy(staged.at[channel], out.at[channel], sems.at[channel])
            )
            copies[-1].start()
    for copy in copies:
        copy.wait()


def row_tables(height, rows):
    def sources(block):
        chips = [(2 * height * chip, 2 * height) for chip in range(rows // 2)]
        chips[block // 2] = ((block ^ 1) * height, height)
        return chips

    base = [2.0 * math.sqrt(math.pi) * s for s in DEVIATIONS]
    gains = [[b * s**k for k in range(3)] for b, s in zip(base, DEVIATIONS)]
    whole, single = summary_table(2 * height), summary_table(height)
    sums = np.zeros((2, ROW_ROWS, height))
    for half, own in enumerate((after(single), before(single))):
        sums[half, :BASIS] = whole[:, half * height : (half + 1) * height]
        sums[half, BASIS : BASIS + SENT] = own
    return operator_tables(height, rows, sources, gains), sums


def col_tables(width, cols):
    def sources(block):
        return [None if b == block else (b * width, width) for b in range(cols)]

    gains = [[s**k for k in range(3)] for s in DEVIATIONS]
    single = summary_table(width)
    sums = np.zeros((COL_ROWS + 2 * LANES, width))
    sums[:BASIS] = single
    sums[COL_ROWS:] = np.concatenate(
        [np.tile(part, (LANES // SENT, 1)) for part in (after(single), before(single))]
    )
    return operator_tables(width, cols, sources, gains), sums


def on_device(rows, cols, image):
    height, width = image.shape
    row_weights, row_sums = row_tables(height, rows)
    col_weights, col_sums = col_tables(width, cols)
    row_op = np.moveaxis(split_table(row_weights), 0, 1)
    col_ops = window_tables(col_weights, width, cols)
    row_sums = np.moveaxis(split_table(row_sums), 0, 1)
    col_sums = split_table(col_sums)

    def in_vmem(count):
        return [pl.BlockSpec(memory_space=pltpu.VMEM)] * count

    params = pltpu.CompilerParams(vmem_limit_bytes=16 * 1024 * 1024)
    operands = [jnp.asarray(x) for x in (row_sums, col_sums, row_op, *col_ops)]
    operands = [pltpu.with_memory_space_constraint(x, pltpu.HBM) for x in [image] + operands]
    other = lax.ppermute(image, "row", [(i, i ^ 1) for i in range(rows)])
    block, row_own, col_own, other_table, col_table, by_rows, by_cols = pl.pallas_call(
        lambda *refs: prepare(cols, *refs),
        out_shape=[
            pltpu.VMEM((height, width), jnp.float32),
            pltpu.VMEM(row_op.shape[1:], jnp.bfloat16),
            pltpu.VMEM((2, col_weights.shape[-1], 6 * width), jnp.bfloat16),
            pltpu.VMEM(row_sums.shape[1:], jnp.bfloat16),
            pltpu.VMEM(col_sums.shape, jnp.bfloat16),
            pltpu.VMEM((ROW_ROWS, width), jnp.float32),
            pltpu.VMEM((COL_ROWS, height), jnp.float32),
        ],
        in_specs=[pl.BlockSpec(memory_space=pltpu.HBM)] * len(operands),
        out_specs=in_vmem(7),
        scratch_shapes=[
            pltpu.VMEM(row_sums.shape[1:], jnp.bfloat16),
            pltpu.SemaphoreType.DMA((9,)),
        ],
        compiler_params=params,
        cost_estimate=pl.CostEstimate(
            flops=6 * (ROW_ROWS + COL_ROWS) * height * width,
            bytes_accessed=4 * 1024 * 1024,
            transcendentals=0,
        ),
        name="prepare",
    )(*operands)
    sent, near = pl.pallas_call(
        lambda *refs: pack(rows, cols, *refs),
        out_shape=[
            pltpu.VMEM((PIECE * rows * cols, LANES), jnp.float32),
            pltpu.VMEM((SENT, width), jnp.float32),
        ],
        in_specs=in_vmem(5),
        out_specs=in_vmem(2),
        compiler_params=params,
        name="pack",
    )(other, other_table, col_table, by_rows, by_cols)
    got = lax.all_to_all(
        sent.reshape(rows * cols, PIECE, 1, LANES),
        ("row", "col"),
        0,
        0,
        axis_index_groups=[exchange_order(rows, cols)],
    )
    features = 2 * len(FEATURES)
    return pl.pallas_call(
        lambda *refs: combine(rows, cols, *refs),
        out_shape=jax.ShapeDtypeStruct((features, height, width), jnp.bfloat16),
        in_specs=in_vmem(5),
        out_specs=pl.BlockSpec(memory_space=pl.ANY),
        scratch_shapes=[
            pltpu.VMEM((features, height, width), jnp.bfloat16),
            pltpu.SemaphoreType.DMA((features,)),
        ],
        compiler_params=params,
        name="combine",
    )(block, got.reshape(sent.shape), near, row_own, col_own)


def solution(mesh):
    rows, cols = mesh.shape["row"], mesh.shape["col"]
    return jax.shard_map(
        lambda image: on_device(rows, cols, image),
        mesh=mesh,
        in_specs=(P("row", "col"),),
        out_specs=P(None, "row", "col"),
        check_vma=False,
    )
```

```python
import math

import jax
import jax.numpy as jnp
import ml_dtypes
import numpy as np
from jax import lax
from jax.experimental import pallas as pl
from jax.experimental.pallas import tpu as pltpu
from jax.sharding import PartitionSpec as P

SIG_A = 128
SIG_B = 256
DEVIATIONS = (SIG_A, SIG_B)

DER_FIRST = (
    1.0 / 280,
    -4.0 / 105,
    1.0 / 5,
    -4.0 / 5,
    0.0,
    4.0 / 5,
    -1.0 / 5,
    4.0 / 105,
    -1.0 / 280,
)
DER_SECOND = (
    -1.0 / 560,
    8.0 / 315,
    -1.0 / 5,
    8.0 / 5,
    -205.0 / 72,
    8.0 / 5,
    -1.0 / 5,
    8.0 / 315,
    -1.0 / 560,
)
IDENTITY = (0.0, 0.0, 0.0, 0.0, 1.0, 0.0, 0.0, 0.0, 0.0)
STENCILS = (IDENTITY, DER_FIRST, DER_SECOND)
DERICHE_POLES = ((1.68, 3.735, 1.783, 0.6318), (-0.6803, -0.2598, 1.723, 1.997))
FEATURES = ((0, 0), (0, 1), (1, 0), (0, 2), (1, 1), (2, 0))

HALO = 4
CAUSAL, FIRST, LAST, ANTICAUSAL = 0, 8, 12, 16
BASIS = 24
SENT = 16
LANES = 128
OWN_ROWS, OTHER_ROWS, COL_ROWS = slice(0, 48), slice(48, 96), slice(96, 128)
TILED_ROWS = slice(128, 128 + 2 * LANES)
PIECE = SENT // 2 + 1


def pole_values(deviation):
    normal_sum = 0.0
    for cos_weight, sin_weight, decay, freq in DERICHE_POLES:
        z = np.exp(complex(-decay, freq) / deviation)
        q = z / (1.0 - z)
        normal_sum += cos_weight + 2.0 * (cos_weight * q.real + sin_weight * q.imag)
    weights = [complex(cw, -sw) / normal_sum for cw, sw, _, _ in DERICHE_POLES]
    exponents = [complex(decay, -freq) / deviation for _, _, decay, freq in DERICHE_POLES]
    return np.array(weights), np.array(exponents)


def all_poles():
    return [pole_values(deviation) for deviation in DEVIATIONS]


def smooth_kernel(poles, distance):
    weights, exponents = poles
    return sum(
        (w * np.exp(-e * np.abs(distance))).real for w, e in zip(weights, exponents)
    )


def summary_table(length):
    cells = np.arange(length)
    table = np.zeros((BASIS, length))
    row = 0
    for _, exponents in all_poles():
        for e in exponents:
            causal = np.exp(-e * (length - 1 - cells))
            anticausal = np.exp(-e * cells)
            table[CAUSAL + row], table[CAUSAL + row + 1] = causal.real, causal.imag
            table[ANTICAUSAL + row], table[ANTICAUSAL + row + 1] = (
                anticausal.real,
                anticausal.imag,
            )
            row += 2
    for i in range(HALO):
        table[FIRST + i, i] = 1.0
        table[LAST + i, length - HALO + i] = 1.0
    return table


def cell_weight(poles, stencil, out_cells, in_cells, total):
    result = np.zeros((len(out_cells), len(in_cells)))
    for t in range(-HALO, HALO + 1):
        field_cells = in_cells - t
        inside = (field_cells >= 0) & (field_cells < total)
        distance = out_cells[:, None] - field_cells[None, :]
        result += stencil[t + HALO] * smooth_kernel(poles, distance) * inside[None, :]
    return result


def summary_weight(level, stencil, out_start, length, start, extent, total):
    poles = all_poles()[level]
    weights, exponents = poles
    out_cells = out_start + np.arange(length)
    after = out_start > start
    base = CAUSAL if after else FIRST
    offset = (CAUSAL if after else ANTICAUSAL) + 4 * level
    sign = 1.0 if after else -1.0
    anchor = start + (extent - 1 if after else 0)
    table = np.zeros((length, BASIS))
    for p, (w, e) in enumerate(zip(weights, exponents)):
        eigen = sum(stencil[t + HALO] * np.exp(-sign * e * t) for t in range(-HALO, HALO + 1))
        gain = w * eigen * np.exp(-e * np.abs(out_cells - anchor))
        table[:, offset + 2 * p] = gain.real
        table[:, offset + 2 * p + 1] = -gain.imag

    def far_form(cells):
        result = np.zeros((length, len(cells)))
        for t in range(-HALO, HALO + 1):
            distance = sign * (out_cells[:, None] - (cells - t)[None, :])
            result += stencil[t + HALO] * sum(
                (w * np.exp(-e * distance)).real for w, e in zip(weights, exponents)
            )
        return result

    for position, first in ((FIRST, start), (LAST, start + extent - HALO)):
        cells = first + np.arange(HALO)
        at_end = (cells[0] == 0) or (cells[-1] == total - 1)
        adjacent = (cells[-1] + 1 == out_cells[0]) or (out_cells[-1] + 1 == cells[0])
        if at_end or adjacent:
            table[:, position : position + HALO] = cell_weight(
                poles, stencil, out_cells, cells, total
            ) - far_form(cells)
    return table[:, base : base + SENT]


def operator_tables(length, blocks, sources, gains):
    tables = np.zeros((blocks, 2, 3, length, length + SENT * len(sources(0))))
    total = length * blocks
    for block in range(blocks):
        cells = block * length + np.arange(length)
        for level, poles in enumerate(all_poles()):
            for k, stencil in enumerate(STENCILS):
                view = tables[block, level, k]
                view[:, :length] = cell_weight(poles, stencil, cells, cells, total)
                for place, source in enumerate(sources(block)):
                    if source is not None:
                        at = length + SENT * place
                        view[:, at : at + SENT] = summary_weight(
                            level, stencil, cells[0], length, *source, total
                        )
                view *= gains[level][k]
    return tables


def split_table(values):
    high = values.astype(ml_dtypes.bfloat16)
    low = (values - high.astype(np.float64)).astype(ml_dtypes.bfloat16)
    return np.stack([high, low])


def split(values):
    high = values.astype(jnp.bfloat16)
    low = (values - high.astype(jnp.float32)).astype(jnp.bfloat16)
    return high, low


def dot3(left, right, dims=((1,), (0,))):
    left = jnp.concatenate([left[0], left[0], left[1]], axis=dims[0][0])
    right = jnp.concatenate([right[0], right[1], right[0]], axis=dims[1][0])
    return lax.dot_general(left, right, (dims, ((), ())), preferred_element_type=jnp.float32)


NT = ((1,), (1,))


def prepare(image, sums, row_op, col_op, col_rest, block, table, row_own, col_own, col_slots, by_rows, by_cols, sems):
    row, col = lax.axis_index("row"), lax.axis_index("col")
    last = col_rest.shape[0] - 1
    variant = jnp.where(col == 0, 0, jnp.where(col == last, 2, 1))
    pairs = [
        (image, block),
        (sums.at[lax.rem(row, 2)], table),
        (row_op.at[row], row_own),
        (col_op.at[variant], col_own),
        (col_rest.at[col], col_slots),
    ]
    copies = [pltpu.make_async_copy(*pair, sems.at[i]) for i, pair in enumerate(pairs)]
    for copy in copies:
        copy.start()
    for copy in copies[:2]:
        copy.wait()
    cells = split(block[...])
    by_rows[...] = dot3([table[i, OWN_ROWS] for i in range(2)], cells)
    by_cols[...] = dot3([table[i, COL_ROWS] for i in range(2)], cells, NT)
    for copy in copies[2:]:
        copy.wait()


def exchange_order(rows, cols):
    def place(device):
        row, col = divmod(device, cols)
        return col % 2, row % 2, col // 2, row // 2

    return sorted(range(rows * cols), key=place)


def after(values):
    return values[CAUSAL : CAUSAL + SENT]


def before(values):
    return values[FIRST : FIRST + SENT]


def lane_place(shape):
    return lax.broadcasted_iota(jnp.int32, shape, 1) // SENT


def pack(rows, cols, other, table, by_rows, by_cols, sent, near):
    row, col = lax.axis_index("row"), lax.axis_index("col")
    chip, half = row // 2, lax.rem(row, 2)
    cells = split(other[...])
    own_rows = by_rows[...]
    other_rows = dot3([table[i, OTHER_ROWS] for i in range(2)], cells)
    other_cols = dot3([table[i, COL_ROWS] for i in range(2)], cells, NT)
    near[...] = other_rows[BASIS : BASIS + SENT]
    over_rows = own_rows[:BASIS] + other_rows[:BASIS]
    own_near, other_near = own_rows[BASIS : BASIS + SENT], near[...]
    own_cols = by_cols[...]
    is_first = half == 0
    nears = [
        jnp.where(is_first, own_near, other_near),
        jnp.where(is_first, other_near, own_near),
    ]
    over_cols = [
        jnp.where(is_first, own_cols, other_cols),
        jnp.where(is_first, other_cols, own_cols),
    ]
    corners = dot3(
        split(jnp.concatenate([over_rows] + nears)),
        [table[i, TILED_ROWS] for i in range(2)],
        NT,
    )

    def share(values):
        return jnp.where(is_first, values[: SENT // 2], values[SENT // 2 :])

    straight = [share(after(over_rows)), share(before(over_rows))]
    across, flat, placed = [], [], []
    for to_half in range(2):
        across.append([share(after(over_cols[to_half])), share(before(over_cols[to_half]))])
    for side in range(2):
        tiled = corners[:, LANES * side : LANES * (side + 1)]
        places = min(cols, LANES // SENT)
        mine = lax.rem(lane_place(tiled.shape), places) == lax.rem(col, places)
        masked = jnp.where(mine, tiled, 0.0)
        placed.append([share(after(masked)), share(before(masked))])
        lines = []
        for to_half in range(2):
            start = BASIS + SENT * (1 - to_half)
            part = share(tiled[start : start + SENT])
            line = lax.broadcasted_iota(jnp.int32, part.shape, 0)
            diagonal = lax.rem(lane_place(part.shape) + line, LANES // SENT) == lax.rem(
                col, LANES // SENT
            )
            lines.append(jnp.sum(jnp.where(diagonal, part, 0.0), axis=0, keepdims=True))
        flat.append(lines)
    none = jnp.zeros((1, LANES), jnp.float32)
    order = exchange_order(rows, cols)
    for to_chip in range(rows // 2):
        is_after = to_chip > chip
        is_here = to_chip == chip
        line = jnp.where(is_after, straight[0], straight[1])
        sides = [jnp.where(is_after, *placed[side]) for side in range(2)]
        for to_half in range(2):
            for to_col in range(cols):
                is_right = to_col > col
                body = jnp.where(to_col == col, line, jnp.where(is_right, *sides))
                body = jnp.where(is_here, jnp.where(is_right, *across[to_half]), body)
                tail = jnp.where(is_right, flat[0][to_half], flat[1][to_half])
                at = PIECE * order.index((2 * to_chip + to_half) * cols + to_col)
                sent[at : at + PIECE - 1] = body
                sent[at + PIECE - 1 : at + PIECE] = jnp.where(is_here, tail, none)


def side_by_side(values, used):
    high, low = split(values)
    if used % LANES == 0:
        return jnp.concatenate([high, low], axis=1)
    lane = lax.broadcasted_iota(jnp.int32, values.shape, 1)
    return jnp.where(lane < used, high, low)


def long_product(own, beside, tall, rest):
    left = jnp.concatenate([own[0], own[0], own[1], beside, beside], axis=1)
    none = jnp.zeros(rest[1].shape, jnp.bfloat16)
    right = jnp.concatenate([tall[0], tall[1], tall[0], rest[0], rest[0], rest[1], none])
    return jnp.dot(left, right, preferred_element_type=jnp.float32)


def combine(rows, cols, block, got, near, row_own, col_own, col_slots, out, staged, sems):
    row, col = lax.axis_index("row"), lax.axis_index("col")
    chip = row // 2
    length, width = block.shape
    groups = -(-SENT * cols // LANES)
    per_group = LANES // SENT
    order = exchange_order(rows, cols)
    nothing = jnp.zeros((SENT, LANES), jnp.float32)
    half_shape = (SENT // 2, LANES)

    def places(from_chip, from_col):
        devices = [(2 * from_chip + half) * cols + from_col for half in range(2)]
        return [PIECE * order.index(device) for device in devices]

    def piece(from_chip, from_col):
        ats = places(from_chip, from_col)
        return jnp.concatenate([got[at : at + PIECE - 1] for at in ats])

    def corner(from_chip, from_col):
        tails = [got[at + PIECE - 1 : at + PIECE] for at in places(from_chip, from_col)]
        return jnp.concatenate([jnp.broadcast_to(tail, half_shape) for tail in tails])

    across = []
    corners = [nothing] * groups
    pieces = [[piece(i, j) for j in range(cols)] for i in range(rows // 2)]
    for from_col in range(cols):
        here = nothing
        tail = nothing
        for from_chip in range(rows // 2):
            here = jnp.where(from_chip == chip, pieces[from_chip][from_col], here)
            tail = jnp.where(from_chip == chip, corner(from_chip, from_col), tail)
        across.append(here)
        tail = [
            pltpu.roll(half, 0, 1, stride=SENT, stride_axis=0)
            for half in (tail[: SENT // 2], tail[SENT // 2 :])
        ]
        tail = jnp.concatenate(tail)
        wanted = (lane_place(tail.shape) == from_col % per_group) & (from_col != col)
        corners[from_col // per_group] += jnp.where(wanted, tail, 0.0)
    if cols < per_group:
        across = across * (per_group // cols)
        corners = [part + pltpu.roll(part, SENT * cols, 1) for part in corners]
    lines = [block[...]]
    slots = [jnp.concatenate(across).T]
    for from_chip in range(rows // 2):
        is_here = from_chip == chip
        line = near[...]
        parts = [jnp.where(is_here, corner_sum, 0.0) for corner_sum in corners]
        for from_col in range(cols):
            found = pieces[from_chip][from_col]
            is_col = from_col == col
            line = jnp.where(jnp.logical_not(is_here) & is_col, found, line)
            group = from_col // per_group
            parts[group] += jnp.where(is_here | is_col, 0.0, found)
        lines.append(line)
        slots.append(jnp.concatenate(parts, axis=1))
    along_cols = long_product(
        split(jnp.concatenate(lines)),
        side_by_side(jnp.concatenate(slots), SENT * cols),
        [col_own[i] for i in range(2)],
        [col_slots[i] for i in range(2)],
    )
    copies = []
    for level in range(2):
        span = 3 * width
        smoothed = split(along_cols[:, span * level : span * (level + 1)])
        products = []
        for k in range(3):
            weights = row_own[level, k]
            met = [part[:, : (3 - k) * width] for part in smoothed]
            products.append(
                long_product(
                    [weights[:, :length], weights[:, length : 2 * length]],
                    weights[:, 2 * length :],
                    [part[:length] for part in met],
                    [part[length:] for part in met],
                )
            )
        for f, (row_stencil, col_stencil) in enumerate(FEATURES):
            feature = products[row_stencil][:, width * col_stencil : width * (col_stencil + 1)]
            channel = len(FEATURES) * level + f
            staged[channel] = feature.astype(jnp.bfloat16)
            copies.append(
                pltpu.make_async_copy(staged.at[channel], out.at[channel], sems.at[channel])
            )
            copies[-1].start()
    for copy in copies:
        copy.wait()


def row_tables(height, rows):
    def sources(block):
        chips = [(2 * height * chip, 2 * height) for chip in range(rows // 2)]
        chips[block // 2] = ((block ^ 1) * height, height)
        return chips

    base = [2.0 * math.sqrt(math.pi) * s for s in DEVIATIONS]
    gains = [[b * s**k for k in range(3)] for b, s in zip(base, DEVIATIONS)]
    whole, single = summary_table(2 * height), summary_table(height)
    sums = np.zeros((2, 48, height))
    for half, own in enumerate((after(single), before(single))):
        sums[half, :BASIS] = whole[:, half * height : (half + 1) * height]
        sums[half, BASIS : BASIS + SENT] = own
    return operator_tables(height, rows, sources, gains), sums


def col_tables(width, cols):
    def sources(block):
        return [None if b == block else (b * width, width) for b in range(cols)]

    gains = [[s**k for k in range(3)] for s in DEVIATIONS]
    single = summary_table(width)
    sums = np.zeros((32 + 2 * LANES, width))
    sums[:BASIS] = single
    sums[32:] = np.concatenate(
        [np.tile(part, (LANES // SENT, 1)) for part in (after(single), before(single))]
    )
    return operator_tables(width, cols, sources, gains), sums


def on_device(rows, cols, image):
    height, width = image.shape
    row_weights, row_sums = row_tables(height, rows)
    col_weights, col_sums = col_tables(width, cols)
    high, low = split_table(row_weights)
    row_op = np.concatenate(
        [part[..., cells] for cells in (slice(height), slice(height, None)) for part in (high, low)],
        axis=-1,
    )
    col_op = np.transpose(col_weights, (0, 4, 1, 2, 3))
    col_op = np.moveaxis(split_table(col_op.reshape(*col_op.shape[:2], -1)), 0, 1)
    col_rest = col_op[:, :, width:]
    col_op = col_op[[0, cols // 2, cols - 1], :, :width]
    sums = np.stack(
        [np.concatenate([row_sums[h], row_sums[1 - h], col_sums]) for h in range(2)]
    )
    sums = np.moveaxis(split_table(sums), 0, 1)

    def in_vmem(count):
        return [pl.BlockSpec(memory_space=pltpu.VMEM)] * count

    params = pltpu.CompilerParams(vmem_limit_bytes=16 * 1024 * 1024)
    operands = [jnp.asarray(x) for x in (sums, row_op, col_op, col_rest)]
    operands = [pltpu.with_memory_space_constraint(x, pltpu.HBM) for x in [image] + operands]
    other = lax.ppermute(image, "row", [(i, i ^ 1) for i in range(rows)])
    block, table, row_own, col_own, col_slots, by_rows, by_cols = pl.pallas_call(
        prepare,
        out_shape=[
            pltpu.VMEM((height, width), jnp.float32),
            *[pltpu.VMEM(x.shape[1:], jnp.bfloat16) for x in (sums, row_op, col_op, col_rest)],
            pltpu.VMEM((48, width), jnp.float32),
            pltpu.VMEM((32, height), jnp.float32),
        ],
        in_specs=[pl.BlockSpec(memory_space=pltpu.HBM)] * len(operands),
        out_specs=in_vmem(7),
        scratch_shapes=[pltpu.SemaphoreType.DMA((5,))],
        compiler_params=params,
        cost_estimate=pl.CostEstimate(
            flops=6 * 80 * height * width, bytes_accessed=4 * 1024 * 1024, transcendentals=0
        ),
        name="prepare",
    )(*operands)
    sent, near = pl.pallas_call(
        lambda *refs: pack(rows, cols, *refs),
        out_shape=[
            pltpu.VMEM((PIECE * rows * cols, LANES), jnp.float32),
            pltpu.VMEM((SENT, width), jnp.float32),
        ],
        in_specs=in_vmem(4),
        out_specs=in_vmem(2),
        compiler_params=params,
        name="pack",
    )(other, table, by_rows, by_cols)
    got = lax.all_to_all(
        sent.reshape(rows * cols, PIECE, 1, LANES),
        ("row", "col"),
        0,
        0,
        axis_index_groups=[exchange_order(rows, cols)],
    )
    features = 2 * len(FEATURES)
    return pl.pallas_call(
        lambda *refs: combine(rows, cols, *refs),
        out_shape=jax.ShapeDtypeStruct((features, height, width), jnp.bfloat16),
        in_specs=in_vmem(6),
        out_specs=pl.BlockSpec(memory_space=pl.ANY),
        scratch_shapes=[
            pltpu.VMEM((features, height, width), jnp.bfloat16),
            pltpu.SemaphoreType.DMA((features,)),
        ],
        compiler_params=params,
        name="combine",
    )(block, got.reshape(sent.shape), near, row_own, col_own, col_slots)


def solution(mesh):
    rows, cols = mesh.shape["row"], mesh.shape["col"]
    return jax.shard_map(
        lambda image: on_device(rows, cols, image),
        mesh=mesh,
        in_specs=(P("row", "col"),),
        out_specs=P(None, "row", "col"),
        check_vma=False,
    )
```

```python
import math

import jax
import jax.numpy as jnp
import ml_dtypes
import numpy as np
from jax import lax
from jax.experimental import pallas as pl
from jax.experimental.pallas import tpu as pltpu
from jax.sharding import PartitionSpec as P

SIG_A = 128
SIG_B = 256
DEVIATIONS = (SIG_A, SIG_B)

DER_FIRST = (
    1.0 / 280,
    -4.0 / 105,
    1.0 / 5,
    -4.0 / 5,
    0.0,
    4.0 / 5,
    -1.0 / 5,
    4.0 / 105,
    -1.0 / 280,
)
DER_SECOND = (
    -1.0 / 560,
    8.0 / 315,
    -1.0 / 5,
    8.0 / 5,
    -205.0 / 72,
    8.0 / 5,
    -1.0 / 5,
    8.0 / 315,
    -1.0 / 560,
)
IDENTITY = (0.0, 0.0, 0.0, 0.0, 1.0, 0.0, 0.0, 0.0, 0.0)
STENCILS = (IDENTITY, DER_FIRST, DER_SECOND)
DERICHE_POLES = ((1.68, 3.735, 1.783, 0.6318), (-0.6803, -0.2598, 1.723, 1.997))
FEATURES = ((0, 0), (0, 1), (1, 0), (0, 2), (1, 1), (2, 0))

HALO = 4
CAUSAL, FIRST, LAST, ANTICAUSAL = 0, 8, 12, 16
BASIS = 24
SENT = 16
LANES = 128
OWN_ROWS, OTHER_ROWS, COL_ROWS = slice(0, 48), slice(48, 96), slice(96, 128)
TILED_ROWS = [slice(128, 144)] * (LANES // SENT) + [slice(144, 160)] * (LANES // SENT)
PIECE = SENT // 2 + 1


def pole_values(deviation):
    normal_sum = 0.0
    for cos_weight, sin_weight, decay, freq in DERICHE_POLES:
        z = np.exp(complex(-decay, freq) / deviation)
        q = z / (1.0 - z)
        normal_sum += cos_weight + 2.0 * (cos_weight * q.real + sin_weight * q.imag)
    weights = [complex(cw, -sw) / normal_sum for cw, sw, _, _ in DERICHE_POLES]
    exponents = [complex(decay, -freq) / deviation for _, _, decay, freq in DERICHE_POLES]
    return np.array(weights), np.array(exponents)


def all_poles():
    return [pole_values(deviation) for deviation in DEVIATIONS]


def smooth_kernel(poles, distance):
    weights, exponents = poles
    return sum(
        (w * np.exp(-e * np.abs(distance))).real for w, e in zip(weights, exponents)
    )


def summary_table(length):
    cells = np.arange(length)
    table = np.zeros((BASIS, length))
    row = 0
    for _, exponents in all_poles():
        for e in exponents:
            causal = np.exp(-e * (length - 1 - cells))
            anticausal = np.exp(-e * cells)
            table[CAUSAL + row], table[CAUSAL + row + 1] = causal.real, causal.imag
            table[ANTICAUSAL + row], table[ANTICAUSAL + row + 1] = (
                anticausal.real,
                anticausal.imag,
            )
            row += 2
    for i in range(HALO):
        table[FIRST + i, i] = 1.0
        table[LAST + i, length - HALO + i] = 1.0
    return table


def cell_weight(poles, stencil, out_cells, in_cells, total):
    result = np.zeros((len(out_cells), len(in_cells)))
    for t in range(-HALO, HALO + 1):
        field_cells = in_cells - t
        inside = (field_cells >= 0) & (field_cells < total)
        distance = out_cells[:, None] - field_cells[None, :]
        result += stencil[t + HALO] * smooth_kernel(poles, distance) * inside[None, :]
    return result


def summary_weight(level, stencil, out_start, length, start, extent, total):
    poles = all_poles()[level]
    weights, exponents = poles
    out_cells = out_start + np.arange(length)
    after = out_start > start
    base = CAUSAL if after else FIRST
    offset = (CAUSAL if after else ANTICAUSAL) + 4 * level
    sign = 1.0 if after else -1.0
    anchor = start + (extent - 1 if after else 0)
    table = np.zeros((length, BASIS))
    for p, (w, e) in enumerate(zip(weights, exponents)):
        eigen = sum(stencil[t + HALO] * np.exp(-sign * e * t) for t in range(-HALO, HALO + 1))
        gain = w * eigen * np.exp(-e * np.abs(out_cells - anchor))
        table[:, offset + 2 * p] = gain.real
        table[:, offset + 2 * p + 1] = -gain.imag

    def far_form(cells):
        result = np.zeros((length, len(cells)))
        for t in range(-HALO, HALO + 1):
            distance = sign * (out_cells[:, None] - (cells - t)[None, :])
            result += stencil[t + HALO] * sum(
                (w * np.exp(-e * distance)).real for w, e in zip(weights, exponents)
            )
        return result

    for position, first in ((FIRST, start), (LAST, start + extent - HALO)):
        cells = first + np.arange(HALO)
        at_end = (cells[0] == 0) or (cells[-1] == total - 1)
        adjacent = (cells[-1] + 1 == out_cells[0]) or (out_cells[-1] + 1 == cells[0])
        if at_end or adjacent:
            table[:, position : position + HALO] = cell_weight(
                poles, stencil, out_cells, cells, total
            ) - far_form(cells)
    return table[:, base : base + SENT]


def operator_tables(length, blocks, sources, gains):
    tables = np.zeros((blocks, 2, 3, length, length + SENT * len(sources(0))))
    total = length * blocks
    for block in range(blocks):
        cells = block * length + np.arange(length)
        for level, poles in enumerate(all_poles()):
            for k, stencil in enumerate(STENCILS):
                view = tables[block, level, k]
                view[:, :length] = cell_weight(poles, stencil, cells, cells, total)
                for place, source in enumerate(sources(block)):
                    if source is not None:
                        at = length + SENT * place
                        view[:, at : at + SENT] = summary_weight(
                            level, stencil, cells[0], length, *source, total
                        )
                view *= gains[level][k]
    return tables


def split_table(values):
    high = values.astype(ml_dtypes.bfloat16)
    low = (values - high.astype(np.float64)).astype(ml_dtypes.bfloat16)
    return np.stack([high, low])


def split(values):
    high = values.astype(jnp.bfloat16)
    low = (values - high.astype(jnp.float32)).astype(jnp.bfloat16)
    return high, low


def dot3(left, right, dims=((1,), (0,))):
    left = jnp.concatenate([left[0], left[0], left[1]], axis=dims[0][0])
    right = jnp.concatenate([right[0], right[1], right[0]], axis=dims[1][0])
    return lax.dot_general(left, right, (dims, ((), ())), preferred_element_type=jnp.float32)


NT = ((1,), (1,))


def is_far(rows, cols):
    row, col = lax.axis_index("row"), lax.axis_index("col")
    chip = row // 2
    return col + chip // max(1, rows // 4) + lax.rem(chip, 2) >= 3


def table_copies(cols, row_op, col_op, col_rest, row_own, col_own, col_slots, sems):
    row, col = lax.axis_index("row"), lax.axis_index("col")
    variant = jnp.where(col == 0, 0, jnp.where(col == cols - 1, 2, 1))
    pairs = [
        (row_op.at[row], row_own),
        (col_op.at[variant], col_own),
        (col_rest.at[col], col_slots),
    ]
    return [pltpu.make_async_copy(*pair, sems.at[i]) for i, pair in enumerate(pairs)]


def prepare(
    rows,
    cols,
    image,
    sums,
    row_op,
    col_op,
    col_rest,
    block,
    table,
    row_own,
    col_own,
    col_slots,
    by_rows,
    by_cols,
    sems,
    table_sems,
):
    half = lax.rem(lax.axis_index("row"), 2)
    copies = [
        pltpu.make_async_copy(image, block, sems.at[0]),
        pltpu.make_async_copy(sums.at[half], table, sems.at[1]),
    ]
    tables = table_copies(cols, row_op, col_op, col_rest, row_own, col_own, col_slots, table_sems)
    far = is_far(rows, cols)
    for copy in copies:
        copy.start()

    @pl.when(jnp.logical_not(far))
    def _():
        for copy in tables:
            copy.start()

    for copy in copies:
        copy.wait()
    cells = split(block[...])
    by_rows[...] = dot3([table[i, OWN_ROWS] for i in range(2)], cells)
    by_cols[...] = dot3([table[i, COL_ROWS] for i in range(2)], cells, NT)

    @pl.when(jnp.logical_not(far))
    def _():
        for copy in tables:
            copy.wait()


def exchange_order(rows, cols):
    def place(device):
        row, col = divmod(device, cols)
        return col % 2, row % 2, col // 2, row // 2

    return sorted(range(rows * cols), key=place)


def after(values):
    return values[CAUSAL : CAUSAL + SENT]


def before(values):
    return values[FIRST : FIRST + SENT]


def lane_place(shape):
    return lax.broadcasted_iota(jnp.int32, shape, 1) // SENT


def pack(rows, cols, other, table, by_rows, by_cols, sent, near):
    row, col = lax.axis_index("row"), lax.axis_index("col")
    chip, half = row // 2, lax.rem(row, 2)
    cells = split(other[...])
    own_rows = by_rows[...]
    other_rows = dot3([table[i, OTHER_ROWS] for i in range(2)], cells)
    other_cols = dot3([table[i, COL_ROWS] for i in range(2)], cells, NT)
    near[...] = other_rows[BASIS : BASIS + SENT]
    over_rows = own_rows[:BASIS] + other_rows[:BASIS]
    own_near, other_near = own_rows[BASIS : BASIS + SENT], near[...]
    own_cols = by_cols[...]
    is_first = half == 0
    nears = [
        jnp.where(is_first, own_near, other_near),
        jnp.where(is_first, other_near, own_near),
    ]
    over_cols = [
        jnp.where(is_first, own_cols, other_cols),
        jnp.where(is_first, other_cols, own_cols),
    ]
    corners = dot3(
        split(jnp.concatenate([over_rows] + nears)),
        [jnp.concatenate([table[i, rows] for rows in TILED_ROWS]) for i in range(2)],
        NT,
    )

    def share(values):
        return jnp.where(is_first, values[: SENT // 2], values[SENT // 2 :])

    straight = [share(after(over_rows)), share(before(over_rows))]
    across, flat, placed = [], [], []
    for to_half in range(2):
        across.append([share(after(over_cols[to_half])), share(before(over_cols[to_half]))])
    for side in range(2):
        tiled = corners[:, LANES * side : LANES * (side + 1)]
        places = min(cols, LANES // SENT)
        mine = lax.rem(lane_place(tiled.shape), places) == lax.rem(col, places)
        masked = jnp.where(mine, tiled, 0.0)
        placed.append([share(after(masked)), share(before(masked))])
        lines = []
        for to_half in range(2):
            start = BASIS + SENT * (1 - to_half)
            part = share(tiled[start : start + SENT])
            line = lax.broadcasted_iota(jnp.int32, part.shape, 0)
            diagonal = lax.rem(lane_place(part.shape) + line, LANES // SENT) == lax.rem(
                col, LANES // SENT
            )
            lines.append(jnp.sum(jnp.where(diagonal, part, 0.0), axis=0, keepdims=True))
        flat.append(lines)
    none = jnp.zeros((1, LANES), jnp.float32)
    order = exchange_order(rows, cols)
    for to_chip in range(rows // 2):
        is_after = to_chip > chip
        is_here = to_chip == chip
        line = jnp.where(is_after, straight[0], straight[1])
        sides = [jnp.where(is_after, *placed[side]) for side in range(2)]
        for to_half in range(2):
            for to_col in range(cols):
                is_right = to_col > col
                body = jnp.where(to_col == col, line, jnp.where(is_right, *sides))
                body = jnp.where(is_here, jnp.where(is_right, *across[to_half]), body)
                tail = jnp.where(is_right, flat[0][to_half], flat[1][to_half])
                at = PIECE * order.index((2 * to_chip + to_half) * cols + to_col)
                sent[at : at + PIECE - 1] = body
                sent[at + PIECE - 1 : at + PIECE] = jnp.where(is_here, tail, none)


def side_by_side(values, used):
    high, low = split(values)
    if used % LANES == 0:
        return jnp.concatenate([high, low], axis=1)
    lane = lax.broadcasted_iota(jnp.int32, values.shape, 1)
    return jnp.where(lane < used, high, low)


def long_product(own, beside, tall, rest):
    left = jnp.concatenate([own[0], own[0], own[1], beside, beside], axis=1)
    none = jnp.zeros(rest[1].shape, jnp.bfloat16)
    right = jnp.concatenate([tall[0], tall[1], tall[0], rest[0], rest[0], rest[1], none])
    return jnp.dot(left, right, preferred_element_type=jnp.float32)


def combine(
    rows,
    cols,
    block,
    got,
    near,
    row_op,
    col_op,
    col_rest,
    row_loaded,
    col_loaded,
    slots_loaded,
    out,
    row_own,
    col_own,
    col_slots,
    staged,
    sems,
    table_sems,
):
    row, col = lax.axis_index("row"), lax.axis_index("col")

    @pl.when(is_far(rows, cols))
    def _():
        tables = table_copies(
            cols, row_op, col_op, col_rest, row_own, col_own, col_slots, table_sems
        )
        for copy in tables:
            copy.start()
        for copy in tables:
            copy.wait()

    chip = row // 2
    length, width = block.shape
    groups = -(-SENT * cols // LANES)
    per_group = LANES // SENT
    order = exchange_order(rows, cols)
    nothing = jnp.zeros((SENT, LANES), jnp.float32)
    half_shape = (SENT // 2, LANES)

    def places(from_chip, from_col):
        devices = [(2 * from_chip + half) * cols + from_col for half in range(2)]
        return [PIECE * order.index(device) for device in devices]

    def piece(from_chip, from_col):
        ats = places(from_chip, from_col)
        return jnp.concatenate([got[at : at + PIECE - 1] for at in ats])

    def corner(from_chip, from_col):
        tails = [got[at + PIECE - 1 : at + PIECE] for at in places(from_chip, from_col)]
        return jnp.concatenate([jnp.broadcast_to(tail, half_shape) for tail in tails])

    across = []
    corners = [nothing] * groups
    pieces = [[piece(i, j) for j in range(cols)] for i in range(rows // 2)]
    for from_col in range(cols):
        here = nothing
        tail = nothing
        for from_chip in range(rows // 2):
            here = jnp.where(from_chip == chip, pieces[from_chip][from_col], here)
            tail = jnp.where(from_chip == chip, corner(from_chip, from_col), tail)
        across.append(here)
        tail = [
            pltpu.roll(half, 0, 1, stride=SENT, stride_axis=0)
            for half in (tail[: SENT // 2], tail[SENT // 2 :])
        ]
        tail = jnp.concatenate(tail)
        wanted = (lane_place(tail.shape) == from_col % per_group) & (from_col != col)
        corners[from_col // per_group] += jnp.where(wanted, tail, 0.0)
    if cols < per_group:
        across = across * (per_group // cols)
        corners = [part + pltpu.roll(part, SENT * cols, 1) for part in corners]
    lines = [block[...]]
    slots = [jnp.concatenate(across).T]
    for from_chip in range(rows // 2):
        is_here = from_chip == chip
        line = near[...]
        parts = [jnp.where(is_here, corner_sum, 0.0) for corner_sum in corners]
        for from_col in range(cols):
            found = pieces[from_chip][from_col]
            is_col = from_col == col
            line = jnp.where(jnp.logical_not(is_here) & is_col, found, line)
            group = from_col // per_group
            parts[group] += jnp.where(is_here | is_col, 0.0, found)
        lines.append(line)
        slots.append(jnp.concatenate(parts, axis=1))
    along_cols = long_product(
        split(jnp.concatenate(lines)),
        side_by_side(jnp.concatenate(slots), SENT * cols),
        [col_own[i] for i in range(2)],
        [col_slots[i] for i in range(2)],
    )
    copies = []
    for level in range(2):
        span = 3 * width
        smoothed = split(along_cols[:, span * level : span * (level + 1)])
        products = []
        for k in range(3):
            weights = row_own[level, k]
            met = [part[:, : (3 - k) * width] for part in smoothed]
            products.append(
                long_product(
                    [weights[:, :length], weights[:, length : 2 * length]],
                    weights[:, 2 * length :],
                    [part[:length] for part in met],
                    [part[length:] for part in met],
                )
            )
        for f, (row_stencil, col_stencil) in enumerate(FEATURES):
            feature = products[row_stencil][:, width * col_stencil : width * (col_stencil + 1)]
            channel = len(FEATURES) * level + f
            staged[channel] = feature.astype(jnp.bfloat16)
            copies.append(
                pltpu.make_async_copy(staged.at[channel], out.at[channel], sems.at[channel])
            )
            copies[-1].start()
    for copy in copies:
        copy.wait()


def row_tables(height, rows):
    def sources(block):
        chips = [(2 * height * chip, 2 * height) for chip in range(rows // 2)]
        chips[block // 2] = ((block ^ 1) * height, height)
        return chips

    base = [2.0 * math.sqrt(math.pi) * s for s in DEVIATIONS]
    gains = [[b * s**k for k in range(3)] for b, s in zip(base, DEVIATIONS)]
    whole, single = summary_table(2 * height), summary_table(height)
    sums = np.zeros((2, 48, height))
    for half, own in enumerate((after(single), before(single))):
        sums[half, :BASIS] = whole[:, half * height : (half + 1) * height]
        sums[half, BASIS : BASIS + SENT] = own
    return operator_tables(height, rows, sources, gains), sums


def col_tables(width, cols):
    def sources(block):
        return [None if b == block else (b * width, width) for b in range(cols)]

    gains = [[s**k for k in range(3)] for s in DEVIATIONS]
    single = summary_table(width)
    sums = np.zeros((32 + 2 * SENT, width))
    sums[:BASIS] = single
    sums[32:] = np.concatenate([after(single), before(single)])
    return operator_tables(width, cols, sources, gains), sums


def on_device(rows, cols, image):
    height, width = image.shape
    row_weights, row_sums = row_tables(height, rows)
    col_weights, col_sums = col_tables(width, cols)
    high, low = split_table(row_weights)
    row_op = np.concatenate(
        [part[..., cells] for cells in (slice(height), slice(height, None)) for part in (high, low)],
        axis=-1,
    )
    col_op = np.transpose(col_weights, (0, 4, 1, 2, 3))
    col_op = np.moveaxis(split_table(col_op.reshape(*col_op.shape[:2], -1)), 0, 1)
    col_rest = col_op[:, :, width:]
    col_op = col_op[[0, cols // 2, cols - 1], :, :width]
    sums = np.stack(
        [np.concatenate([row_sums[h], row_sums[1 - h], col_sums]) for h in range(2)]
    )
    sums = np.moveaxis(split_table(sums), 0, 1)

    def in_vmem(count):
        return [pl.BlockSpec(memory_space=pltpu.VMEM)] * count

    params = pltpu.CompilerParams(vmem_limit_bytes=16 * 1024 * 1024)
    operands = [jnp.asarray(x) for x in (sums, row_op, col_op, col_rest)]
    operands = [pltpu.with_memory_space_constraint(x, pltpu.HBM) for x in [image] + operands]
    other = lax.ppermute(image, "row", [(i, i ^ 1) for i in range(rows)])
    block, table, row_own, col_own, col_slots, by_rows, by_cols = pl.pallas_call(
        lambda *refs: prepare(rows, cols, *refs),
        out_shape=[
            pltpu.VMEM((height, width), jnp.float32),
            *[pltpu.VMEM(x.shape[1:], jnp.bfloat16) for x in (sums, row_op, col_op, col_rest)],
            pltpu.VMEM((48, width), jnp.float32),
            pltpu.VMEM((32, height), jnp.float32),
        ],
        in_specs=[pl.BlockSpec(memory_space=pltpu.HBM)] * len(operands),
        out_specs=in_vmem(7),
        scratch_shapes=[pltpu.SemaphoreType.DMA((2,)), pltpu.SemaphoreType.DMA((3,))],
        compiler_params=params,
        cost_estimate=pl.CostEstimate(
            flops=6 * 80 * height * width, bytes_accessed=4 * 1024 * 1024, transcendentals=0
        ),
        name="prepare",
    )(*operands)
    sent, near = pl.pallas_call(
        lambda *refs: pack(rows, cols, *refs),
        out_shape=[
            pltpu.VMEM((PIECE * rows * cols, LANES), jnp.float32),
            pltpu.VMEM((SENT, width), jnp.float32),
        ],
        in_specs=in_vmem(4),
        out_specs=in_vmem(2),
        compiler_params=params,
        name="pack",
    )(other, table, by_rows, by_cols)
    got = lax.all_to_all(
        sent.reshape(rows * cols, PIECE, 1, LANES),
        ("row", "col"),
        0,
        0,
        axis_index_groups=[exchange_order(rows, cols)],
    )
    features = 2 * len(FEATURES)
    weights = [row_own, col_own, col_slots]
    result = pl.pallas_call(
        lambda *refs: combine(rows, cols, *refs),
        out_shape=[
            jax.ShapeDtypeStruct((features, height, width), jnp.bfloat16),
            *[pltpu.VMEM(x.shape, x.dtype) for x in weights],
        ],
        in_specs=in_vmem(3) + [pl.BlockSpec(memory_space=pltpu.HBM)] * 3 + in_vmem(3),
        out_specs=[pl.BlockSpec(memory_space=pl.ANY)] + in_vmem(3),
        input_output_aliases={6: 1, 7: 2, 8: 3},
        scratch_shapes=[
            pltpu.VMEM((features, height, width), jnp.bfloat16),
            pltpu.SemaphoreType.DMA((features,)),
            pltpu.SemaphoreType.DMA((3,)),
        ],
        compiler_params=params,
        name="combine",
    )(block, got.reshape(sent.shape), near, *operands[2:], *weights)
    return result[0]


def solution(mesh):
    rows, cols = mesh.shape["row"], mesh.shape["col"]
    return jax.shard_map(
        lambda image: on_device(rows, cols, image),
        mesh=mesh,
        in_specs=(P("row", "col"),),
        out_specs=P(None, "row", "col"),
        check_vma=False,
    )
```

```python
import math

import jax
import jax.numpy as jnp
import ml_dtypes
import numpy as np
from jax import lax
from jax.experimental import pallas as pl
from jax.experimental.pallas import tpu as pltpu
from jax.sharding import PartitionSpec as P

SIG_A = 128
SIG_B = 256
DEVIATIONS = (SIG_A, SIG_B)

DER_FIRST = (
    1.0 / 280,
    -4.0 / 105,
    1.0 / 5,
    -4.0 / 5,
    0.0,
    4.0 / 5,
    -1.0 / 5,
    4.0 / 105,
    -1.0 / 280,
)
DER_SECOND = (
    -1.0 / 560,
    8.0 / 315,
    -1.0 / 5,
    8.0 / 5,
    -205.0 / 72,
    8.0 / 5,
    -1.0 / 5,
    8.0 / 315,
    -1.0 / 560,
)
IDENTITY = (0.0, 0.0, 0.0, 0.0, 1.0, 0.0, 0.0, 0.0, 0.0)
STENCILS = (IDENTITY, DER_FIRST, DER_SECOND)
DERICHE_POLES = ((1.68, 3.735, 1.783, 0.6318), (-0.6803, -0.2598, 1.723, 1.997))
FEATURES = ((0, 0), (0, 1), (1, 0), (0, 2), (1, 1), (2, 0))

HALO = 4
CAUSAL, FIRST, LAST, ANTICAUSAL = 0, 8, 12, 16
BASIS = 24
SENT = 16
LANES = 128
OWN_ROWS, OTHER_ROWS, COL_ROWS = slice(0, 48), slice(48, 96), slice(96, 128)
TILED_ROWS = [slice(128, 144)] * (LANES // SENT) + [slice(144, 160)] * (LANES // SENT)
PIECE = SENT // 2 + 1


def pole_values(deviation):
    normal_sum = 0.0
    for cos_weight, sin_weight, decay, freq in DERICHE_POLES:
        z = np.exp(complex(-decay, freq) / deviation)
        q = z / (1.0 - z)
        normal_sum += cos_weight + 2.0 * (cos_weight * q.real + sin_weight * q.imag)
    weights = [complex(cw, -sw) / normal_sum for cw, sw, _, _ in DERICHE_POLES]
    exponents = [complex(decay, -freq) / deviation for _, _, decay, freq in DERICHE_POLES]
    return np.array(weights), np.array(exponents)


def all_poles():
    return [pole_values(deviation) for deviation in DEVIATIONS]


def smooth_kernel(poles, distance):
    weights, exponents = poles
    return sum(
        (w * np.exp(-e * np.abs(distance))).real for w, e in zip(weights, exponents)
    )


def summary_table(length):
    cells = np.arange(length)
    table = np.zeros((BASIS, length))
    row = 0
    for _, exponents in all_poles():
        for e in exponents:
            causal = np.exp(-e * (length - 1 - cells))
            anticausal = np.exp(-e * cells)
            table[CAUSAL + row], table[CAUSAL + row + 1] = causal.real, causal.imag
            table[ANTICAUSAL + row], table[ANTICAUSAL + row + 1] = (
                anticausal.real,
                anticausal.imag,
            )
            row += 2
    for i in range(HALO):
        table[FIRST + i, i] = 1.0
        table[LAST + i, length - HALO + i] = 1.0
    return table


def cell_weight(poles, stencil, out_cells, in_cells, total):
    result = np.zeros((len(out_cells), len(in_cells)))
    for t in range(-HALO, HALO + 1):
        field_cells = in_cells - t
        inside = (field_cells >= 0) & (field_cells < total)
        distance = out_cells[:, None] - field_cells[None, :]
        result += stencil[t + HALO] * smooth_kernel(poles, distance) * inside[None, :]
    return result


def summary_weight(level, stencil, out_start, length, start, extent, total):
    poles = all_poles()[level]
    weights, exponents = poles
    out_cells = out_start + np.arange(length)
    after = out_start > start
    base = CAUSAL if after else FIRST
    offset = (CAUSAL if after else ANTICAUSAL) + 4 * level
    sign = 1.0 if after else -1.0
    anchor = start + (extent - 1 if after else 0)
    table = np.zeros((length, BASIS))
    for p, (w, e) in enumerate(zip(weights, exponents)):
        eigen = sum(stencil[t + HALO] * np.exp(-sign * e * t) for t in range(-HALO, HALO + 1))
        gain = w * eigen * np.exp(-e * np.abs(out_cells - anchor))
        table[:, offset + 2 * p] = gain.real
        table[:, offset + 2 * p + 1] = -gain.imag

    def far_form(cells):
        result = np.zeros((length, len(cells)))
        for t in range(-HALO, HALO + 1):
            distance = sign * (out_cells[:, None] - (cells - t)[None, :])
            result += stencil[t + HALO] * sum(
                (w * np.exp(-e * distance)).real for w, e in zip(weights, exponents)
            )
        return result

    for position, first in ((FIRST, start), (LAST, start + extent - HALO)):
        cells = first + np.arange(HALO)
        at_end = (cells[0] == 0) or (cells[-1] == total - 1)
        adjacent = (cells[-1] + 1 == out_cells[0]) or (out_cells[-1] + 1 == cells[0])
        if at_end or adjacent:
            table[:, position : position + HALO] = cell_weight(
                poles, stencil, out_cells, cells, total
            ) - far_form(cells)
    return table[:, base : base + SENT]


def operator_tables(length, blocks, sources, gains):
    tables = np.zeros((blocks, 2, 3, length, length + SENT * len(sources(0))))
    total = length * blocks
    for block in range(blocks):
        cells = block * length + np.arange(length)
        for level, poles in enumerate(all_poles()):
            for k, stencil in enumerate(STENCILS):
                view = tables[block, level, k]
                view[:, :length] = cell_weight(poles, stencil, cells, cells, total)
                for place, source in enumerate(sources(block)):
                    if source is not None:
                        at = length + SENT * place
                        view[:, at : at + SENT] = summary_weight(
                            level, stencil, cells[0], length, *source, total
                        )
                view *= gains[level][k]
    return tables


def split_table(values):
    high = values.astype(ml_dtypes.bfloat16)
    low = (values - high.astype(np.float64)).astype(ml_dtypes.bfloat16)
    return np.stack([high, low])


def split(values):
    high = values.astype(jnp.bfloat16)
    low = (values - high.astype(jnp.float32)).astype(jnp.bfloat16)
    return high, low


def dot3(left, right, dims=((1,), (0,))):
    left = jnp.concatenate([left[0], left[0], left[1]], axis=dims[0][0])
    right = jnp.concatenate([right[0], right[1], right[0]], axis=dims[1][0])
    return lax.dot_general(left, right, (dims, ((), ())), preferred_element_type=jnp.float32)


NT = ((1,), (1,))


def is_far(rows, cols):
    row, col = lax.axis_index("row"), lax.axis_index("col")
    chip = row // 2
    return col + chip // max(1, rows // 4) + lax.rem(chip, 2) >= 3


def table_copies(cols, row_op, col_op, col_rest, row_own, col_own, col_slots, sems):
    row, col = lax.axis_index("row"), lax.axis_index("col")
    variant = jnp.where(col == 0, 0, jnp.where(col == cols - 1, 2, 1))
    pairs = [
        (row_op.at[row], row_own),
        (col_op.at[variant], col_own),
        (col_rest.at[col], col_slots),
    ]
    return [pltpu.make_async_copy(*pair, sems.at[i]) for i, pair in enumerate(pairs)]


def prepare(
    rows,
    cols,
    image,
    sums,
    row_op,
    col_op,
    col_rest,
    block,
    table,
    row_own,
    col_own,
    col_slots,
    by_rows,
    by_cols,
    sems,
    table_sems,
):
    half = lax.rem(lax.axis_index("row"), 2)
    copies = [
        pltpu.make_async_copy(image, block, sems.at[0]),
        pltpu.make_async_copy(sums.at[half], table, sems.at[1]),
    ]
    tables = table_copies(cols, row_op, col_op, col_rest, row_own, col_own, col_slots, table_sems)
    far = is_far(rows, cols)
    for copy in copies:
        copy.start()

    @pl.when(jnp.logical_not(far))
    def _():
        for copy in tables:
            copy.start()

    for copy in copies:
        copy.wait()
    cells = split(block[...])
    by_rows[...] = dot3([table[i, OWN_ROWS] for i in range(2)], cells)
    by_cols[...] = dot3([table[i, COL_ROWS] for i in range(2)], cells, NT)

    @pl.when(jnp.logical_not(far))
    def _():
        for copy in tables:
            copy.wait()


def exchange_order(rows, cols):
    def place(device):
        row, col = divmod(device, cols)
        chip, half = divmod(row, 2)
        return (col ^ half) % 2, (col ^ chip ^ chip // 2) % 2, col // 2, chip

    return sorted(range(rows * cols), key=place)


def after(values):
    return values[CAUSAL : CAUSAL + SENT]


def before(values):
    return values[FIRST : FIRST + SENT]


def lane_place(shape):
    return lax.broadcasted_iota(jnp.int32, shape, 1) // SENT


def pack(rows, cols, other, table, by_rows, by_cols, sent, near):
    row, col = lax.axis_index("row"), lax.axis_index("col")
    chip, half = row // 2, lax.rem(row, 2)
    cells = split(other[...])
    own_rows = by_rows[...]
    other_rows = dot3([table[i, OTHER_ROWS] for i in range(2)], cells)
    other_cols = dot3([table[i, COL_ROWS] for i in range(2)], cells, NT)
    near[...] = other_rows[BASIS : BASIS + SENT]
    over_rows = own_rows[:BASIS] + other_rows[:BASIS]
    own_near, other_near = own_rows[BASIS : BASIS + SENT], near[...]
    own_cols = by_cols[...]
    is_first = half == 0
    nears = [
        jnp.where(is_first, own_near, other_near),
        jnp.where(is_first, other_near, own_near),
    ]
    over_cols = [
        jnp.where(is_first, own_cols, other_cols),
        jnp.where(is_first, other_cols, own_cols),
    ]
    corners = dot3(
        split(jnp.concatenate([over_rows] + nears)),
        [jnp.concatenate([table[i, rows] for rows in TILED_ROWS]) for i in range(2)],
        NT,
    )

    def share(values):
        return jnp.where(is_first, values[: SENT // 2], values[SENT // 2 :])

    straight = [share(after(over_rows)), share(before(over_rows))]
    across, flat, placed = [], [], []
    for to_half in range(2):
        across.append([share(after(over_cols[to_half])), share(before(over_cols[to_half]))])
    for side in range(2):
        tiled = corners[:, LANES * side : LANES * (side + 1)]
        places = min(cols, LANES // SENT)
        mine = lax.rem(lane_place(tiled.shape), places) == lax.rem(col, places)
        masked = jnp.where(mine, tiled, 0.0)
        placed.append([share(after(masked)), share(before(masked))])
        lines = []
        for to_half in range(2):
            start = BASIS + SENT * (1 - to_half)
            part = share(tiled[start : start + SENT])
            line = lax.broadcasted_iota(jnp.int32, part.shape, 0)
            diagonal = lax.rem(lane_place(part.shape) + line, LANES // SENT) == lax.rem(
                col, LANES // SENT
            )
            lines.append(jnp.sum(jnp.where(diagonal, part, 0.0), axis=0, keepdims=True))
        flat.append(lines)
    none = jnp.zeros((1, LANES), jnp.float32)
    order = exchange_order(rows, cols)
    for to_chip in range(rows // 2):
        is_after = to_chip > chip
        is_here = to_chip == chip
        line = jnp.where(is_after, straight[0], straight[1])
        sides = [jnp.where(is_after, *placed[side]) for side in range(2)]
        for to_half in range(2):
            for to_col in range(cols):
                is_right = to_col > col
                body = jnp.where(to_col == col, line, jnp.where(is_right, *sides))
                body = jnp.where(is_here, jnp.where(is_right, *across[to_half]), body)
                tail = jnp.where(is_right, flat[0][to_half], flat[1][to_half])
                at = PIECE * order.index((2 * to_chip + to_half) * cols + to_col)
                sent[at : at + PIECE - 1] = body
                sent[at + PIECE - 1 : at + PIECE] = jnp.where(is_here, tail, none)


def side_by_side(values, used):
    high, low = split(values)
    if used % LANES == 0:
        return jnp.concatenate([high, low], axis=1)
    lane = lax.broadcasted_iota(jnp.int32, values.shape, 1)
    return jnp.where(lane < used, high, low)


def long_product(own, beside, tall, rest):
    left = jnp.concatenate([own[0], own[0], own[1], beside, beside], axis=1)
    none = jnp.zeros(rest[1].shape, jnp.bfloat16)
    right = jnp.concatenate([tall[0], tall[1], tall[0], rest[0], rest[0], rest[1], none])
    return jnp.dot(left, right, preferred_element_type=jnp.float32)


def combine(
    rows,
    cols,
    block,
    got,
    near,
    row_op,
    col_op,
    col_rest,
    row_loaded,
    col_loaded,
    slots_loaded,
    out,
    row_own,
    col_own,
    col_slots,
    staged,
    sems,
    table_sems,
):
    row, col = lax.axis_index("row"), lax.axis_index("col")

    @pl.when(is_far(rows, cols))
    def _():
        tables = table_copies(
            cols, row_op, col_op, col_rest, row_own, col_own, col_slots, table_sems
        )
        for copy in tables:
            copy.start()
        for copy in tables:
            copy.wait()

    chip = row // 2
    length, width = block.shape
    groups = -(-SENT * cols // LANES)
    per_group = LANES // SENT
    order = exchange_order(rows, cols)
    nothing = jnp.zeros((SENT, LANES), jnp.float32)
    half_shape = (SENT // 2, LANES)

    def places(from_chip, from_col):
        devices = [(2 * from_chip + half) * cols + from_col for half in range(2)]
        return [PIECE * order.index(device) for device in devices]

    def piece(from_chip, from_col):
        ats = places(from_chip, from_col)
        return jnp.concatenate([got[at : at + PIECE - 1] for at in ats])

    def corner(from_chip, from_col):
        tails = [got[at + PIECE - 1 : at + PIECE] for at in places(from_chip, from_col)]
        return jnp.concatenate([jnp.broadcast_to(tail, half_shape) for tail in tails])

    across = []
    corners = [nothing] * groups
    pieces = [[piece(i, j) for j in range(cols)] for i in range(rows // 2)]
    for from_col in range(cols):
        here = nothing
        tail = nothing
        for from_chip in range(rows // 2):
            here = jnp.where(from_chip == chip, pieces[from_chip][from_col], here)
            tail = jnp.where(from_chip == chip, corner(from_chip, from_col), tail)
        across.append(here)
        tail = [
            pltpu.roll(half, 0, 1, stride=SENT, stride_axis=0)
            for half in (tail[: SENT // 2], tail[SENT // 2 :])
        ]
        tail = jnp.concatenate(tail)
        wanted = (lane_place(tail.shape) == from_col % per_group) & (from_col != col)
        corners[from_col // per_group] += jnp.where(wanted, tail, 0.0)
    if cols < per_group:
        across = across * (per_group // cols)
        corners = [part + pltpu.roll(part, SENT * cols, 1) for part in corners]
    lines = [block[...]]
    slots = [jnp.concatenate(across).T]
    for from_chip in range(rows // 2):
        is_here = from_chip == chip
        line = near[...]
        parts = [jnp.where(is_here, corner_sum, 0.0) for corner_sum in corners]
        for from_col in range(cols):
            found = pieces[from_chip][from_col]
            is_col = from_col == col
            line = jnp.where(jnp.logical_not(is_here) & is_col, found, line)
            group = from_col // per_group
            parts[group] += jnp.where(is_here | is_col, 0.0, found)
        lines.append(line)
        slots.append(jnp.concatenate(parts, axis=1))
    along_cols = long_product(
        split(jnp.concatenate(lines)),
        side_by_side(jnp.concatenate(slots), SENT * cols),
        [col_own[i] for i in range(2)],
        [col_slots[i] for i in range(2)],
    )
    copies = []
    for level in range(2):
        span = 3 * width
        smoothed = split(along_cols[:, span * level : span * (level + 1)])
        products = []
        for k in range(3):
            weights = row_own[level, k]
            met = [part[:, : (3 - k) * width] for part in smoothed]
            products.append(
                long_product(
                    [weights[:, :length], weights[:, length : 2 * length]],
                    weights[:, 2 * length :],
                    [part[:length] for part in met],
                    [part[length:] for part in met],
                )
            )
        for f, (row_stencil, col_stencil) in enumerate(FEATURES):
            feature = products[row_stencil][:, width * col_stencil : width * (col_stencil + 1)]
            channel = len(FEATURES) * level + f
            staged[channel] = feature.astype(jnp.bfloat16)
            copies.append(
                pltpu.make_async_copy(staged.at[channel], out.at[channel], sems.at[channel])
            )
            copies[-1].start()
    for copy in copies:
        copy.wait()


def row_tables(height, rows):
    def sources(block):
        chips = [(2 * height * chip, 2 * height) for chip in range(rows // 2)]
        chips[block // 2] = ((block ^ 1) * height, height)
        return chips

    base = [2.0 * math.sqrt(math.pi) * s for s in DEVIATIONS]
    gains = [[b * s**k for k in range(3)] for b, s in zip(base, DEVIATIONS)]
    whole, single = summary_table(2 * height), summary_table(height)
    sums = np.zeros((2, 48, height))
    for half, own in enumerate((after(single), before(single))):
        sums[half, :BASIS] = whole[:, half * height : (half + 1) * height]
        sums[half, BASIS : BASIS + SENT] = own
    return operator_tables(height, rows, sources, gains), sums


def col_tables(width, cols):
    def sources(block):
        return [None if b == block else (b * width, width) for b in range(cols)]

    gains = [[s**k for k in range(3)] for s in DEVIATIONS]
    single = summary_table(width)
    sums = np.zeros((32 + 2 * SENT, width))
    sums[:BASIS] = single
    sums[32:] = np.concatenate([after(single), before(single)])
    return operator_tables(width, cols, sources, gains), sums


def on_device(rows, cols, image):
    height, width = image.shape
    row_weights, row_sums = row_tables(height, rows)
    col_weights, col_sums = col_tables(width, cols)
    high, low = split_table(row_weights)
    row_op = np.concatenate(
        [part[..., cells] for cells in (slice(height), slice(height, None)) for part in (high, low)],
        axis=-1,
    )
    col_op = np.transpose(col_weights, (0, 4, 1, 2, 3))
    col_op = np.moveaxis(split_table(col_op.reshape(*col_op.shape[:2], -1)), 0, 1)
    col_rest = col_op[:, :, width:]
    col_op = col_op[[0, cols // 2, cols - 1], :, :width]
    sums = np.stack(
        [np.concatenate([row_sums[h], row_sums[1 - h], col_sums]) for h in range(2)]
    )
    sums = np.moveaxis(split_table(sums), 0, 1)

    def in_vmem(count):
        return [pl.BlockSpec(memory_space=pltpu.VMEM)] * count

    params = pltpu.CompilerParams(vmem_limit_bytes=16 * 1024 * 1024)
    operands = [jnp.asarray(x) for x in (sums, row_op, col_op, col_rest)]
    operands = [pltpu.with_memory_space_constraint(x, pltpu.HBM) for x in [image] + operands]
    other = lax.ppermute(image, "row", [(i, i ^ 1) for i in range(rows)])
    block, table, row_own, col_own, col_slots, by_rows, by_cols = pl.pallas_call(
        lambda *refs: prepare(rows, cols, *refs),
        out_shape=[
            pltpu.VMEM((height, width), jnp.float32),
            *[pltpu.VMEM(x.shape[1:], jnp.bfloat16) for x in (sums, row_op, col_op, col_rest)],
            pltpu.VMEM((48, width), jnp.float32),
            pltpu.VMEM((32, height), jnp.float32),
        ],
        in_specs=[pl.BlockSpec(memory_space=pltpu.HBM)] * len(operands),
        out_specs=in_vmem(7),
        scratch_shapes=[pltpu.SemaphoreType.DMA((2,)), pltpu.SemaphoreType.DMA((3,))],
        compiler_params=params,
        cost_estimate=pl.CostEstimate(
            flops=6 * 80 * height * width, bytes_accessed=4 * 1024 * 1024, transcendentals=0
        ),
        name="prepare",
    )(*operands)
    sent, near = pl.pallas_call(
        lambda *refs: pack(rows, cols, *refs),
        out_shape=[
            pltpu.VMEM((PIECE * rows * cols, LANES), jnp.float32),
            pltpu.VMEM((SENT, width), jnp.float32),
        ],
        in_specs=in_vmem(4),
        out_specs=in_vmem(2),
        compiler_params=params,
        name="pack",
    )(other, table, by_rows, by_cols)
    got = lax.all_to_all(
        sent.reshape(rows * cols, PIECE, 1, LANES),
        ("row", "col"),
        0,
        0,
        axis_index_groups=[exchange_order(rows, cols)],
    )
    features = 2 * len(FEATURES)
    weights = [row_own, col_own, col_slots]
    result = pl.pallas_call(
        lambda *refs: combine(rows, cols, *refs),
        out_shape=[
            jax.ShapeDtypeStruct((features, height, width), jnp.bfloat16),
            *[pltpu.VMEM(x.shape, x.dtype) for x in weights],
        ],
        in_specs=in_vmem(3) + [pl.BlockSpec(memory_space=pltpu.HBM)] * 3 + in_vmem(3),
        out_specs=[pl.BlockSpec(memory_space=pl.ANY)] + in_vmem(3),
        input_output_aliases={6: 1, 7: 2, 8: 3},
        scratch_shapes=[
            pltpu.VMEM((features, height, width), jnp.bfloat16),
            pltpu.SemaphoreType.DMA((features,)),
            pltpu.SemaphoreType.DMA((3,)),
        ],
        compiler_params=params,
        name="combine",
    )(block, got.reshape(sent.shape), near, *operands[2:], *weights)
    return result[0]


def solution(mesh):
    rows, cols = mesh.shape["row"], mesh.shape["col"]
    return jax.shard_map(
        lambda image: on_device(rows, cols, image),
        mesh=mesh,
        in_specs=(P("row", "col"),),
        out_specs=P(None, "row", "col"),
        check_vma=False,
    )
```

```python
import math

import jax
import jax.numpy as jnp
import ml_dtypes
import numpy as np
from jax import lax
from jax.experimental import pallas as pl
from jax.experimental.pallas import tpu as pltpu
from jax.sharding import PartitionSpec as P

SIG_A = 128
SIG_B = 256
DEVIATIONS = (SIG_A, SIG_B)

DER_FIRST = (
    1.0 / 280,
    -4.0 / 105,
    1.0 / 5,
    -4.0 / 5,
    0.0,
    4.0 / 5,
    -1.0 / 5,
    4.0 / 105,
    -1.0 / 280,
)
DER_SECOND = (
    -1.0 / 560,
    8.0 / 315,
    -1.0 / 5,
    8.0 / 5,
    -205.0 / 72,
    8.0 / 5,
    -1.0 / 5,
    8.0 / 315,
    -1.0 / 560,
)
IDENTITY = (0.0, 0.0, 0.0, 0.0, 1.0, 0.0, 0.0, 0.0, 0.0)
STENCILS = (IDENTITY, DER_FIRST, DER_SECOND)
DERICHE_POLES = ((1.68, 3.735, 1.783, 0.6318), (-0.6803, -0.2598, 1.723, 1.997))
FEATURES = ((0, 0), (0, 1), (1, 0), (0, 2), (1, 1), (2, 0))

HALO = 4
CAUSAL, FIRST, LAST, ANTICAUSAL = 0, 8, 12, 16
BASIS = 24
SENT = 16
LANES = 128
OWN_ROWS, OTHER_ROWS, COL_ROWS = slice(0, 48), slice(48, 96), slice(96, 128)
TILED_ROWS = [slice(128, 144)] * (LANES // SENT) + [slice(144, 160)] * (LANES // SENT)
PIECE = SENT // 2 + 1


def pole_values(deviation):
    normal_sum = 0.0
    for cos_weight, sin_weight, decay, freq in DERICHE_POLES:
        z = np.exp(complex(-decay, freq) / deviation)
        q = z / (1.0 - z)
        normal_sum += cos_weight + 2.0 * (cos_weight * q.real + sin_weight * q.imag)
    weights = [complex(cw, -sw) / normal_sum for cw, sw, _, _ in DERICHE_POLES]
    exponents = [complex(decay, -freq) / deviation for _, _, decay, freq in DERICHE_POLES]
    return np.array(weights), np.array(exponents)


def all_poles():
    return [pole_values(deviation) for deviation in DEVIATIONS]


def smooth_kernel(poles, distance):
    weights, exponents = poles
    return sum(
        (w * np.exp(-e * np.abs(distance))).real for w, e in zip(weights, exponents)
    )


def summary_table(length):
    cells = np.arange(length)
    table = np.zeros((BASIS, length))
    row = 0
    for _, exponents in all_poles():
        for e in exponents:
            causal = np.exp(-e * (length - 1 - cells))
            anticausal = np.exp(-e * cells)
            table[CAUSAL + row], table[CAUSAL + row + 1] = causal.real, causal.imag
            table[ANTICAUSAL + row], table[ANTICAUSAL + row + 1] = (
                anticausal.real,
                anticausal.imag,
            )
            row += 2
    for i in range(HALO):
        table[FIRST + i, i] = 1.0
        table[LAST + i, length - HALO + i] = 1.0
    return table


def cell_weight(poles, stencil, out_cells, in_cells, total):
    result = np.zeros((len(out_cells), len(in_cells)))
    for t in range(-HALO, HALO + 1):
        field_cells = in_cells - t
        inside = (field_cells >= 0) & (field_cells < total)
        distance = out_cells[:, None] - field_cells[None, :]
        result += stencil[t + HALO] * smooth_kernel(poles, distance) * inside[None, :]
    return result


def summary_weight(level, stencil, out_start, length, start, extent, total):
    poles = all_poles()[level]
    weights, exponents = poles
    out_cells = out_start + np.arange(length)
    after = out_start > start
    base = CAUSAL if after else FIRST
    offset = (CAUSAL if after else ANTICAUSAL) + 4 * level
    sign = 1.0 if after else -1.0
    anchor = start + (extent - 1 if after else 0)
    table = np.zeros((length, BASIS))
    for p, (w, e) in enumerate(zip(weights, exponents)):
        eigen = sum(stencil[t + HALO] * np.exp(-sign * e * t) for t in range(-HALO, HALO + 1))
        gain = w * eigen * np.exp(-e * np.abs(out_cells - anchor))
        table[:, offset + 2 * p] = gain.real
        table[:, offset + 2 * p + 1] = -gain.imag

    def far_form(cells):
        result = np.zeros((length, len(cells)))
        for t in range(-HALO, HALO + 1):
            distance = sign * (out_cells[:, None] - (cells - t)[None, :])
            result += stencil[t + HALO] * sum(
                (w * np.exp(-e * distance)).real for w, e in zip(weights, exponents)
            )
        return result

    for position, first in ((FIRST, start), (LAST, start + extent - HALO)):
        cells = first + np.arange(HALO)
        at_end = (cells[0] == 0) or (cells[-1] == total - 1)
        adjacent = (cells[-1] + 1 == out_cells[0]) or (out_cells[-1] + 1 == cells[0])
        if at_end or adjacent:
            table[:, position : position + HALO] = cell_weight(
                poles, stencil, out_cells, cells, total
            ) - far_form(cells)
    return table[:, base : base + SENT]


def operator_tables(length, blocks, sources, gains):
    tables = np.zeros((blocks, 2, 3, length, length + SENT * len(sources(0))))
    total = length * blocks
    for block in range(blocks):
        cells = block * length + np.arange(length)
        for level, poles in enumerate(all_poles()):
            for k, stencil in enumerate(STENCILS):
                view = tables[block, level, k]
                view[:, :length] = cell_weight(poles, stencil, cells, cells, total)
                for place, source in enumerate(sources(block)):
                    if source is not None:
                        at = length + SENT * place
                        view[:, at : at + SENT] = summary_weight(
                            level, stencil, cells[0], length, *source, total
                        )
                view *= gains[level][k]
    return tables


def split_table(values):
    high = values.astype(ml_dtypes.bfloat16)
    low = (values - high.astype(np.float64)).astype(ml_dtypes.bfloat16)
    return np.stack([high, low])


def split(values):
    high = values.astype(jnp.bfloat16)
    low = (values - high.astype(jnp.float32)).astype(jnp.bfloat16)
    return high, low


def dot3(left, right, dims=((1,), (0,))):
    left = jnp.concatenate([left[0], left[0], left[1]], axis=dims[0][0])
    right = jnp.concatenate([right[0], right[1], right[0]], axis=dims[1][0])
    return lax.dot_general(left, right, (dims, ((), ())), preferred_element_type=jnp.float32)


NT = ((1,), (1,))


def is_far(rows, cols):
    row, col = lax.axis_index("row"), lax.axis_index("col")
    chip = row // 2
    return col + chip // max(1, rows // 4) + lax.rem(chip, 2) >= 3


def table_copies(cols, row_op, col_op, col_rest, row_own, col_own, col_slots, sems):
    row, col = lax.axis_index("row"), lax.axis_index("col")
    variant = jnp.where(col == 0, 0, jnp.where(col == cols - 1, 2, 1))
    pairs = [
        (row_op.at[row], row_own),
        (col_op.at[variant], col_own),
        (col_rest.at[col], col_slots),
    ]
    return [pltpu.make_async_copy(*pair, sems.at[i]) for i, pair in enumerate(pairs)]


def side_by_side(values, used):
    high, low = split(values)
    if used % LANES == 0:
        return jnp.concatenate([high, low], axis=1)
    lane = lax.broadcasted_iota(jnp.int32, values.shape, 1)
    return jnp.where(lane < used, high, low)


def long_product(own, beside, tall, rest):
    left = jnp.concatenate([own[0], own[0], own[1], beside, beside], axis=1)
    none = jnp.zeros(rest[1].shape, jnp.bfloat16)
    right = jnp.concatenate([tall[0], tall[1], tall[0], rest[0], rest[0], rest[1], none])
    return jnp.dot(left, right, preferred_element_type=jnp.float32)


def short_product(beside, rest):
    none = jnp.zeros(rest[1].shape, jnp.bfloat16)
    left = jnp.concatenate([beside, beside], axis=1)
    right = jnp.concatenate([rest[0], rest[0], rest[1], none])
    return jnp.dot(left, right, preferred_element_type=jnp.float32)


def prepare(
    rows,
    cols,
    image,
    sums,
    row_op,
    col_op,
    col_rest,
    block,
    table,
    row_own,
    col_own,
    col_slots,
    by_rows,
    by_cols,
    ahead,
    sems,
    table_sems,
):
    half = lax.rem(lax.axis_index("row"), 2)
    copies = [
        pltpu.make_async_copy(image, block, sems.at[0]),
        pltpu.make_async_copy(sums.at[half], table, sems.at[1]),
    ]
    tables = table_copies(cols, row_op, col_op, col_rest, row_own, col_own, col_slots, table_sems)
    far = is_far(rows, cols)
    for copy in copies:
        copy.start()

    @pl.when(jnp.logical_not(far))
    def _():
        for copy in tables:
            copy.start()

    for copy in copies:
        copy.wait()
    cells = split(block[...])
    by_rows[...] = dot3([table[i, OWN_ROWS] for i in range(2)], cells)
    by_cols[...] = dot3([table[i, COL_ROWS] for i in range(2)], cells, NT)

    @pl.when(jnp.logical_not(far))
    def _():
        for copy in tables:
            copy.wait()
        ahead[...] = dot3(split(block[...]), [col_own[i] for i in range(2)])


def exchange_order(rows, cols):
    def place(device):
        row, col = divmod(device, cols)
        chip, half = divmod(row, 2)
        return (col ^ half) % 2, (col ^ chip ^ chip // 2) % 2, col // 2, chip

    return sorted(range(rows * cols), key=place)


def after(values):
    return values[CAUSAL : CAUSAL + SENT]


def before(values):
    return values[FIRST : FIRST + SENT]


def lane_place(shape):
    return lax.broadcasted_iota(jnp.int32, shape, 1) // SENT


def pack(rows, cols, other, table, by_rows, by_cols, sent, near):
    row, col = lax.axis_index("row"), lax.axis_index("col")
    chip, half = row // 2, lax.rem(row, 2)
    cells = split(other[...])
    own_rows = by_rows[...]
    other_rows = dot3([table[i, OTHER_ROWS] for i in range(2)], cells)
    other_cols = dot3([table[i, COL_ROWS] for i in range(2)], cells, NT)
    near[...] = other_rows[BASIS : BASIS + SENT]
    over_rows = own_rows[:BASIS] + other_rows[:BASIS]
    own_near, other_near = own_rows[BASIS : BASIS + SENT], near[...]
    own_cols = by_cols[...]
    is_first = half == 0
    nears = [
        jnp.where(is_first, own_near, other_near),
        jnp.where(is_first, other_near, own_near),
    ]
    over_cols = [
        jnp.where(is_first, own_cols, other_cols),
        jnp.where(is_first, other_cols, own_cols),
    ]
    corners = dot3(
        split(jnp.concatenate([over_rows] + nears)),
        [jnp.concatenate([table[i, rows] for rows in TILED_ROWS]) for i in range(2)],
        NT,
    )

    def share(values):
        return jnp.where(is_first, values[: SENT // 2], values[SENT // 2 :])

    straight = [share(after(over_rows)), share(before(over_rows))]
    across, flat, placed = [], [], []
    for to_half in range(2):
        across.append([share(after(over_cols[to_half])), share(before(over_cols[to_half]))])
    for side in range(2):
        tiled = corners[:, LANES * side : LANES * (side + 1)]
        places = min(cols, LANES // SENT)
        mine = lax.rem(lane_place(tiled.shape), places) == lax.rem(col, places)
        masked = jnp.where(mine, tiled, 0.0)
        placed.append([share(after(masked)), share(before(masked))])
        lines = []
        for to_half in range(2):
            start = BASIS + SENT * (1 - to_half)
            part = share(tiled[start : start + SENT])
            line = lax.broadcasted_iota(jnp.int32, part.shape, 0)
            diagonal = lax.rem(lane_place(part.shape) + line, LANES // SENT) == lax.rem(
                col, LANES // SENT
            )
            lines.append(jnp.sum(jnp.where(diagonal, part, 0.0), axis=0, keepdims=True))
        flat.append(lines)
    none = jnp.zeros((1, LANES), jnp.float32)
    order = exchange_order(rows, cols)
    for to_chip in range(rows // 2):
        is_after = to_chip > chip
        is_here = to_chip == chip
        line = jnp.where(is_after, straight[0], straight[1])
        sides = [jnp.where(is_after, *placed[side]) for side in range(2)]
        for to_half in range(2):
            for to_col in range(cols):
                is_right = to_col > col
                body = jnp.where(to_col == col, line, jnp.where(is_right, *sides))
                body = jnp.where(is_here, jnp.where(is_right, *across[to_half]), body)
                tail = jnp.where(is_right, flat[0][to_half], flat[1][to_half])
                at = PIECE * order.index((2 * to_chip + to_half) * cols + to_col)
                sent[at : at + PIECE - 1] = body
                sent[at + PIECE - 1 : at + PIECE] = jnp.where(is_here, tail, none)


def combine(
    rows,
    cols,
    block,
    got,
    near,
    row_op,
    col_op,
    col_rest,
    row_loaded,
    col_loaded,
    slots_loaded,
    ahead_known,
    out,
    row_own,
    col_own,
    col_slots,
    ahead,
    staged,
    sems,
    table_sems,
):
    row, col = lax.axis_index("row"), lax.axis_index("col")

    @pl.when(is_far(rows, cols))
    def _():
        tables = table_copies(
            cols, row_op, col_op, col_rest, row_own, col_own, col_slots, table_sems
        )
        for copy in tables:
            copy.start()
        for copy in tables:
            copy.wait()
        ahead[...] = dot3(split(block[...]), [col_own[i] for i in range(2)])

    chip = row // 2
    length, width = block.shape
    groups = -(-SENT * cols // LANES)
    per_group = LANES // SENT
    order = exchange_order(rows, cols)
    nothing = jnp.zeros((SENT, LANES), jnp.float32)
    half_shape = (SENT // 2, LANES)

    def places(from_chip, from_col):
        devices = [(2 * from_chip + half) * cols + from_col for half in range(2)]
        return [PIECE * order.index(device) for device in devices]

    def piece(from_chip, from_col):
        ats = places(from_chip, from_col)
        return jnp.concatenate([got[at : at + PIECE - 1] for at in ats])

    def corner(from_chip, from_col):
        tails = [got[at + PIECE - 1 : at + PIECE] for at in places(from_chip, from_col)]
        return jnp.concatenate([jnp.broadcast_to(tail, half_shape) for tail in tails])

    across = []
    corners = [nothing] * groups
    pieces = [[piece(i, j) for j in range(cols)] for i in range(rows // 2)]
    for from_col in range(cols):
        here = nothing
        tail = nothing
        for from_chip in range(rows // 2):
            here = jnp.where(from_chip == chip, pieces[from_chip][from_col], here)
            tail = jnp.where(from_chip == chip, corner(from_chip, from_col), tail)
        across.append(here)
        tail = [
            pltpu.roll(half, 0, 1, stride=SENT, stride_axis=0)
            for half in (tail[: SENT // 2], tail[SENT // 2 :])
        ]
        tail = jnp.concatenate(tail)
        wanted = (lane_place(tail.shape) == from_col % per_group) & (from_col != col)
        corners[from_col // per_group] += jnp.where(wanted, tail, 0.0)
    if cols < per_group:
        across = across * (per_group // cols)
        corners = [part + pltpu.roll(part, SENT * cols, 1) for part in corners]
    lines, slots = [], []
    own_slots = jnp.concatenate(across).T
    for from_chip in range(rows // 2):
        is_here = from_chip == chip
        line = near[...]
        parts = [jnp.where(is_here, corner_sum, 0.0) for corner_sum in corners]
        for from_col in range(cols):
            found = pieces[from_chip][from_col]
            is_col = from_col == col
            line = jnp.where(jnp.logical_not(is_here) & is_col, found, line)
            group = from_col // per_group
            parts[group] += jnp.where(is_here | is_col, 0.0, found)
        lines.append(line)
        slots.append(jnp.concatenate(parts, axis=1))
    rest = [col_slots[i] for i in range(2)]
    along_cols = jnp.concatenate(
        [
            ahead[...] + short_product(side_by_side(own_slots, SENT * cols), rest),
            long_product(
                split(jnp.concatenate(lines)),
                side_by_side(jnp.concatenate(slots), SENT * cols),
                [col_own[i] for i in range(2)],
                rest,
            ),
        ]
    )
    copies = []
    for level in range(2):
        span = 3 * width
        smoothed = split(along_cols[:, span * level : span * (level + 1)])
        products = []
        for k in range(3):
            weights = row_own[level, k]
            met = [part[:, : (3 - k) * width] for part in smoothed]
            products.append(
                long_product(
                    [weights[:, :length], weights[:, length : 2 * length]],
                    weights[:, 2 * length :],
                    [part[:length] for part in met],
                    [part[length:] for part in met],
                )
            )
        for f, (row_stencil, col_stencil) in enumerate(FEATURES):
            feature = products[row_stencil][:, width * col_stencil : width * (col_stencil + 1)]
            channel = len(FEATURES) * level + f
            staged[channel] = feature.astype(jnp.bfloat16)
            copies.append(
                pltpu.make_async_copy(staged.at[channel], out.at[channel], sems.at[channel])
            )
            copies[-1].start()
    for copy in copies:
        copy.wait()


def row_tables(height, rows):
    def sources(block):
        chips = [(2 * height * chip, 2 * height) for chip in range(rows // 2)]
        chips[block // 2] = ((block ^ 1) * height, height)
        return chips

    base = [2.0 * math.sqrt(math.pi) * s for s in DEVIATIONS]
    gains = [[b * s**k for k in range(3)] for b, s in zip(base, DEVIATIONS)]
    whole, single = summary_table(2 * height), summary_table(height)
    sums = np.zeros((2, 48, height))
    for half, own in enumerate((after(single), before(single))):
        sums[half, :BASIS] = whole[:, half * height : (half + 1) * height]
        sums[half, BASIS : BASIS + SENT] = own
    return operator_tables(height, rows, sources, gains), sums


def col_tables(width, cols):
    def sources(block):
        return [None if b == block else (b * width, width) for b in range(cols)]

    gains = [[s**k for k in range(3)] for s in DEVIATIONS]
    single = summary_table(width)
    sums = np.zeros((32 + 2 * SENT, width))
    sums[:BASIS] = single
    sums[32:] = np.concatenate([after(single), before(single)])
    return operator_tables(width, cols, sources, gains), sums


def on_device(rows, cols, image):
    height, width = image.shape
    row_weights, row_sums = row_tables(height, rows)
    col_weights, col_sums = col_tables(width, cols)
    high, low = split_table(row_weights)
    row_op = np.concatenate(
        [part[..., cells] for cells in (slice(height), slice(height, None)) for part in (high, low)],
        axis=-1,
    )
    col_op = np.transpose(col_weights, (0, 4, 1, 2, 3))
    col_op = np.moveaxis(split_table(col_op.reshape(*col_op.shape[:2], -1)), 0, 1)
    col_rest = col_op[:, :, width:]
    col_op = col_op[[0, cols // 2, cols - 1], :, :width]
    sums = np.stack(
        [np.concatenate([row_sums[h], row_sums[1 - h], col_sums]) for h in range(2)]
    )
    sums = np.moveaxis(split_table(sums), 0, 1)

    def in_vmem(count):
        return [pl.BlockSpec(memory_space=pltpu.VMEM)] * count

    params = pltpu.CompilerParams(vmem_limit_bytes=16 * 1024 * 1024)
    operands = [jnp.asarray(x) for x in (sums, row_op, col_op, col_rest)]
    operands = [pltpu.with_memory_space_constraint(x, pltpu.HBM) for x in [image] + operands]
    other = lax.ppermute(image, "row", [(i, i ^ 1) for i in range(rows)])
    block, table, row_own, col_own, col_slots, by_rows, by_cols, ahead = pl.pallas_call(
        lambda *refs: prepare(rows, cols, *refs),
        out_shape=[
            pltpu.VMEM((height, width), jnp.float32),
            *[pltpu.VMEM(x.shape[1:], jnp.bfloat16) for x in (sums, row_op, col_op, col_rest)],
            pltpu.VMEM((48, width), jnp.float32),
            pltpu.VMEM((32, height), jnp.float32),
            pltpu.VMEM((height, 6 * width), jnp.float32),
        ],
        in_specs=[pl.BlockSpec(memory_space=pltpu.HBM)] * len(operands),
        out_specs=in_vmem(8),
        scratch_shapes=[pltpu.SemaphoreType.DMA((2,)), pltpu.SemaphoreType.DMA((3,))],
        compiler_params=params,
        cost_estimate=pl.CostEstimate(
            flops=6 * 80 * height * width, bytes_accessed=4 * 1024 * 1024, transcendentals=0
        ),
        name="prepare",
    )(*operands)
    sent, near = pl.pallas_call(
        lambda *refs: pack(rows, cols, *refs),
        out_shape=[
            pltpu.VMEM((PIECE * rows * cols, LANES), jnp.float32),
            pltpu.VMEM((SENT, width), jnp.float32),
        ],
        in_specs=in_vmem(4),
        out_specs=in_vmem(2),
        compiler_params=params,
        name="pack",
    )(other, table, by_rows, by_cols)
    got = lax.all_to_all(
        sent.reshape(rows * cols, PIECE, 1, LANES),
        ("row", "col"),
        0,
        0,
        axis_index_groups=[exchange_order(rows, cols)],
    )
    features = 2 * len(FEATURES)
    kept = [row_own, col_own, col_slots, ahead]
    result = pl.pallas_call(
        lambda *refs: combine(rows, cols, *refs),
        out_shape=[
            jax.ShapeDtypeStruct((features, height, width), jnp.bfloat16),
            *[pltpu.VMEM(x.shape, x.dtype) for x in kept],
        ],
        in_specs=in_vmem(3) + [pl.BlockSpec(memory_space=pltpu.HBM)] * 3 + in_vmem(4),
        out_specs=[pl.BlockSpec(memory_space=pl.ANY)] + in_vmem(4),
        input_output_aliases={6: 1, 7: 2, 8: 3, 9: 4},
        scratch_shapes=[
            pltpu.VMEM((features, height, width), jnp.bfloat16),
            pltpu.SemaphoreType.DMA((features,)),
            pltpu.SemaphoreType.DMA((3,)),
        ],
        compiler_params=params,
        name="combine",
    )(block, got.reshape(sent.shape), near, *operands[2:], *kept)
    return result[0]


def solution(mesh):
    rows, cols = mesh.shape["row"], mesh.shape["col"]
    return jax.shard_map(
        lambda image: on_device(rows, cols, image),
        mesh=mesh,
        in_specs=(P("row", "col"),),
        out_specs=P(None, "row", "col"),
        check_vma=False,
    )
```

```python
import math

import jax
import jax.numpy as jnp
import ml_dtypes
import numpy as np
from jax import lax
from jax.experimental import pallas as pl
from jax.experimental.pallas import tpu as pltpu
from jax.sharding import PartitionSpec as P

SIG_A = 128
SIG_B = 256
DEVIATIONS = (SIG_A, SIG_B)

DER_FIRST = (
    1.0 / 280,
    -4.0 / 105,
    1.0 / 5,
    -4.0 / 5,
    0.0,
    4.0 / 5,
    -1.0 / 5,
    4.0 / 105,
    -1.0 / 280,
)
DER_SECOND = (
    -1.0 / 560,
    8.0 / 315,
    -1.0 / 5,
    8.0 / 5,
    -205.0 / 72,
    8.0 / 5,
    -1.0 / 5,
    8.0 / 315,
    -1.0 / 560,
)
IDENTITY = (0.0, 0.0, 0.0, 0.0, 1.0, 0.0, 0.0, 0.0, 0.0)
STENCILS = (IDENTITY, DER_FIRST, DER_SECOND)
DERICHE_POLES = ((1.68, 3.735, 1.783, 0.6318), (-0.6803, -0.2598, 1.723, 1.997))
FEATURES = ((0, 0), (0, 1), (1, 0), (0, 2), (1, 1), (2, 0))

HALO = 4
CAUSAL, FIRST, LAST, ANTICAUSAL = 0, 8, 12, 16
BASIS = 24
SENT = 16
LANES = 128
OWN_ROWS, OTHER_ROWS, COL_ROWS = slice(0, 48), slice(48, 96), slice(96, 128)
TILED_ROWS = [slice(128, 144)] * (LANES // SENT) + [slice(144, 160)] * (LANES // SENT)
PIECE = SENT // 2 + 1


def pole_values(deviation):
    normal_sum = 0.0
    for cos_weight, sin_weight, decay, freq in DERICHE_POLES:
        z = np.exp(complex(-decay, freq) / deviation)
        q = z / (1.0 - z)
        normal_sum += cos_weight + 2.0 * (cos_weight * q.real + sin_weight * q.imag)
    weights = [complex(cw, -sw) / normal_sum for cw, sw, _, _ in DERICHE_POLES]
    exponents = [complex(decay, -freq) / deviation for _, _, decay, freq in DERICHE_POLES]
    return np.array(weights), np.array(exponents)


def all_poles():
    return [pole_values(deviation) for deviation in DEVIATIONS]


def smooth_kernel(poles, distance):
    weights, exponents = poles
    return sum(
        (w * np.exp(-e * np.abs(distance))).real for w, e in zip(weights, exponents)
    )


def summary_table(length):
    cells = np.arange(length)
    table = np.zeros((BASIS, length))
    row = 0
    for _, exponents in all_poles():
        for e in exponents:
            causal = np.exp(-e * (length - 1 - cells))
            anticausal = np.exp(-e * cells)
            table[CAUSAL + row], table[CAUSAL + row + 1] = causal.real, causal.imag
            table[ANTICAUSAL + row], table[ANTICAUSAL + row + 1] = (
                anticausal.real,
                anticausal.imag,
            )
            row += 2
    for i in range(HALO):
        table[FIRST + i, i] = 1.0
        table[LAST + i, length - HALO + i] = 1.0
    return table


def cell_weight(poles, stencil, out_cells, in_cells, total):
    result = np.zeros((len(out_cells), len(in_cells)))
    for t in range(-HALO, HALO + 1):
        field_cells = in_cells - t
        inside = (field_cells >= 0) & (field_cells < total)
        distance = out_cells[:, None] - field_cells[None, :]
        result += stencil[t + HALO] * smooth_kernel(poles, distance) * inside[None, :]
    return result


def summary_weight(level, stencil, out_start, length, start, extent, total):
    poles = all_poles()[level]
    weights, exponents = poles
    out_cells = out_start + np.arange(length)
    after = out_start > start
    base = CAUSAL if after else FIRST
    offset = (CAUSAL if after else ANTICAUSAL) + 4 * level
    sign = 1.0 if after else -1.0
    anchor = start + (extent - 1 if after else 0)
    table = np.zeros((length, BASIS))
    for p, (w, e) in enumerate(zip(weights, exponents)):
        eigen = sum(stencil[t + HALO] * np.exp(-sign * e * t) for t in range(-HALO, HALO + 1))
        gain = w * eigen * np.exp(-e * np.abs(out_cells - anchor))
        table[:, offset + 2 * p] = gain.real
        table[:, offset + 2 * p + 1] = -gain.imag

    def far_form(cells):
        result = np.zeros((length, len(cells)))
        for t in range(-HALO, HALO + 1):
            distance = sign * (out_cells[:, None] - (cells - t)[None, :])
            result += stencil[t + HALO] * sum(
                (w * np.exp(-e * distance)).real for w, e in zip(weights, exponents)
            )
        return result

    for position, first in ((FIRST, start), (LAST, start + extent - HALO)):
        cells = first + np.arange(HALO)
        at_end = (cells[0] == 0) or (cells[-1] == total - 1)
        adjacent = (cells[-1] + 1 == out_cells[0]) or (out_cells[-1] + 1 == cells[0])
        if at_end or adjacent:
            table[:, position : position + HALO] = cell_weight(
                poles, stencil, out_cells, cells, total
            ) - far_form(cells)
    return table[:, base : base + SENT]


def operator_tables(length, blocks, sources, gains):
    tables = np.zeros((blocks, 2, 3, length, length + SENT * len(sources(0))))
    total = length * blocks
    for block in range(blocks):
        cells = block * length + np.arange(length)
        for level, poles in enumerate(all_poles()):
            for k, stencil in enumerate(STENCILS):
                view = tables[block, level, k]
                view[:, :length] = cell_weight(poles, stencil, cells, cells, total)
                for place, source in enumerate(sources(block)):
                    if source is not None:
                        at = length + SENT * place
                        view[:, at : at + SENT] = summary_weight(
                            level, stencil, cells[0], length, *source, total
                        )
                view *= gains[level][k]
    return tables


def split_table(values):
    high = values.astype(ml_dtypes.bfloat16)
    low = (values - high.astype(np.float64)).astype(ml_dtypes.bfloat16)
    return np.stack([high, low])


def split(values):
    high = values.astype(jnp.bfloat16)
    low = (values - high.astype(jnp.float32)).astype(jnp.bfloat16)
    return high, low


def dot3(left, right, dims=((1,), (0,))):
    left = jnp.concatenate([left[0], left[0], left[1]], axis=dims[0][0])
    right = jnp.concatenate([right[0], right[1], right[0]], axis=dims[1][0])
    return lax.dot_general(left, right, (dims, ((), ())), preferred_element_type=jnp.float32)


NT = ((1,), (1,))


def is_far(rows, cols):
    row, col = lax.axis_index("row"), lax.axis_index("col")
    chip = row // 2
    return col + chip // max(1, rows // 4) + lax.rem(chip, 2) >= 3


def table_copies(cols, row_op, col_op, col_rest, row_own, col_own, col_slots, sems):
    row, col = lax.axis_index("row"), lax.axis_index("col")
    variant = jnp.where(col == 0, 0, jnp.where(col == cols - 1, 2, 1))
    pairs = [
        (row_op.at[row], row_own),
        (col_op.at[variant], col_own),
        (col_rest.at[col], col_slots),
    ]
    return [pltpu.make_async_copy(*pair, sems.at[i]) for i, pair in enumerate(pairs)]


def side_by_side(values, used):
    high, low = split(values)
    if used % LANES == 0:
        return jnp.concatenate([high, low], axis=1)
    lane = lax.broadcasted_iota(jnp.int32, values.shape, 1)
    return jnp.where(lane < used, high, low)


def long_product(own, beside, tall, rest):
    left = jnp.concatenate([own[0], own[0], own[1], beside, beside], axis=1)
    none = jnp.zeros(rest[1].shape, jnp.bfloat16)
    right = jnp.concatenate([tall[0], tall[1], tall[0], rest[0], rest[0], rest[1], none])
    return jnp.dot(left, right, preferred_element_type=jnp.float32)


def short_product(beside, rest):
    none = jnp.zeros(rest[1].shape, jnp.bfloat16)
    left = jnp.concatenate([beside, beside], axis=1)
    right = jnp.concatenate([rest[0], rest[0], rest[1], none])
    return jnp.dot(left, right, preferred_element_type=jnp.float32)


def prepare(
    rows,
    cols,
    image,
    sums,
    row_op,
    col_op,
    col_rest,
    block,
    table,
    row_own,
    col_own,
    col_slots,
    by_rows,
    by_cols,
    ahead,
    sems,
    table_sems,
):
    half = lax.rem(lax.axis_index("row"), 2)
    copies = [
        pltpu.make_async_copy(image, block, sems.at[0]),
        pltpu.make_async_copy(sums.at[half], table, sems.at[1]),
    ]
    tables = table_copies(cols, row_op, col_op, col_rest, row_own, col_own, col_slots, table_sems)
    far = is_far(rows, cols)
    for copy in copies:
        copy.start()

    @pl.when(jnp.logical_not(far))
    def _():
        for copy in tables:
            copy.start()

    for copy in copies:
        copy.wait()
    cells = split(block[...])
    by_rows[...] = dot3([table[i, OWN_ROWS] for i in range(2)], cells)
    by_cols[...] = dot3([table[i, COL_ROWS] for i in range(2)], cells, NT)

    @pl.when(jnp.logical_not(far))
    def _():
        for copy in tables:
            copy.wait()
        ahead[...] = dot3(split(block[...]), [col_own[i] for i in range(2)])


def exchange_order(rows, cols):
    def place(device):
        row, col = divmod(device, cols)
        chip, half = divmod(row, 2)
        return -((col ^ half) % 2), (col ^ chip ^ chip // 2) % 2, col // 2, chip

    return sorted(range(rows * cols), key=place)


def after(values):
    return values[CAUSAL : CAUSAL + SENT]


def before(values):
    return values[FIRST : FIRST + SENT]


def lane_place(shape):
    return lax.broadcasted_iota(jnp.int32, shape, 1) // SENT


def pack(rows, cols, other, table, by_rows, by_cols, sent, near):
    row, col = lax.axis_index("row"), lax.axis_index("col")
    chip, half = row // 2, lax.rem(row, 2)
    cells = split(other[...])
    own_rows = by_rows[...]
    other_rows = dot3([table[i, OTHER_ROWS] for i in range(2)], cells)
    other_cols = dot3([table[i, COL_ROWS] for i in range(2)], cells, NT)
    near[...] = other_rows[BASIS : BASIS + SENT]
    over_rows = own_rows[:BASIS] + other_rows[:BASIS]
    own_near, other_near = own_rows[BASIS : BASIS + SENT], near[...]
    own_cols = by_cols[...]
    is_first = half == 0
    nears = [
        jnp.where(is_first, own_near, other_near),
        jnp.where(is_first, other_near, own_near),
    ]
    over_cols = [
        jnp.where(is_first, own_cols, other_cols),
        jnp.where(is_first, other_cols, own_cols),
    ]
    corners = dot3(
        split(jnp.concatenate([over_rows] + nears)),
        [jnp.concatenate([table[i, rows] for rows in TILED_ROWS]) for i in range(2)],
        NT,
    )

    def share(values):
        return jnp.where(is_first, values[: SENT // 2], values[SENT // 2 :])

    straight = [share(after(over_rows)), share(before(over_rows))]
    across, flat, placed = [], [], []
    for to_half in range(2):
        across.append([share(after(over_cols[to_half])), share(before(over_cols[to_half]))])
    for side in range(2):
        tiled = corners[:, LANES * side : LANES * (side + 1)]
        places = min(cols, LANES // SENT)
        mine = lax.rem(lane_place(tiled.shape), places) == lax.rem(col, places)
        masked = jnp.where(mine, tiled, 0.0)
        placed.append([share(after(masked)), share(before(masked))])
        lines = []
        for to_half in range(2):
            start = BASIS + SENT * (1 - to_half)
            part = share(tiled[start : start + SENT])
            line = lax.broadcasted_iota(jnp.int32, part.shape, 0)
            diagonal = lax.rem(lane_place(part.shape) + line, LANES // SENT) == lax.rem(
                col, LANES // SENT
            )
            lines.append(jnp.sum(jnp.where(diagonal, part, 0.0), axis=0, keepdims=True))
        flat.append(lines)
    none = jnp.zeros((1, LANES), jnp.float32)
    order = exchange_order(rows, cols)
    for to_chip in range(rows // 2):
        is_after = to_chip > chip
        is_here = to_chip == chip
        line = jnp.where(is_after, straight[0], straight[1])
        sides = [jnp.where(is_after, *placed[side]) for side in range(2)]
        for to_half in range(2):
            for to_col in range(cols):
                is_right = to_col > col
                body = jnp.where(to_col == col, line, jnp.where(is_right, *sides))
                body = jnp.where(is_here, jnp.where(is_right, *across[to_half]), body)
                tail = jnp.where(is_right, flat[0][to_half], flat[1][to_half])
                at = PIECE * order.index((2 * to_chip + to_half) * cols + to_col)
                sent[at : at + PIECE - 1] = body
                sent[at + PIECE - 1 : at + PIECE] = jnp.where(is_here, tail, none)


def combine(
    rows,
    cols,
    block,
    got,
    near,
    row_op,
    col_op,
    col_rest,
    row_loaded,
    col_loaded,
    slots_loaded,
    ahead_known,
    out,
    row_own,
    col_own,
    col_slots,
    ahead,
    staged,
    sems,
    table_sems,
):
    row, col = lax.axis_index("row"), lax.axis_index("col")

    @pl.when(is_far(rows, cols))
    def _():
        tables = table_copies(
            cols, row_op, col_op, col_rest, row_own, col_own, col_slots, table_sems
        )
        for copy in tables:
            copy.start()
        for copy in tables:
            copy.wait()
        ahead[...] = dot3(split(block[...]), [col_own[i] for i in range(2)])

    chip = row // 2
    length, width = block.shape
    groups = -(-SENT * cols // LANES)
    per_group = LANES // SENT
    order = exchange_order(rows, cols)
    nothing = jnp.zeros((SENT, LANES), jnp.float32)
    half_shape = (SENT // 2, LANES)

    def places(from_chip, from_col):
        devices = [(2 * from_chip + half) * cols + from_col for half in range(2)]
        return [PIECE * order.index(device) for device in devices]

    def piece(from_chip, from_col):
        ats = places(from_chip, from_col)
        return jnp.concatenate([got[at : at + PIECE - 1] for at in ats])

    def corner(from_chip, from_col):
        tails = [got[at + PIECE - 1 : at + PIECE] for at in places(from_chip, from_col)]
        return jnp.concatenate([jnp.broadcast_to(tail, half_shape) for tail in tails])

    across = []
    corners = [nothing] * groups
    pieces = [[piece(i, j) for j in range(cols)] for i in range(rows // 2)]
    for from_col in range(cols):
        here = nothing
        tail = nothing
        for from_chip in range(rows // 2):
            here = jnp.where(from_chip == chip, pieces[from_chip][from_col], here)
            tail = jnp.where(from_chip == chip, corner(from_chip, from_col), tail)
        across.append(here)
        tail = [
            pltpu.roll(half, 0, 1, stride=SENT, stride_axis=0)
            for half in (tail[: SENT // 2], tail[SENT // 2 :])
        ]
        tail = jnp.concatenate(tail)
        wanted = (lane_place(tail.shape) == from_col % per_group) & (from_col != col)
        corners[from_col // per_group] += jnp.where(wanted, tail, 0.0)
    if cols < per_group:
        across = across * (per_group // cols)
        corners = [part + pltpu.roll(part, SENT * cols, 1) for part in corners]
    lines, slots = [], []
    own_slots = jnp.concatenate(across).T
    for from_chip in range(rows // 2):
        is_here = from_chip == chip
        line = near[...]
        parts = [jnp.where(is_here, corner_sum, 0.0) for corner_sum in corners]
        for from_col in range(cols):
            found = pieces[from_chip][from_col]
            is_col = from_col == col
            line = jnp.where(jnp.logical_not(is_here) & is_col, found, line)
            group = from_col // per_group
            parts[group] += jnp.where(is_here | is_col, 0.0, found)
        lines.append(line)
        slots.append(jnp.concatenate(parts, axis=1))
    rest = [col_slots[i] for i in range(2)]
    along_cols = jnp.concatenate(
        [
            ahead[...] + short_product(side_by_side(own_slots, SENT * cols), rest),
            long_product(
                split(jnp.concatenate(lines)),
                side_by_side(jnp.concatenate(slots), SENT * cols),
                [col_own[i] for i in range(2)],
                rest,
            ),
        ]
    )
    copies = []
    for level in range(2):
        span = 3 * width
        smoothed = split(along_cols[:, span * level : span * (level + 1)])
        products = []
        for k in range(3):
            weights = row_own[level, k]
            met = [part[:, : (3 - k) * width] for part in smoothed]
            products.append(
                long_product(
                    [weights[:, :length], weights[:, length : 2 * length]],
                    weights[:, 2 * length :],
                    [part[:length] for part in met],
                    [part[length:] for part in met],
                )
            )
        for f, (row_stencil, col_stencil) in enumerate(FEATURES):
            feature = products[row_stencil][:, width * col_stencil : width * (col_stencil + 1)]
            channel = len(FEATURES) * level + f
            staged[channel] = feature.astype(jnp.bfloat16)
            copies.append(
                pltpu.make_async_copy(staged.at[channel], out.at[channel], sems.at[channel])
            )
            copies[-1].start()
    for copy in copies:
        copy.wait()


def row_tables(height, rows):
    def sources(block):
        chips = [(2 * height * chip, 2 * height) for chip in range(rows // 2)]
        chips[block // 2] = ((block ^ 1) * height, height)
        return chips

    base = [2.0 * math.sqrt(math.pi) * s for s in DEVIATIONS]
    gains = [[b * s**k for k in range(3)] for b, s in zip(base, DEVIATIONS)]
    whole, single = summary_table(2 * height), summary_table(height)
    sums = np.zeros((2, 48, height))
    for half, own in enumerate((after(single), before(single))):
        sums[half, :BASIS] = whole[:, half * height : (half + 1) * height]
        sums[half, BASIS : BASIS + SENT] = own
    return operator_tables(height, rows, sources, gains), sums


def col_tables(width, cols):
    def sources(block):
        return [None if b == block else (b * width, width) for b in range(cols)]

    gains = [[s**k for k in range(3)] for s in DEVIATIONS]
    single = summary_table(width)
    sums = np.zeros((32 + 2 * SENT, width))
    sums[:BASIS] = single
    sums[32:] = np.concatenate([after(single), before(single)])
    return operator_tables(width, cols, sources, gains), sums


def on_device(rows, cols, image):
    height, width = image.shape
    row_weights, row_sums = row_tables(height, rows)
    col_weights, col_sums = col_tables(width, cols)
    high, low = split_table(row_weights)
    row_op = np.concatenate(
        [part[..., cells] for cells in (slice(height), slice(height, None)) for part in (high, low)],
        axis=-1,
    )
    col_op = np.transpose(col_weights, (0, 4, 1, 2, 3))
    col_op = np.moveaxis(split_table(col_op.reshape(*col_op.shape[:2], -1)), 0, 1)
    col_rest = col_op[:, :, width:]
    col_op = col_op[[0, cols // 2, cols - 1], :, :width]
    sums = np.stack(
        [np.concatenate([row_sums[h], row_sums[1 - h], col_sums]) for h in range(2)]
    )
    sums = np.moveaxis(split_table(sums), 0, 1)

    def in_vmem(count):
        return [pl.BlockSpec(memory_space=pltpu.VMEM)] * count

    params = pltpu.CompilerParams(vmem_limit_bytes=16 * 1024 * 1024)
    operands = [jnp.asarray(x) for x in (sums, row_op, col_op, col_rest)]
    operands = [pltpu.with_memory_space_constraint(x, pltpu.HBM) for x in [image] + operands]
    other = lax.ppermute(image, "row", [(i, i ^ 1) for i in range(rows)])
    block, table, row_own, col_own, col_slots, by_rows, by_cols, ahead = pl.pallas_call(
        lambda *refs: prepare(rows, cols, *refs),
        out_shape=[
            pltpu.VMEM((height, width), jnp.float32),
            *[pltpu.VMEM(x.shape[1:], jnp.bfloat16) for x in (sums, row_op, col_op, col_rest)],
            pltpu.VMEM((48, width), jnp.float32),
            pltpu.VMEM((32, height), jnp.float32),
            pltpu.VMEM((height, 6 * width), jnp.float32),
        ],
        in_specs=[pl.BlockSpec(memory_space=pltpu.HBM)] * len(operands),
        out_specs=in_vmem(8),
        scratch_shapes=[pltpu.SemaphoreType.DMA((2,)), pltpu.SemaphoreType.DMA((3,))],
        compiler_params=params,
        cost_estimate=pl.CostEstimate(
            flops=6 * 80 * height * width, bytes_accessed=4 * 1024 * 1024, transcendentals=0
        ),
        name="prepare",
    )(*operands)
    sent, near = pl.pallas_call(
        lambda *refs: pack(rows, cols, *refs),
        out_shape=[
            pltpu.VMEM((PIECE * rows * cols, LANES), jnp.float32),
            pltpu.VMEM((SENT, width), jnp.float32),
        ],
        in_specs=in_vmem(4),
        out_specs=in_vmem(2),
        compiler_params=params,
        name="pack",
    )(other, table, by_rows, by_cols)
    got = lax.all_to_all(
        sent.reshape(rows * cols, PIECE, 1, LANES),
        ("row", "col"),
        0,
        0,
        axis_index_groups=[exchange_order(rows, cols)],
    )
    features = 2 * len(FEATURES)
    kept = [row_own, col_own, col_slots, ahead]
    result = pl.pallas_call(
        lambda *refs: combine(rows, cols, *refs),
        out_shape=[
            jax.ShapeDtypeStruct((features, height, width), jnp.bfloat16),
            *[pltpu.VMEM(x.shape, x.dtype) for x in kept],
        ],
        in_specs=in_vmem(3) + [pl.BlockSpec(memory_space=pltpu.HBM)] * 3 + in_vmem(4),
        out_specs=[pl.BlockSpec(memory_space=pl.ANY)] + in_vmem(4),
        input_output_aliases={6: 1, 7: 2, 8: 3, 9: 4},
        scratch_shapes=[
            pltpu.VMEM((features, height, width), jnp.bfloat16),
            pltpu.SemaphoreType.DMA((features,)),
            pltpu.SemaphoreType.DMA((3,)),
        ],
        compiler_params=params,
        name="combine",
    )(block, got.reshape(sent.shape), near, *operands[2:], *kept)
    return result[0]


def solution(mesh):
    rows, cols = mesh.shape["row"], mesh.shape["col"]
    return jax.shard_map(
        lambda image: on_device(rows, cols, image),
        mesh=mesh,
        in_specs=(P("row", "col"),),
        out_specs=P(None, "row", "col"),
        check_vma=False,
    )
```

```python
import math

import jax
import jax.numpy as jnp
import ml_dtypes
import numpy as np
from jax import lax
from jax.experimental import pallas as pl
from jax.experimental.pallas import tpu as pltpu
from jax.sharding import PartitionSpec as P

SIG_A = 128
SIG_B = 256
DEVIATIONS = (SIG_A, SIG_B)

DER_FIRST = (
    1.0 / 280,
    -4.0 / 105,
    1.0 / 5,
    -4.0 / 5,
    0.0,
    4.0 / 5,
    -1.0 / 5,
    4.0 / 105,
    -1.0 / 280,
)
DER_SECOND = (
    -1.0 / 560,
    8.0 / 315,
    -1.0 / 5,
    8.0 / 5,
    -205.0 / 72,
    8.0 / 5,
    -1.0 / 5,
    8.0 / 315,
    -1.0 / 560,
)
IDENTITY = (0.0, 0.0, 0.0, 0.0, 1.0, 0.0, 0.0, 0.0, 0.0)
STENCILS = (IDENTITY, DER_FIRST, DER_SECOND)
DERICHE_POLES = ((1.68, 3.735, 1.783, 0.6318), (-0.6803, -0.2598, 1.723, 1.997))
FEATURES = ((0, 0), (0, 1), (1, 0), (0, 2), (1, 1), (2, 0))

HALO = 4
CAUSAL, FIRST, LAST, ANTICAUSAL = 0, 8, 12, 16
BASIS = 24
SENT = 16
LANES = 128
OWN_ROWS, OTHER_ROWS, COL_ROWS = slice(0, 48), slice(48, 96), slice(96, 128)
TILED_ROWS = slice(128, 256), slice(256, 384)
PIECE = SENT // 2 + 1


def pole_values(deviation):
    normal_sum = 0.0
    for cos_weight, sin_weight, decay, freq in DERICHE_POLES:
        z = np.exp(complex(-decay, freq) / deviation)
        q = z / (1.0 - z)
        normal_sum += cos_weight + 2.0 * (cos_weight * q.real + sin_weight * q.imag)
    weights = [complex(cw, -sw) / normal_sum for cw, sw, _, _ in DERICHE_POLES]
    exponents = [complex(decay, -freq) / deviation for _, _, decay, freq in DERICHE_POLES]
    return np.array(weights), np.array(exponents)


def all_poles():
    return [pole_values(deviation) for deviation in DEVIATIONS]


def smooth_kernel(poles, distance):
    weights, exponents = poles
    return sum(
        (w * np.exp(-e * np.abs(distance))).real for w, e in zip(weights, exponents)
    )


def summary_table(length):
    cells = np.arange(length)
    table = np.zeros((BASIS, length))
    row = 0
    for _, exponents in all_poles():
        for e in exponents:
            causal = np.exp(-e * (length - 1 - cells))
            anticausal = np.exp(-e * cells)
            table[CAUSAL + row], table[CAUSAL + row + 1] = causal.real, causal.imag
            table[ANTICAUSAL + row], table[ANTICAUSAL + row + 1] = (
                anticausal.real,
                anticausal.imag,
            )
            row += 2
    for i in range(HALO):
        table[FIRST + i, i] = 1.0
        table[LAST + i, length - HALO + i] = 1.0
    return table


def cell_weight(poles, stencil, out_cells, in_cells, total):
    result = np.zeros((len(out_cells), len(in_cells)))
    for t in range(-HALO, HALO + 1):
        field_cells = in_cells - t
        inside = (field_cells >= 0) & (field_cells < total)
        distance = out_cells[:, None] - field_cells[None, :]
        result += stencil[t + HALO] * smooth_kernel(poles, distance) * inside[None, :]
    return result


def summary_weight(level, stencil, out_start, length, start, extent, total):
    poles = all_poles()[level]
    weights, exponents = poles
    out_cells = out_start + np.arange(length)
    after = out_start > start
    base = CAUSAL if after else FIRST
    offset = (CAUSAL if after else ANTICAUSAL) + 4 * level
    sign = 1.0 if after else -1.0
    anchor = start + (extent - 1 if after else 0)
    table = np.zeros((length, BASIS))
    for p, (w, e) in enumerate(zip(weights, exponents)):
        eigen = sum(stencil[t + HALO] * np.exp(-sign * e * t) for t in range(-HALO, HALO + 1))
        gain = w * eigen * np.exp(-e * np.abs(out_cells - anchor))
        table[:, offset + 2 * p] = gain.real
        table[:, offset + 2 * p + 1] = -gain.imag

    def far_form(cells):
        result = np.zeros((length, len(cells)))
        for t in range(-HALO, HALO + 1):
            distance = sign * (out_cells[:, None] - (cells - t)[None, :])
            result += stencil[t + HALO] * sum(
                (w * np.exp(-e * distance)).real for w, e in zip(weights, exponents)
            )
        return result

    for position, first in ((FIRST, start), (LAST, start + extent - HALO)):
        cells = first + np.arange(HALO)
        at_end = (cells[0] == 0) or (cells[-1] == total - 1)
        adjacent = (cells[-1] + 1 == out_cells[0]) or (out_cells[-1] + 1 == cells[0])
        if at_end or adjacent:
            table[:, position : position + HALO] = cell_weight(
                poles, stencil, out_cells, cells, total
            ) - far_form(cells)
    return table[:, base : base + SENT]


def operator_tables(length, blocks, sources, gains):
    tables = np.zeros((blocks, 2, 3, length, length + SENT * len(sources(0))))
    total = length * blocks
    for block in range(blocks):
        cells = block * length + np.arange(length)
        for level, poles in enumerate(all_poles()):
            for k, stencil in enumerate(STENCILS):
                view = tables[block, level, k]
                view[:, :length] = cell_weight(poles, stencil, cells, cells, total)
                for place, source in enumerate(sources(block)):
                    if source is not None:
                        at = length + SENT * place
                        view[:, at : at + SENT] = summary_weight(
                            level, stencil, cells[0], length, *source, total
                        )
                view *= gains[level][k]
    return tables


def split_table(values):
    high = values.astype(ml_dtypes.bfloat16)
    low = (values - high.astype(np.float64)).astype(ml_dtypes.bfloat16)
    return np.stack([high, low])


def split(values):
    high = values.astype(jnp.bfloat16)
    low = (values - high.astype(jnp.float32)).astype(jnp.bfloat16)
    return high, low


def dot3(left, right, dims=((1,), (0,))):
    left = jnp.concatenate([left[0], left[0], left[1]], axis=dims[0][0])
    right = jnp.concatenate([right[0], right[1], right[0]], axis=dims[1][0])
    return lax.dot_general(left, right, (dims, ((), ())), preferred_element_type=jnp.float32)


NT = ((1,), (1,))


def is_far(rows, cols):
    row, col = lax.axis_index("row"), lax.axis_index("col")
    chip = row // 2
    return col + chip // max(1, rows // 4) + lax.rem(chip, 2) >= 3


def table_copies(cols, row_op, col_op, col_rest, row_own, col_own, col_slots, sems):
    row, col = lax.axis_index("row"), lax.axis_index("col")
    variant = jnp.where(col == 0, 0, jnp.where(col == cols - 1, 2, 1))
    pairs = [
        (row_op.at[row], row_own),
        (col_op.at[variant], col_own),
        (col_rest.at[col], col_slots),
    ]
    return [pltpu.make_async_copy(*pair, sems.at[i]) for i, pair in enumerate(pairs)]


def side_by_side(values, used):
    high, low = split(values)
    if used % LANES == 0:
        return jnp.concatenate([high, low], axis=1)
    lane = lax.broadcasted_iota(jnp.int32, values.shape, 1)
    return jnp.where(lane < used, high, low)


def long_product(own, beside, tall, rest):
    left = jnp.concatenate([own[0], own[0], own[1], beside, beside], axis=1)
    none = jnp.zeros(rest[1].shape, jnp.bfloat16)
    right = jnp.concatenate([tall[0], tall[1], tall[0], rest[0], rest[0], rest[1], none])
    return jnp.dot(left, right, preferred_element_type=jnp.float32)


def short_product(beside, rest):
    none = jnp.zeros(rest[1].shape, jnp.bfloat16)
    left = jnp.concatenate([beside, beside], axis=1)
    right = jnp.concatenate([rest[0], rest[0], rest[1], none])
    return jnp.dot(left, right, preferred_element_type=jnp.float32)


def prepare(
    rows,
    cols,
    image,
    sums,
    row_op,
    col_op,
    col_rest,
    block,
    table,
    row_own,
    col_own,
    col_slots,
    by_rows,
    by_cols,
    ahead,
    sems,
    table_sems,
):
    half = lax.rem(lax.axis_index("row"), 2)
    copies = [
        pltpu.make_async_copy(image, block, sems.at[0]),
        pltpu.make_async_copy(sums.at[half], table, sems.at[1]),
    ]
    tables = table_copies(cols, row_op, col_op, col_rest, row_own, col_own, col_slots, table_sems)
    far = is_far(rows, cols)
    for copy in copies:
        copy.start()

    @pl.when(jnp.logical_not(far))
    def _():
        for copy in tables:
            copy.start()

    for copy in copies:
        copy.wait()
    cells = split(block[...])
    by_rows[...] = dot3([table[i, OWN_ROWS] for i in range(2)], cells)
    by_cols[...] = dot3([table[i, COL_ROWS] for i in range(2)], cells, NT)

    @pl.when(jnp.logical_not(far))
    def _():
        for copy in tables:
            copy.wait()
        ahead[...] = dot3(split(block[...]), [col_own[i] for i in range(2)])


def exchange_order(rows, cols):
    def place(device):
        row, col = divmod(device, cols)
        chip, half = divmod(row, 2)
        return -((col ^ half) % 2), (col ^ chip ^ chip // 2) % 2, col // 2, chip

    return sorted(range(rows * cols), key=place)


def after(values):
    return values[CAUSAL : CAUSAL + SENT]


def before(values):
    return values[FIRST : FIRST + SENT]


def lane_place(shape):
    return lax.broadcasted_iota(jnp.int32, shape, 1) // SENT


def pack(rows, cols, other, table, by_rows, by_cols, sent, near):
    row, col = lax.axis_index("row"), lax.axis_index("col")
    chip, half = row // 2, lax.rem(row, 2)
    cells = split(other[...])
    own_rows = by_rows[...]
    other_rows = dot3([table[i, OTHER_ROWS] for i in range(2)], cells)
    other_cols = dot3([table[i, COL_ROWS] for i in range(2)], cells, NT)
    near[...] = other_rows[BASIS : BASIS + SENT]
    over_rows = own_rows[:BASIS] + other_rows[:BASIS]
    own_near, other_near = own_rows[BASIS : BASIS + SENT], near[...]
    own_cols = by_cols[...]
    is_first = half == 0
    nears = [
        jnp.where(is_first, own_near, other_near),
        jnp.where(is_first, other_near, own_near),
    ]
    over_cols = [
        jnp.where(is_first, own_cols, other_cols),
        jnp.where(is_first, other_cols, own_cols),
    ]
    corners = dot3(
        split(jnp.concatenate([over_rows] + nears)),
        [jnp.concatenate([table[i, rows] for rows in TILED_ROWS], axis=1) for i in range(2)],
    )

    def share(values):
        return jnp.where(is_first, values[: SENT // 2], values[SENT // 2 :])

    straight = [share(after(over_rows)), share(before(over_rows))]
    across, flat, placed = [], [], []
    for to_half in range(2):
        across.append([share(after(over_cols[to_half])), share(before(over_cols[to_half]))])
    for side in range(2):
        tiled = corners[:, LANES * side : LANES * (side + 1)]
        places = min(cols, LANES // SENT)
        mine = lax.rem(lane_place(tiled.shape), places) == lax.rem(col, places)
        masked = jnp.where(mine, tiled, 0.0)
        placed.append([share(after(masked)), share(before(masked))])
        lines = []
        for to_half in range(2):
            start = BASIS + SENT * (1 - to_half)
            part = share(tiled[start : start + SENT])
            line = lax.broadcasted_iota(jnp.int32, part.shape, 0)
            diagonal = lax.rem(lane_place(part.shape) + line, LANES // SENT) == lax.rem(
                col, LANES // SENT
            )
            lines.append(jnp.sum(jnp.where(diagonal, part, 0.0), axis=0, keepdims=True))
        flat.append(lines)
    none = jnp.zeros((1, LANES), jnp.float32)
    order = exchange_order(rows, cols)
    for to_chip in range(rows // 2):
        is_after = to_chip > chip
        is_here = to_chip == chip
        line = jnp.where(is_after, straight[0], straight[1])
        sides = [jnp.where(is_after, *placed[side]) for side in range(2)]
        for to_half in range(2):
            for to_col in range(cols):
                is_right = to_col > col
                body = jnp.where(to_col == col, line, jnp.where(is_right, *sides))
                body = jnp.where(is_here, jnp.where(is_right, *across[to_half]), body)
                tail = jnp.where(is_right, flat[0][to_half], flat[1][to_half])
                at = PIECE * order.index((2 * to_chip + to_half) * cols + to_col)
                sent[at : at + PIECE - 1] = body
                sent[at + PIECE - 1 : at + PIECE] = jnp.where(is_here, tail, none)


def combine(
    rows,
    cols,
    block,
    got,
    near,
    row_op,
    col_op,
    col_rest,
    row_loaded,
    col_loaded,
    slots_loaded,
    ahead_known,
    out,
    row_own,
    col_own,
    col_slots,
    ahead,
    staged,
    sems,
    table_sems,
):
    row, col = lax.axis_index("row"), lax.axis_index("col")

    @pl.when(is_far(rows, cols))
    def _():
        tables = table_copies(
            cols, row_op, col_op, col_rest, row_own, col_own, col_slots, table_sems
        )
        for copy in tables:
            copy.start()
        for copy in tables:
            copy.wait()
        ahead[...] = dot3(split(block[...]), [col_own[i] for i in range(2)])

    chip = row // 2
    length, width = block.shape
    groups = -(-SENT * cols // LANES)
    per_group = LANES // SENT
    order = exchange_order(rows, cols)
    nothing = jnp.zeros((SENT, LANES), jnp.float32)
    half_shape = (SENT // 2, LANES)

    def places(from_chip, from_col):
        devices = [(2 * from_chip + half) * cols + from_col for half in range(2)]
        return [PIECE * order.index(device) for device in devices]

    def piece(from_chip, from_col):
        ats = places(from_chip, from_col)
        return jnp.concatenate([got[at : at + PIECE - 1] for at in ats])

    def corner(from_chip, from_col):
        tails = [got[at + PIECE - 1 : at + PIECE] for at in places(from_chip, from_col)]
        return jnp.concatenate([jnp.broadcast_to(tail, half_shape) for tail in tails])

    across = []
    corners = [nothing] * groups
    pieces = [[piece(i, j) for j in range(cols)] for i in range(rows // 2)]
    for from_col in range(cols):
        here = nothing
        tail = nothing
        for from_chip in range(rows // 2):
            here = jnp.where(from_chip == chip, pieces[from_chip][from_col], here)
            tail = jnp.where(from_chip == chip, corner(from_chip, from_col), tail)
        across.append(here)
        tail = [
            pltpu.roll(half, 0, 1, stride=SENT, stride_axis=0)
            for half in (tail[: SENT // 2], tail[SENT // 2 :])
        ]
        tail = jnp.concatenate(tail)
        wanted = (lane_place(tail.shape) == from_col % per_group) & (from_col != col)
        corners[from_col // per_group] += jnp.where(wanted, tail, 0.0)
    if cols < per_group:
        across = across * (per_group // cols)
        corners = [part + pltpu.roll(part, SENT * cols, 1) for part in corners]
    lines, slots = [], []
    own_slots = jnp.concatenate(across).T
    for from_chip in range(rows // 2):
        is_here = from_chip == chip
        line = near[...]
        parts = [jnp.where(is_here, corner_sum, 0.0) for corner_sum in corners]
        for from_col in range(cols):
            found = pieces[from_chip][from_col]
            is_col = from_col == col
            line = jnp.where(jnp.logical_not(is_here) & is_col, found, line)
            group = from_col // per_group
            parts[group] += jnp.where(is_here | is_col, 0.0, found)
        lines.append(line)
        slots.append(jnp.concatenate(parts, axis=1))
    rest = [col_slots[i] for i in range(2)]
    along_cols = jnp.concatenate(
        [
            ahead[...] + short_product(side_by_side(own_slots, SENT * cols), rest),
            long_product(
                split(jnp.concatenate(lines)),
                side_by_side(jnp.concatenate(slots), SENT * cols),
                [col_own[i] for i in range(2)],
                rest,
            ),
        ]
    )
    copies = []
    for level in range(2):
        span = 3 * width
        smoothed = split(along_cols[:, span * level : span * (level + 1)])
        products = []
        for k in range(3):
            weights = row_own[level, k]
            met = [part[:, : (3 - k) * width] for part in smoothed]
            products.append(
                long_product(
                    [weights[:, :length], weights[:, length : 2 * length]],
                    weights[:, 2 * length :],
                    [part[:length] for part in met],
                    [part[length:] for part in met],
                )
            )
        for f, (row_stencil, col_stencil) in enumerate(FEATURES):
            feature = products[row_stencil][:, width * col_stencil : width * (col_stencil + 1)]
            channel = len(FEATURES) * level + f
            staged[channel] = feature.astype(jnp.bfloat16)
            if f + 1 == len(FEATURES) or level:
                done = pl.ds(channel, 1) if level else pl.ds(0, len(FEATURES))
                copies.append(
                    pltpu.make_async_copy(staged.at[done], out.at[done], sems.at[channel])
                )
                copies[-1].start()
    for copy in copies:
        copy.wait()


def row_tables(height, rows):
    def sources(block):
        chips = [(2 * height * chip, 2 * height) for chip in range(rows // 2)]
        chips[block // 2] = ((block ^ 1) * height, height)
        return chips

    base = [2.0 * math.sqrt(math.pi) * s for s in DEVIATIONS]
    gains = [[b * s**k for k in range(3)] for b, s in zip(base, DEVIATIONS)]
    whole, single = summary_table(2 * height), summary_table(height)
    sums = np.zeros((2, 48, height))
    for half, own in enumerate((after(single), before(single))):
        sums[half, :BASIS] = whole[:, half * height : (half + 1) * height]
        sums[half, BASIS : BASIS + SENT] = own
    return operator_tables(height, rows, sources, gains), sums


def col_tables(width, cols):
    def sources(block):
        return [None if b == block else (b * width, width) for b in range(cols)]

    gains = [[s**k for k in range(3)] for s in DEVIATIONS]
    single = summary_table(width)
    sums = np.zeros((32 + 2 * width, LANES))
    sums[:BASIS, :width] = single
    sums[32:] = np.concatenate(
        [np.tile(part, (LANES // SENT, 1)).T for part in (after(single), before(single))]
    )
    return operator_tables(width, cols, sources, gains), sums


def on_device(rows, cols, image):
    height, width = image.shape
    row_weights, row_sums = row_tables(height, rows)
    col_weights, col_sums = col_tables(width, cols)
    high, low = split_table(row_weights)
    row_op = np.concatenate(
        [part[..., cells] for cells in (slice(height), slice(height, None)) for part in (high, low)],
        axis=-1,
    )
    col_op = np.transpose(col_weights, (0, 4, 1, 2, 3))
    col_op = np.moveaxis(split_table(col_op.reshape(*col_op.shape[:2], -1)), 0, 1)
    col_rest = col_op[:, :, width:]
    col_op = col_op[[0, cols // 2, cols - 1], :, :width]
    sums = np.stack(
        [np.concatenate([row_sums[h], row_sums[1 - h], col_sums]) for h in range(2)]
    )
    sums = np.moveaxis(split_table(sums), 0, 1)

    def in_vmem(count):
        return [pl.BlockSpec(memory_space=pltpu.VMEM)] * count

    params = pltpu.CompilerParams(vmem_limit_bytes=16 * 1024 * 1024)
    operands = [jnp.asarray(x) for x in (sums, row_op, col_op, col_rest)]
    operands = [pltpu.with_memory_space_constraint(x, pltpu.HBM) for x in [image] + operands]
    other = lax.ppermute(image, "row", [(i, i ^ 1) for i in range(rows)])
    block, table, row_own, col_own, col_slots, by_rows, by_cols, ahead = pl.pallas_call(
        lambda *refs: prepare(rows, cols, *refs),
        out_shape=[
            pltpu.VMEM((height, width), jnp.float32),
            *[pltpu.VMEM(x.shape[1:], jnp.bfloat16) for x in (sums, row_op, col_op, col_rest)],
            pltpu.VMEM((48, width), jnp.float32),
            pltpu.VMEM((32, height), jnp.float32),
            pltpu.VMEM((height, 6 * width), jnp.float32),
        ],
        in_specs=[pl.BlockSpec(memory_space=pltpu.HBM)] * len(operands),
        out_specs=in_vmem(8),
        scratch_shapes=[pltpu.SemaphoreType.DMA((2,)), pltpu.SemaphoreType.DMA((3,))],
        compiler_params=params,
        cost_estimate=pl.CostEstimate(
            flops=6 * 80 * height * width, bytes_accessed=4 * 1024 * 1024, transcendentals=0
        ),
        name="prepare",
    )(*operands)
    sent, near = pl.pallas_call(
        lambda *refs: pack(rows, cols, *refs),
        out_shape=[
            pltpu.VMEM((PIECE * rows * cols, LANES), jnp.float32),
            pltpu.VMEM((SENT, width), jnp.float32),
        ],
        in_specs=in_vmem(4),
        out_specs=in_vmem(2),
        compiler_params=params,
        name="pack",
    )(other, table, by_rows, by_cols)
    got = lax.all_to_all(
        sent.reshape(rows * cols, PIECE, 1, LANES),
        ("row", "col"),
        0,
        0,
        axis_index_groups=[exchange_order(rows, cols)],
    )
    features = 2 * len(FEATURES)
    kept = [row_own, col_own, col_slots, ahead]
    result = pl.pallas_call(
        lambda *refs: combine(rows, cols, *refs),
        out_shape=[
            jax.ShapeDtypeStruct((features, height, width), jnp.bfloat16),
            *[pltpu.VMEM(x.shape, x.dtype) for x in kept],
        ],
        in_specs=in_vmem(3) + [pl.BlockSpec(memory_space=pltpu.HBM)] * 3 + in_vmem(4),
        out_specs=[pl.BlockSpec(memory_space=pl.ANY)] + in_vmem(4),
        input_output_aliases={6: 1, 7: 2, 8: 3, 9: 4},
        scratch_shapes=[
            pltpu.VMEM((features, height, width), jnp.bfloat16),
            pltpu.SemaphoreType.DMA((features,)),
            pltpu.SemaphoreType.DMA((3,)),
        ],
        compiler_params=params,
        name="combine",
    )(block, got.reshape(sent.shape), near, *operands[2:], *kept)
    return result[0]


def solution(mesh):
    rows, cols = mesh.shape["row"], mesh.shape["col"]
    return jax.shard_map(
        lambda image: on_device(rows, cols, image),
        mesh=mesh,
        in_specs=(P("row", "col"),),
        out_specs=P(None, "row", "col"),
        check_vma=False,
    )
```
